128 devices in a mesh: slab: 32 (over y, z, core), brick: 4 (over x).
Axes of the slice: x: 4, y: 4, z: 4, core: 2. Of those that a mesh axis runs over, the one named last changes fastest.
Arguments:
- charges: float32 [4, 131072], P(None, ('slab', 'brick')), may hold values from -8 to 8
- fractions: float32 [3, 131072], P(None, ('slab', 'brick')), may hold values from 0 to 1
- inner_cell: int32 [131072], P(('slab', 'brick')), may hold values from 0 to 4095
- dest_slab: int32 [131072, 1], P(('slab', 'brick')), may hold values from 0 to 31; in each aligned block of 1024 rows (0 to 1023, 1024 to 2047, ...) at most 64 rows name the same one
- filter_amp: float32 [2, 16], replicated, may hold values from -24 to 24
Outputs:
- potentials: float32 [4, 131072], P(None, ('slab', 'brick'))
The draws below stay inside these ranges and needn't reach their ends.
Inputs may be any that keep to these rules, and one draw needn't show every extreme that they name: `dest_slab`: among the atoms of one device, no z-slab is named by more than 64 atoms.
All inputs are finite; a program needn't handle non-finite values.
Results may differ from the reference program's by a relative error of at most 0.0044.
Values may be sent and summed in bfloat16 or wider, within the bound.
A program may use at most 128 MiB of HBM per device.

```python
import math
import jax
import jax.numpy as jnp
import numpy as np
from jax import lax

G = 256
C = 4
PAIRS = 2
RADIAL = 16
BIN = 16
ATOMS_DEV = 1024
CAP = 64
ATOMS = 131072
ZS = 8
XW = 8
YB = 64
N_SLAB = 32
N_BRICK = 4


def draw_charges(key, part):
    key = jax.random.fold_in(key, 11)
    noise_key = jax.random.fold_in(key, 0)
    noise_part = jax.random.normal(noise_key, (C, ATOMS), jnp.float32)
    return jnp.clip(noise_part, -6.0, 6.0)


def draw_filter_amp(key, part):
    key = jax.random.fold_in(key, 23)
    normal_key = jax.random.fold_in(key, 0)
    base_part = jax.random.normal(normal_key, (PAIRS, RADIAL), jnp.float32)
    return jnp.clip(4.0 * base_part, -24.0, 24.0)


def plant(array, rng, low, largest):
    shape = array.shape
    index_at = [jax.random.randint(jax.random.fold_in(rng, axis), (), 0, shape[axis]) for axis in range(len(shape))]
    array = array.at[tuple(index_at)].set(low)
    longest = shape.index(max(shape))
    index_at[longest] = (index_at[longest] + 1) % shape[longest]
    return array.at[tuple(index_at)].set(largest)


def levels(rng, extent, cuts, least, largest):
    factor_of, own = 1.0, jax.random.fold_in(rng, 6)
    for axis_at, parts in cuts:
        draws = jnp.exp(jax.random.uniform(jax.random.fold_in(own, axis_at), (parts,), jnp.float32, least / len(cuts), largest / len(cuts)))
        factor_of = factor_of * jnp.repeat(draws, extent[axis_at] // parts).reshape([-1 if axis == axis_at else 1 for axis in range(len(extent))])
    return factor_of


def assign_block(key, own, number, rows, number_of, top, reach, lean):
    sequence = jax.random.permutation(key, number_of)
    crowded, ordinary = shares(number_of, rows * top, reach, lean, True), shares(number_of, rows * top, reach, lean, False)
    places = jnp.arange(number_of)

    def named(lengths, offset_by):
        used = int((lengths > 0).sum())
        fixed = max(1, used // 4)
        moved = fixed + (places - fixed + offset_by * (used - fixed)) % max(1, number_of - fixed)
        return jnp.zeros((number_of,), jnp.int32).at[sequence[jnp.where(places < fixed, places, moved)]].set(jnp.asarray(lengths, jnp.int32))

    lengths = jnp.where(number % 4 == 0, named(crowded, number // 4), named(ordinary, number - number // 4 - 1))
    mixed = jax.random.permutation(jax.random.fold_in(own, 3), number_of)
    source_of, taker = mixed[0:number_of // 2 * 2:2], mixed[1:number_of // 2 * 2:2]
    slack = jnp.minimum(lengths[source_of] - 1, reach - lengths[taker]) // 2
    slack = jnp.where((source_of == sequence[0]) | (taker == sequence[0]) | (lengths[taker] == 0), 0, jnp.maximum(slack, 0))
    moved = jax.random.randint(jax.random.fold_in(own, 4), (number_of // 2,), 0, 1 << 20) % (slack + 1)
    lengths = lengths.at[source_of].add(-moved).at[taker].add(moved)
    members = jnp.searchsorted(jnp.cumsum(lengths), jnp.arange(rows * top), side="right").astype(jnp.int32)
    listing = members.reshape(top, rows).T
    listing = listing[jax.random.permutation(jax.random.fold_in(own, 1), rows)]
    offset_by = jax.random.randint(jax.random.fold_in(own, 2), (rows, 1), 0, top)
    return jnp.take_along_axis(listing, (jnp.arange(top)[None, :] + offset_by) % top, axis=1)


def shares(number_of, total, limit, lean, full):
    weights = [(1 << 20) // math.isqrt(rank ** lean) + 1 for rank in range(1, number_of + 1)]
    largest = limit if full else min(limit, max(-(-total // number_of), total * weights[0] // sum(weights)))
    least = 1 if total - largest >= number_of - 1 else 0
    given, surplus = [largest] + [least] * (number_of - 1), total - largest - least * (number_of - 1)
    while surplus > 0:
        candidates = [i for i in range(1, number_of) if given[i] < largest] or [i for i in range(1, number_of) if given[i] < limit]
        mass, left = sum([weights[i] for i in candidates]), surplus
        for i in candidates:
            extra = min(limit - given[i], max(1, left * weights[i] // mass), surplus)
            given[i] = given[i] + extra
            surplus = surplus - extra
    return np.array(given)


def setup_inputs(seed: int = 0) -> dict:
    keys = jax.random.split(jax.random.key(seed), 6)
    charges = draw_charges(jax.random.fold_in(keys[5], 71), 0)
    fractions = jnp.clip(1.0 * jax.random.uniform(keys[1], (3, ATOMS), jnp.float32) ** levels(keys[1], (3, ATOMS), ((1, 128),), -0.2, 0.2), 0.0, 1.0)
    inner_cell = plant(jax.random.randint(keys[2], (ATOMS,), 0, ZS * XW * YB), jax.random.fold_in(keys[2], 1), 0, (ZS * XW * YB) - 1).astype(jnp.int32)
    dest_slab_keys = jax.random.split(jax.random.fold_in(keys[3], 1), ATOMS // ATOMS_DEV)
    dest_slab_turns = jax.random.permutation(jax.random.fold_in(keys[3], 3), ATOMS // ATOMS_DEV)
    dest_slab = jax.vmap(lambda own, number: assign_block(jax.random.fold_in(keys[3], 2), own, number, ATOMS_DEV, N_SLAB, 1, CAP, 2))(dest_slab_keys, dest_slab_turns).reshape((ATOMS, 1))
    filter_amp = draw_filter_amp(jax.random.fold_in(keys[5], 71), 0)
    return dict(charges=charges, fractions=fractions, inner_cell=inner_cell, dest_slab=dest_slab, filter_amp=filter_amp)


def spline_weights(fraction):
    remainder = 1.0 - fraction
    square = fraction * fraction
    cubed = square * fraction
    return (remainder * remainder * remainder / 6.0, (3.0 * cubed - 6.0 * square + 4.0) / 6.0, (-3.0 * cubed + 3.0 * square + 3.0 * fraction + 1.0) / 6.0, cubed / 6.0)

def bump(magnitude, center, width):
    scaled = (magnitude - center * width) / width
    return jnp.exp(-0.5 * scaled * scaled)

def rounded(values):
    return lax.optimization_barrier(values.astype(jnp.bfloat16)).astype(jnp.float32)

def signed_freq(frequency, length):
    return jnp.where(frequency < length // 2, frequency, frequency - length).astype(jnp.float32)

def reference(charges, fractions, inner_cell, dest_slab, filter_amp):
    slab_depth = G // N_SLAB
    height = G // N_BRICK
    atom_index = jnp.arange(charges.shape[1], dtype=jnp.int32)
    device = atom_index // ATOMS_DEV
    slab_index = device // N_BRICK
    brick_index = device % N_BRICK
    z_cell = dest_slab[:, 0] * slab_depth + inner_cell % slab_depth
    y_cell = brick_index * height + inner_cell // (slab_depth * slab_depth)
    x_cell = slab_index * slab_depth + inner_cell // slab_depth % slab_depth
    weight_z = spline_weights(fractions[0])
    weight_y = spline_weights(fractions[1])
    weight_x = spline_weights(fractions[2])
    density = jnp.zeros((C, G, G, G), jnp.float32)
    for z_offset in range(4):
        for y_offset in range(4):
            plane_weight = rounded(weight_z[z_offset] * weight_y[y_offset])
            z_at = (z_cell + z_offset - 1) % G
            y_at = (y_cell + y_offset - 1) % G
            for x_offset in range(4):
                line_charge = rounded(charges * weight_x[x_offset][None, :])
                x_at = (x_cell + x_offset - 1) % G
                density = density.at[:, z_at, y_at, x_at].add(line_charge * plane_weight[None, :])
    frequency = signed_freq(jnp.arange(G, dtype=jnp.int32), G)
    squares = frequency[:, None, None] * frequency[:, None, None] + frequency[None, :, None] * frequency[None, :, None]
    squares = squares + frequency[None, None, :] * frequency[None, None, :]
    magnitude = jnp.sqrt(squares)
    amp_rows = filter_amp[jnp.arange(C, dtype=jnp.int32) % PAIRS]

    def one_channel(pieces):
        grid_values, amp_row = pieces
        gain_mesh = jnp.zeros((G, G, G), jnp.float32)
        for center in range(RADIAL):
            gain_mesh = gain_mesh + amp_row[center] * bump(magnitude, float(center), float(BIN))
        spectrum = jnp.fft.fftn(grid_values) * gain_mesh
        return jnp.real(jnp.fft.ifftn(spectrum)).astype(jnp.float32)
    potential = lax.map(one_channel, (density, amp_rows)).astype(jnp.bfloat16)
    potentials = jnp.zeros(charges.shape, jnp.float32)
    for z_offset in range(4):
        for y_offset in range(4):
            plane_weight = rounded(weight_z[z_offset] * weight_y[y_offset])
            z_at = (z_cell + z_offset - 1) % G
            y_at = (y_cell + y_offset - 1) % G
            for x_offset in range(4):
                x_at = (x_cell + x_offset - 1) % G
                values = potential[:, z_at, y_at, x_at].astype(jnp.float32)
                potentials = potentials + plane_weight[None, :] * values * weight_x[x_offset][None, :]
    return potentials
```

```python
import math

import numpy as np

import jax
import jax.numpy as jnp
import ml_dtypes
from jax import lax
from jax.experimental import pallas as pl
from jax.experimental.pallas import tpu as pltpu
from jax.sharding import PartitionSpec as P

G = 256
BIN = 16
SLABS = 32
BRICKS = 4
CAP = 64
BF = jnp.bfloat16
MESH = pl.DeviceIdType.MESH


def waves():
    places = np.arange(G)
    angles = 2.0 * np.pi * ((places[:, None] * places[None, :]) % G) / G
    return np.cos(angles), np.sin(angles)


def forward_table():
    cosine, sine = waves()
    return np.stack([np.stack([cosine, sine], 1), np.stack([-sine, cosine], 1)], 0)


def inverse_table():
    cosine, sine = waves()
    return np.stack([np.stack([cosine, -sine], 1), np.stack([sine, cosine], 1)], 0) / G


def spline_weights(fraction):
    remainder = 1.0 - fraction
    square = fraction * fraction
    cubed = square * fraction
    return (
        remainder * remainder * remainder / 6.0,
        (3.0 * cubed - 6.0 * square + 4.0) / 6.0,
        (-3.0 * cubed + 3.0 * square + 3.0 * fraction + 1.0) / 6.0,
        cubed / 6.0,
    )


GROUPS = 8
LANES = 256
PLACES = 132
WINDOW = 48
HALVES = 2
UNITS = 4
CHIP_ORDER = (
    (2, 2), (0, 1), (1, 0), (0, 3), (3, 0), (1, 2), (2, 1), (3, 2), (2, 3), (0, 2), (2, 0), (1, 1), (3, 3), (1, 3), (3, 1),
)
WIDE = 11
ROWS = 24
BACK_ROWS = 32
BACK_ORDER = (1, 2, 3, 4, 5, 6, 7, 8, 0, 9, 10)
VMEM_LIMIT = 56 * 1024 * 1024


def rounded_table(table):
    return np.ascontiguousarray(table).astype(ml_dtypes.bfloat16)


def rim_table():
    table = np.zeros((128, WIDE, 2, 64), np.float32)
    for x in range(WIDE):
        for r in range(2):
            for start, y in ((0, 0), (32, 1), (64, 63)):
                table[start + x * 2 + r, x, r, y] = 1.0
    return table.reshape(128, WIDE * 128)


def make_tables():
    forward = forward_table()
    inverse = inverse_table()
    both = np.stack(waves())
    where = np.arange(G)
    where = (where // 16 * 16 + where % 8 * 2 + where // 8 % 2 - 1) % G
    order = np.arange(G).reshape(SLABS, HALVES, 4).transpose(1, 0, 2).reshape(G)
    tables = (
        rim_table(),
        both[:, order][:, :, where].reshape(2, HALVES, 128, G).transpose(1, 0, 2, 3).reshape(512, G),
        both.reshape(512, G),
        forward.reshape(2, G, 2, BRICKS, 64).transpose(3, 2, 4, 0, 1).reshape(512, 512),
        inverse.reshape(2, BRICKS, 64, 2, G).transpose(3, 4, 1, 0, 2).reshape(512, 512),
        both.reshape(512, G) / G,
        both[:, where][:, :, order].reshape(512, G) / G,
    )
    return [rounded_table(table) for table in tables]


def dot(a, b):
    return lax.dot_general(a, b, (((1,), (0,)), ((), ())), preferred_element_type=jnp.float32)


def dot_nt(a, b):
    return lax.dot_general(a, b, (((1,), (1,)), ((), ())), preferred_element_type=jnp.float32)


def iota(shape, dim):
    return lax.broadcasted_iota(jnp.int32, shape, dim)


def double(values):
    high = values.astype(BF).astype(jnp.float32)
    return high, values - high


def dense(cell, fraction, places):
    weights = spline_weights(fraction)
    total = 0.0
    for j in range(4):
        total = total + jnp.where(places == cell + j, weights[j], 0.0)
    return total


def slot_lanes(g):
    return pl.ds(pl.multiple_of(g * LANES, LANES), LANES)


def line_weights(held, places):
    code = held[7:8, :].astype(jnp.int32)
    return dense((code >> 3) & 7, held[6:7, :], places)


def remote(src, dst, sems, at, target):
    copy = pltpu.make_async_remote_copy(
        src_ref=src,
        dst_ref=dst,
        send_sem=sems.at[0, at],
        recv_sem=sems.at[1, at],
        device_id=target,
        device_id_type=MESH,
    )
    copy.start()
    return copy


def kernel(
    charge_ref, frac_ref, cell_ref, target_ref, amp_ref,
    rim_far, zt_far, xt_far, yt_far, iyt_far, ixt_far, izt_far,
    out_ref,
    rim_ref, zt, xt, yt, iyt, ixt, izt,
    sorted_ref, read_ref, rank_ref, pairs, rim_pairs, rim_sums, rim_near, rim_part, mesh, mesh_back, slices,
    rim_out, rim_in, rim_out2, rim_in2, side_out, side_in, freq, freq_back,
    block, from_slab, to_brick, from_brick, back_brick, got_brick, back_slab, got_slab, after, potential, gain,
    table_sems, near_sems, slab_sems, brick_sems, brick_sems2, slab_sems2,
):
    slab = lax.axis_index("slab")
    brick = lax.axis_index("brick")
    left = {"slab": lax.rem(slab + SLABS - 1, SLABS)}
    right = {"slab": lax.rem(slab + 1, SLABS)}
    down = {"brick": lax.rem(brick + BRICKS - 1, BRICKS)}
    up = {"brick": lax.rem(brick + 1, BRICKS)}

    barrier = pltpu.get_barrier_semaphore()

    for step in range(1, SLABS):
        pl.semaphore_signal(
            barrier, inc=1, device_id={"slab": lax.rem(slab + step, SLABS)}, device_id_type=MESH
        )
    for step in range(1, BRICKS):
        pl.semaphore_signal(
            barrier, inc=1, device_id={"brick": lax.rem(brick + step, BRICKS)}, device_id_type=MESH
        )

    loads = []
    for at, (far, near) in enumerate(
        ((rim_far, rim_ref), (zt_far, zt), (xt_far, xt), (yt_far, yt), (iyt_far, iyt), (ixt_far, ixt), (izt_far, izt))
    ):
        load = pltpu.make_async_copy(far, near, table_sems.at[at])
        load.start()
        loads.append(load)

    atoms = charge_ref.shape[1]
    blocks = atoms // 128
    target = target_ref[...]
    here = jnp.where(iota((SLABS, atoms), 0) == target, 1.0, 0.0)
    stacked = jnp.concatenate([here[:, b * 128 : b * 128 + 128] for b in range(blocks)], axis=0).astype(BF)
    earlier = jnp.where(iota((128, 128), 0) < iota((128, 128), 1), 1.0, 0.0)
    counts = dot(stacked, jnp.concatenate([earlier, jnp.ones((128, 128), jnp.float32)], axis=1).astype(BF))
    ahead = jnp.zeros((SLABS, 128), jnp.float32)
    ranks = []
    for b in range(blocks):
        rows = slice(b * SLABS, b * SLABS + SLABS)
        ranks.append(counts[rows, 0:128] + ahead)
        ahead = ahead + counts[rows, 128:]
    rank = jnp.sum(here * jnp.concatenate(ranks, axis=1), axis=0, keepdims=True).astype(jnp.int32)
    rank_ref[...] = jnp.where((iota((128, atoms), 0) & 63) == rank, 1.0, 0.0).astype(BF)
    payload = jnp.concatenate([charge_ref[...], frac_ref[...], cell_ref[...].astype(jnp.float32)], axis=0)
    parts = double(payload)
    low_half = iota((8, 128), 1) < 64

    def sort(g, carry):
        rows = []
        for part in parts:
            rows += [jnp.where(target == g * 8 + t, part, 0.0) for t in range(8)]
        moved = dot_nt(jnp.concatenate(rows, axis=0).astype(BF), rank_ref[...])
        moved = moved[0:64] + moved[64:128]
        tiles = [
            jnp.where(low_half, moved[16 * t : 16 * t + 8], moved[16 * t + 8 : 16 * t + 16]) for t in range(4)
        ]
        sorted_ref[:, pl.ds(pl.multiple_of(g * 512, 512), 512)] = jnp.concatenate(tiles, axis=1)
        return carry

    lax.fori_loop(0, SLABS // 8, sort, 0, unroll=4)

    slab_of = iota((ROWS, LANES), 1) >> 6
    x_of = iota((ROWS, LANES), 0) >> 1
    first_part = (iota((ROWS, LANES), 0) & 1) == 0

    def line(held, p):
        return jnp.where(first_part, held[p : p + 1, :], held[2 + p : 3 + p, :]) * line_weights(held, x_of)

    rim_sums[...] = jnp.zeros(rim_sums.shape, jnp.float32)
    window_row = iota((WINDOW, LANES), 0)
    window_place = (window_row >> 4) * 16 + (window_row & 7) * 2 + ((window_row >> 3) & 1)
    slab_start = (iota((1, LANES), 1) >> 6) * 8

    def make_rims(g, carry):
        held = sorted_ref[:, slot_lanes(g)]
        code = held[7:8, :].astype(jnp.int32)
        wz = dense((code & 7) + slab_start, held[4:5, :], window_place)
        lines = [line(held, p) for p in range(2)]
        blocks, columns = [], []
        for h, y in enumerate((64, 65, -1)):
            rim = (wz * dense((code >> 6) - 1, held[5:6, :], y)).astype(BF)
            rim_pairs[g, pl.ds(h * WINDOW, WINDOW), :] = rim
            blocks.append(rim)
            rows = []
            for p in range(2):
                if h:
                    rows.append(jnp.zeros((32 * h, LANES), jnp.float32))
                rows += [lines[p], jnp.zeros((128 - ROWS - 32 * h, LANES), jnp.float32)]
            columns.append(jnp.concatenate(rows, axis=0).astype(BF))
        at = pl.ds(pl.multiple_of(g * 32, 16), WINDOW)
        rim_sums[at, :] = rim_sums[at, :] + dot_nt(
            jnp.concatenate(blocks, axis=1), jnp.concatenate(columns, axis=1)
        )
        return carry

    lax.fori_loop(0, GROUPS, make_rims, 0, unroll=4)
    rim_sums[0:16, :] = rim_sums[0:16, :] + rim_sums[G : G + 16, :]
    near = {}
    for p in range(2):
        rim_out[p] = rim_sums[0:G, p * 128 : p * 128 + 128].astype(BF)
    pl.semaphore_wait(barrier, SLABS - 1 + BRICKS - 1)
    for p in range(2):
        near["up", p] = remote(rim_out.at[p], rim_in.at[p, 0], near_sems, 8 * p, up)
        near["down", p] = remote(rim_out.at[p], rim_in.at[p, 1], near_sems, 8 * p + 1, down)

    mesh[:, 0:2] = jnp.zeros((2, 2, ROWS, 128), jnp.float32)

    def spread(p):
        def one(g, carry):
            held = sorted_ref[:, slot_lanes(g)]
            if p == 0:
                code = held[7:8, :].astype(jnp.int32)
                wz = dense(code & 7, held[4:5, :], iota((16, LANES), 0))
                wy = dense((code >> 6) - 1, held[5:6, :], iota((64, LANES), 0))
            own = line(held, p)
            lines = jnp.concatenate([jnp.where(slab_of == i, own, 0.0) for i in range(4)], axis=0).astype(BF)
            for z in (4, 8, 0):
                if p == 0:
                    pairs[g, z // 4] = jnp.concatenate(
                        [wy * wz[z + k : z + k + 1, :] for k in range(4)], axis=0
                    ).astype(BF)
                tile = dot_nt(lines, pairs[g, z // 4])
                for i in range(4):
                    for side in range(2):
                        at = g * 16 + i * 4 + z // 2 + side
                        part = tile[i * ROWS : i * ROWS + ROWS, side * 128 : side * 128 + 128]
                        mesh[p, at] = part if z else mesh[p, at] + part
            return carry

        lax.fori_loop(0, GROUPS, one, 0, unroll=4)
        mesh[p, 0] = mesh[p, 0] + mesh[p, 128]
        mesh[p, 1] = mesh[p, 1] + mesh[p, 129]

    low_all = iota((G, 128), 1) < 64
    sign = jnp.where(low_all, 1.0, -1.0)

    def turn(values):
        return sign[0 : values.shape[0]] * pltpu.roll(values, 64, 1)

    def cut(p):
        def one(step, carry):
            for part in range(3):
                turned = jnp.swapaxes(mesh[p, pl.ds(step * 8, 8), pl.ds(part * 8, 8), :], 0, 1)
                for x in range(4 * part, min(4 * part + 4, WIDE)):
                    a, b = turned[x % 4 * 2], turned[x % 4 * 2 + 1]
                    slices[p, x, pl.ds(pl.multiple_of(step * 16, 16), 16), :] = jnp.concatenate(
                        [
                            jnp.where(low_half, a, pltpu.roll(b, 64, 1)),
                            jnp.where(low_half, pltpu.roll(a, 64, 1), b),
                        ],
                        axis=0,
                    )
            return carry

        lax.fori_loop(0, 16, one, 0, unroll=2)

    def pack_rims(p, which):
        return dot_nt(
            jnp.concatenate([potential[p, x] for x in which], axis=1),
            jnp.concatenate([rim_ref[:, x * 128 : x * 128 + 128] for x in which], axis=1),
        )

    def both_rims(arrived, p):
        return jnp.where(low_all, arrived[p, 0].astype(jnp.float32), arrived[p, 1].astype(jnp.float32))

    def send_sides(p):
        near["up", p].wait_recv()
        near["down", p].wait_recv()
        added = dot(both_rims(rim_in, p).astype(BF), rim_ref[...])
        for x in range(WIDE):
            slices[p, x] = slices[p, x] + added[:, x * 128 : x * 128 + 128]
        side_out[p, 0] = slices[p, 9].astype(BF)
        side_out[p, 1] = slices[p, 10].astype(BF)
        side_out[p, 2] = slices[p, 0].astype(BF)
        near["right", p] = remote(
            side_out.at[p, pl.ds(0, 2)], side_in.at[p, pl.ds(0, 2)], near_sems, 8 * p + 2, right
        )
        near["left", p] = remote(side_out.at[p, pl.ds(2, 1)], side_in.at[p, pl.ds(2, 1)], near_sems, 8 * p + 3, left)

    def signed(k):
        return jnp.where(k < G // 2, k, k - G).astype(jnp.float32)

    def make_gain():
        fx = signed(brick * 64 + iota((64, G), 0))
        fy = signed(iota((64, G), 1))
        flat = fx * fx + fy * fy

        def one(index, carry):
            fz = signed(slab * 8 + index)
            magnitude = jnp.sqrt(fz * fz + flat)
            scaled = magnitude * (1.0 / BIN) - 8.0
            middle = jnp.exp(-0.5 * scaled * scaled)
            sums = [amp_ref[p, 8] * middle for p in range(2)]
            for way in (1, -1):
                ratio = jnp.exp(way * scaled - 0.5)
                bump = middle
                for center in range(8 + way, 16 if way > 0 else -1, way):
                    bump = bump * ratio
                    ratio = ratio * math.exp(-1.0)
                    sums = [sums[p] + amp_ref[p, center] * bump for p in range(2)]
            for p in range(2):
                gain[p, pl.ds(pl.multiple_of(index * 64, 64), 64), :] = sums[p]
            return carry

        lax.fori_loop(0, 8, one, 0)

    def send(src, dst, u, axis, me, count, sems):
        def one(step, carry):
            peer = lax.rem(me + step, count)
            pltpu.make_async_remote_copy(
                src_ref=src.at[u, peer],
                dst_ref=dst.at[u, me],
                send_sem=sems.at[0, u],
                recv_sem=sems.at[1, u],
                device_id={axis: peer},
                device_id_type=MESH,
            ).start()
            return carry

        lax.fori_loop(1, count, one, 0)

    def send_slabs(make, src, dst, u, sems):
        def to(peer):
            pltpu.make_async_remote_copy(
                src_ref=src.at[u, peer],
                dst_ref=dst.at[u, slab],
                send_sem=sems.at[0, u],
                recv_sem=sems.at[1, u],
                device_id={"slab": peer},
                device_id_type=MESH,
            ).start()

        for dy, dz in CHIP_ORDER:
            pair = lax.rem(slab // 8 + dy, 4) * 4 + lax.rem(slab // 2 + dz, 4)
            make(pair)
            to(2 * pair)
            to(2 * pair + 1)
        make(slab // 2)
        to(slab + 1 - 2 * lax.rem(slab, 2))
        dst[u, slab] = src[u, slab]

    def wait(buf, u, count, sems, which):
        part = buf.at[u, pl.ds(0, count - 1)]
        pltpu.make_async_copy(part, part, sems.at[which, u]).wait()

    def z_pair(p, x):
        rhs = jnp.concatenate([slices[p, x], slices[p, x + 1]], axis=1).astype(BF)
        out = dot(zt[...], rhs)
        for half in range(HALVES):
            for k in range(2):
                lanes = slice(k * 128, k * 128 + 128)
                u = out[half * 256 : half * 256 + 128, lanes]
                v = out[half * 256 + 128 : half * 256 + 256, lanes]
                freq[half, x - 1 + k] = u + turn(v)

    def inner_z(p):
        z_pair(p, 3)
        z_pair(p, 5)

    def outer_z(p):
        near["right", p].wait_recv()
        slices[p, 1] = slices[p, 1] + side_in[p, 0].astype(jnp.float32)
        slices[p, 2] = slices[p, 2] + side_in[p, 1].astype(jnp.float32)
        z_pair(p, 1)
        near["left", p].wait_recv()
        slices[p, 8] = slices[p, 8] + side_in[p, 2].astype(jnp.float32)
        z_pair(p, 7)

        for half in range(HALVES):

            def pack(pair, half=half):
                turned = jnp.swapaxes(freq[half, :, pl.ds(pl.multiple_of(pair * 8, 8), 8), :], 0, 1)
                block[2 * p + half, pl.ds(2 * pair, 2)] = turned.reshape(2, 2, 16, 128).astype(BF)

            send_slabs(pack, block, from_slab, 2 * p + half, slab_sems)

    def x_stage(u):
        wait(from_slab, u, SLABS, slab_sems, 1)
        cols = []
        for two in range(2):
            held = from_slab[u, :, two].astype(jnp.float32)
            cols += [held[:, 0:8].reshape(G, 128), held[:, 8:16].reshape(G, 128)]
        out = dot(xt[...], jnp.concatenate(cols, axis=1).astype(BF))
        for k in range(4):
            lanes = slice(k * 128, k * 128 + 128)
            done = (out[0:G, lanes] + turn(out[G:, lanes])).astype(BF)
            to_brick[u, :, k] = done.reshape(BRICKS, 64, 128)
        send(to_brick, from_brick, u, "brick", brick, BRICKS, brick_sems)
        from_brick[u, brick] = to_brick[u, brick]

    def y_stage(u):
        wait(from_brick, u, BRICKS, brick_sems, 1)
        rows = jnp.concatenate([from_brick[u, b].reshape(G, 128) for b in range(BRICKS)], axis=1)
        spectrum = dot(rows, yt[...])
        weight = gain[u // 2, pl.ds(u % 2 * 256, 256), :]
        filtered = jnp.concatenate([spectrum[:, :G] * weight, spectrum[:, G:] * weight], axis=1)
        back = dot(filtered.astype(BF), iyt[...]).astype(BF)
        for b in range(BRICKS):
            back_brick[u, b] = back[:, b * 128 : b * 128 + 128].reshape(4, 64, 128)
        send(back_brick, got_brick, u, "brick", brick, BRICKS, brick_sems2)
        got_brick[u, brick] = back_brick[u, brick]

    def i_stage(u):
        wait(got_brick, u, BRICKS, brick_sems2, 1)
        after[...] = dot(ixt[...], jnp.concatenate([got_brick[u, :, k].reshape(G, 128) for k in range(4)], axis=1))

        def make(pair):
            at = pl.multiple_of(pair * 16, 16)
            done = []
            for k in range(4):
                lanes = pl.ds(k * 128, 128)
                values = after[pl.ds(at, 16), lanes] - turn(after[pl.ds(G + at, 16), lanes])
                done.append(values.reshape(2, 8, 128))
            for two in range(2):
                back_slab[u, pl.ds(2 * pair, 2), two] = jnp.concatenate(done[2 * two : 2 * two + 2], axis=1).astype(BF)

        send_slabs(make, back_slab, got_slab, u, slab_sems2)

    def home(p):
        for half in range(HALVES):
            wait(got_slab, 2 * p + half, SLABS, slab_sems2, 1)

            def unpack(s, carry, half=half):
                rows = []
                for eight in range(2):
                    held = got_slab[2 * p + half, pl.ds(4 * s + 2 * eight, 2)].astype(jnp.float32)
                    rows.append(jnp.swapaxes(held.reshape(8, 8, 128), 0, 1))
                at = pl.multiple_of(half * 128 + s * 16, 16)
                freq_back[:, pl.ds(at, 16), :] = jnp.concatenate(rows, axis=1).astype(BF)
                return carry

            lax.fori_loop(0, SLABS // 4, unpack, 0, unroll=4)

        def back_z(x):
            out = dot(izt[...], jnp.concatenate([freq_back[x - 1], freq_back[x]], axis=1))
            for k in range(2):
                lanes = slice(k * 128, k * 128 + 128)
                potential[p, x + k] = (out[0:G, lanes] - turn(out[G:, lanes])).astype(BF)

        back_z(1)
        near["left2", p] = remote(
            potential.at[p, pl.ds(1, 2)], potential.at[p, pl.ds(9, 2)], near_sems, 8 * p + 4, left
        )
        back_z(7)
        near["right2", p] = remote(
            potential.at[p, pl.ds(8, 1)], potential.at[p, pl.ds(0, 1)], near_sems, 8 * p + 5, right
        )
        back_z(3)
        back_z(5)
        rim_part[...] = pack_rims(p, range(1, 9))
        place(p, 0)

    def place(p, part):
        def one(step, carry):
            rows = pl.ds(pl.multiple_of(step * 16, 16), 16)
            blank = jnp.zeros((8, 128), jnp.float32)
            turned = []
            for four in range(2):
                tiles = []
                for x in BACK_ORDER[8 * part + 4 * four : 8 * part + 4 * four + 4]:
                    held = potential[p, x, rows, :].astype(jnp.float32)
                    a, b = held[0:8], held[8:16]
                    tiles.append(jnp.where(low_half, a, pltpu.roll(b, 64, 1)))
                    tiles.append(jnp.where(low_half, pltpu.roll(a, 64, 1), b))
                tiles += [blank] * (8 - len(tiles))
                turned.append(jnp.swapaxes(jnp.stack(tiles, axis=0), 0, 1))
            mesh_back[p, pl.ds(step * 8, 8), pl.ds(part * 16, 16), :] = jnp.concatenate(turned, axis=1).astype(BF)
            return carry

        lax.fori_loop(0, 16, one, 0, unroll=4)

    def send_back_rims(p):
        near["left2", p].wait_recv()
        near["right2", p].wait_recv()
        rim_out2[p] = (rim_part[...] + pack_rims(p, (0, 9, 10))).astype(BF)
        near["down2", p] = remote(rim_out2.at[p], rim_in2.at[p, 0], near_sems, 8 * p + 6, down)
        near["up2", p] = remote(rim_out2.at[p], rim_in2.at[p, 1], near_sems, 8 * p + 7, up)
        place(p, 1)
        mesh_back[p, 128] = mesh_back[p, 0]
        mesh_back[p, 129] = mesh_back[p, 1]

    rim_x = iota((BACK_ROWS, LANES), 0) >> 1
    back_x = jnp.where(rim_x < 8, rim_x + 1, jnp.where(rim_x == 8, 0, jnp.where(rim_x < WIDE, rim_x, 99)))
    back_slab_of = iota((BACK_ROWS, LANES), 1) >> 6
    rim_of = iota((WINDOW, 128), 1) >> 5

    def reduce_x(own):
        return own[0:8] + own[8:16] + own[16:24] + own[24:32]

    def read_mesh(p):
        def one(g, carry):
            seen = jnp.zeros((4 * BACK_ROWS, LANES), jnp.float32)
            for z in range(0, 12, 4):
                rows = []
                for i in range(4):
                    at = g * 16 + i * 4 + z // 2
                    rows.append(jnp.concatenate([mesh_back[p, at + side] for side in range(2)], axis=1))
                seen = seen + dot(jnp.concatenate(rows, axis=0), pairs[g, z // 4])
            own = jnp.zeros((BACK_ROWS, LANES), jnp.float32)
            for i in range(4):
                own = own + jnp.where(back_slab_of == i, seen[i * BACK_ROWS : i * BACK_ROWS + BACK_ROWS], 0.0)
            read_ref[:, slot_lanes(g)] = reduce_x(own * line_weights(sorted_ref[:, slot_lanes(g)], back_x))
            return carry

        lax.fori_loop(0, GROUPS, one, 0, unroll=4)

    def read_rims(p):
        near["down2", p].wait_recv()
        near["up2", p].wait_recv()
        rims = both_rims(rim_in2, p)
        rim_near[0:G, :] = rims
        rim_near[G : G + 16, :] = rims[0:16]

        def one(g, carry):
            window = rim_near[pl.ds(pl.multiple_of(g * 32, 16), WINDOW), :]
            window = jnp.concatenate([jnp.where(rim_of == h, window, 0.0) for h in range(3)], axis=0).astype(BF)
            rim = lax.dot_general(
                window, rim_pairs[g], (((0,), (0,)), ((), ())), preferred_element_type=jnp.float32
            )
            own = rim[0:32] + rim[32:64] + rim[64:96]
            readings = reduce_x(own * line_weights(sorted_ref[:, slot_lanes(g)], rim_x)) + read_ref[:, slot_lanes(g)]
            readings = readings + pltpu.roll(readings, 4, 0)
            read_ref[:, slot_lanes(g)] = readings + pltpu.roll(readings, 2, 0)
            return carry

        lax.fori_loop(0, GROUPS, one, 0, unroll=4)

        def unsort(g, total):
            rows = []
            for part in double(read_ref[:, pl.ds(pl.multiple_of(g * 512, 512), 512)]):
                for t in range(4):
                    tile = part[:, t * 128 : t * 128 + 128]
                    rows += [jnp.where(low_half, tile, 0.0), jnp.where(low_half, 0.0, tile)]
            moved = dot(jnp.concatenate(rows, axis=0).astype(BF), rank_ref[...])
            moved = moved[0:64] + moved[64:128]
            for t in range(8):
                total = total + jnp.where(target == g * 8 + t, moved[t * 8 : t * 8 + 8], 0.0)
            return total

        total = lax.fori_loop(0, SLABS // 8, unsort, jnp.zeros((8, atoms), jnp.float32), unroll=4)
        out_ref[p : p + 1, :] = total[0:1]
        out_ref[2 + p : 3 + p, :] = total[1:2]

    spread(0)
    cut(0)
    loads[0].wait()
    send_sides(0)
    for load in loads[1:]:
        load.wait()
    inner_z(0)
    make_gain()
    outer_z(0)
    spread(1)
    cut(1)
    send_sides(1)
    x_stage(0)
    x_stage(1)
    inner_z(1)
    outer_z(1)
    y_stage(0)
    y_stage(1)
    x_stage(2)
    x_stage(3)
    i_stage(0)
    i_stage(1)
    y_stage(2)
    y_stage(3)
    i_stage(2)
    i_stage(3)
    home(0)
    send_back_rims(0)
    home(1)
    read_mesh(0)
    send_back_rims(1)
    read_rims(0)
    read_mesh(1)
    read_rims(1)
    for copy in near.values():
        copy.wait_send()
    for u in range(UNITS):
        wait(block, u, SLABS, slab_sems, 0)
        wait(back_slab, u, SLABS, slab_sems2, 0)
        wait(to_brick, u, BRICKS, brick_sems, 0)
        wait(back_brick, u, BRICKS, brick_sems2, 0)


def body(charges, fractions, inner_cell, dest_slab, filter_amp):
    vmem = pl.BlockSpec(memory_space=pltpu.VMEM)
    anywhere = pl.BlockSpec(memory_space=pl.ANY)
    dma = pltpu.SemaphoreType.DMA
    atoms = charges.shape[1]
    tables = [jnp.asarray(table) for table in make_tables()]
    to_slab = (UNITS, SLABS, 2, 16, 128)
    to_brick = (UNITS, BRICKS, 4, 64, 128)
    return pl.pallas_call(
        kernel,
        out_shape=jax.ShapeDtypeStruct((4, atoms), jnp.float32),
        in_specs=[vmem] * 4 + [pl.BlockSpec(memory_space=pltpu.SMEM)] + [anywhere] * len(tables),
        out_specs=vmem,
        scratch_shapes=[pltpu.VMEM(table.shape, BF) for table in tables]
        + [
            pltpu.VMEM((8, SLABS * CAP), jnp.float32),
            pltpu.VMEM((8, SLABS * CAP), jnp.float32),
            pltpu.VMEM((128, atoms), BF),
            pltpu.VMEM((GROUPS, 3, 256, LANES), BF),
            pltpu.VMEM((GROUPS, 3 * WINDOW, LANES), BF),
            pltpu.VMEM((G + 16, 256), jnp.float32),
            pltpu.VMEM((G + 16, 128), jnp.float32),
            pltpu.VMEM((G, 128), jnp.float32),
            pltpu.VMEM((2, PLACES, ROWS, 128), jnp.float32),
            pltpu.VMEM((2, PLACES, BACK_ROWS, 128), BF),
            pltpu.VMEM((2, WIDE, G, 128), jnp.float32),
            pltpu.VMEM((2, G, 128), BF),
            pltpu.VMEM((2, 2, G, 128), BF),
            pltpu.VMEM((2, G, 128), BF),
            pltpu.VMEM((2, 2, G, 128), BF),
            pltpu.VMEM((2, 3, G, 128), BF),
            pltpu.VMEM((2, 3, G, 128), BF),
            pltpu.VMEM((HALVES, 8, 128, 128), jnp.float32),
            pltpu.VMEM((8, G, 128), BF),
        ]
        + [pltpu.VMEM(to_slab, BF)] * 2
        + [pltpu.VMEM(to_brick, BF)] * 4
        + [pltpu.VMEM(to_slab, BF)] * 2
        + [
            pltpu.VMEM((512, 512), jnp.float32),
            pltpu.VMEM((2, WIDE, G, 128), BF),
            pltpu.VMEM((2, 512, G), jnp.float32),
            dma((len(tables),)),
            dma((2, 16)),
        ]
        + [dma((2, UNITS))] * 4,
        compiler_params=pltpu.CompilerParams(collective_id=0, has_side_effects=True, vmem_limit_bytes=VMEM_LIMIT),
    )(
        charges, fractions, inner_cell.reshape(1, -1), dest_slab.reshape(1, -1), filter_amp, *tables
    )


def solution(mesh):
    in_specs = (
        P(None, ("slab", "brick")),
        P(None, ("slab", "brick")),
        P(("slab", "brick")),
        P(("slab", "brick"), None),
        P(),
    )
    out_specs = P(None, ("slab", "brick"))
    return jax.shard_map(body, mesh=mesh, in_specs=in_specs, out_specs=out_specs, check_vma=False)
```

```python
import math

import numpy as np

import jax
import jax.numpy as jnp
import ml_dtypes
from jax import lax
from jax.experimental import pallas as pl
from jax.experimental.pallas import tpu as pltpu
from jax.sharding import PartitionSpec as P

G = 256
BIN = 16
SLABS = 32
BRICKS = 4
CAP = 64
BF = jnp.bfloat16
MESH = pl.DeviceIdType.MESH


def waves():
    places = np.arange(G)
    angles = 2.0 * np.pi * ((places[:, None] * places[None, :]) % G) / G
    return np.cos(angles), np.sin(angles)


def forward_table():
    cosine, sine = waves()
    return np.stack([np.stack([cosine, sine], 1), np.stack([-sine, cosine], 1)], 0)


def inverse_table():
    cosine, sine = waves()
    return np.stack([np.stack([cosine, -sine], 1), np.stack([sine, cosine], 1)], 0) / G


def spline_weights(fraction):
    remainder = 1.0 - fraction
    square = fraction * fraction
    cubed = square * fraction
    return (
        remainder * remainder * remainder / 6.0,
        (3.0 * cubed - 6.0 * square + 4.0) / 6.0,
        (-3.0 * cubed + 3.0 * square + 3.0 * fraction + 1.0) / 6.0,
        cubed / 6.0,
    )


GROUPS = 8
LANES = 256
PLACES = 132
WINDOW = 48
HALVES = 2
UNITS = 4
CHIP_ORDER = (
    (2, 2), (0, 1), (1, 0), (0, 3), (3, 0), (1, 2), (2, 1), (3, 2), (2, 3), (0, 2), (2, 0), (1, 1), (3, 3), (1, 3), (3, 1),
)
WIDE = 11
ORDER = (1, 2, 3, 4, 5, 6, 7, 8, 0, 9, 10)
SIDES = (9, 10, 0)
EDGES = (1, 2, 8)
ROWS = 24
BACK_ROWS = 32
VMEM_LIMIT = 56 * 1024 * 1024


def rounded_table(table):
    return np.ascontiguousarray(table).astype(ml_dtypes.bfloat16)


def rim_table():
    table = np.zeros((128, WIDE, 2, 64), np.float32)
    for at, x in enumerate(ORDER):
        for r in range(2):
            for start, y in ((0, 0), (32, 1), (64, 63)):
                table[start + at * 2 + r, x, r, y] = 1.0
    return table.reshape(128, WIDE * 128)


def make_tables():
    forward = forward_table()
    inverse = inverse_table()
    both = np.stack(waves())
    where = np.arange(G)
    where = (where // 16 * 16 + where % 8 * 2 + where // 8 % 2 - 1) % G
    order = np.arange(G).reshape(SLABS, HALVES, 4).transpose(1, 0, 2).reshape(G)
    tables = (
        rim_table(),
        both[:, order][:, :, where].reshape(2, HALVES, 128, G).transpose(1, 0, 2, 3).reshape(512, G),
        both.reshape(512, G),
        forward.reshape(2, G, 2, BRICKS, 64).transpose(3, 2, 4, 0, 1).reshape(512, 512),
        inverse.reshape(2, BRICKS, 64, 2, G).transpose(3, 4, 1, 0, 2).reshape(512, 512),
        both.reshape(512, G) / G,
        both[:, where][:, :, order].reshape(512, G) / G,
    )
    return [rounded_table(table) for table in tables]


def dot(a, b):
    return lax.dot_general(a, b, (((1,), (0,)), ((), ())), preferred_element_type=jnp.float32)


def dot_nt(a, b):
    return lax.dot_general(a, b, (((1,), (1,)), ((), ())), preferred_element_type=jnp.float32)


def iota(shape, dim):
    return lax.broadcasted_iota(jnp.int32, shape, dim)


def double(values):
    high = values.astype(BF).astype(jnp.float32)
    return high, values - high


def dense(cell, weights, places):
    total = 0.0
    for j in range(4):
        total = total + jnp.where(places == cell + j, weights[j], 0.0)
    return total


def slot_lanes(g):
    return pl.ds(pl.multiple_of(g * LANES, LANES), LANES)


def row_x(shape):
    at = iota(shape, 0) >> 1
    return jnp.where(at < 8, at + 1, jnp.where(at == 8, 0, jnp.where(at < WIDE, at, 99)))


def remote(src, dst, sems, at, target):
    copy = pltpu.make_async_remote_copy(
        src_ref=src,
        dst_ref=dst,
        send_sem=sems.at[0, at],
        recv_sem=sems.at[1, at],
        device_id=target,
        device_id_type=MESH,
    )
    copy.start()
    return copy


def kernel(
    charge_ref, frac_ref, cell_ref, target_ref, amp_ref,
    rim_far, zt_far, xt_far, yt_far, iyt_far, ixt_far, izt_far,
    out_ref,
    rim_ref, zt, xt, yt, iyt, ixt, izt,
    sorted_ref, spline_ref, line_ref, read_ref, rank_ref, pairs, rim_pairs, rim_sums, rim_near, rim_part, mesh, mesh_back, added, edges, slices,
    rim_out, rim_in, rim_out2, rim_in2, side_out, side_in, freq, freq_back,
    block, from_slab, to_brick, from_brick, back_brick, got_brick, back_slab, got_slab, after, potential, gain,
    table_sems, near_sems, slab_sems, brick_sems, brick_sems2, slab_sems2,
):
    slab = lax.axis_index("slab")
    brick = lax.axis_index("brick")
    left = {"slab": lax.rem(slab + SLABS - 1, SLABS)}
    right = {"slab": lax.rem(slab + 1, SLABS)}
    down = {"brick": lax.rem(brick + BRICKS - 1, BRICKS)}
    up = {"brick": lax.rem(brick + 1, BRICKS)}

    barrier = pltpu.get_barrier_semaphore()

    for step in range(1, SLABS):
        pl.semaphore_signal(
            barrier, inc=1, device_id={"slab": lax.rem(slab + step, SLABS)}, device_id_type=MESH
        )
    for step in range(1, BRICKS):
        pl.semaphore_signal(
            barrier, inc=1, device_id={"brick": lax.rem(brick + step, BRICKS)}, device_id_type=MESH
        )

    loads = []
    for at, (far, near) in enumerate(
        ((rim_far, rim_ref), (zt_far, zt), (xt_far, xt), (yt_far, yt), (iyt_far, iyt), (ixt_far, ixt), (izt_far, izt))
    ):
        load = pltpu.make_async_copy(far, near, table_sems.at[at])
        load.start()
        loads.append(load)

    atoms = charge_ref.shape[1]
    blocks = atoms // 128
    target = target_ref[...]
    here = jnp.where(iota((SLABS, atoms), 0) == target, 1.0, 0.0)
    stacked = jnp.concatenate([here[:, b * 128 : b * 128 + 128] for b in range(blocks)], axis=0).astype(BF)
    earlier = jnp.where(iota((128, 128), 0) < iota((128, 128), 1), 1.0, 0.0)
    counts = dot(stacked, jnp.concatenate([earlier, jnp.ones((128, 128), jnp.float32)], axis=1).astype(BF))
    ahead = jnp.zeros((SLABS, 128), jnp.float32)
    ranks = []
    for b in range(blocks):
        rows = slice(b * SLABS, b * SLABS + SLABS)
        ranks.append(counts[rows, 0:128] + ahead)
        ahead = ahead + counts[rows, 128:]
    rank = jnp.sum(here * jnp.concatenate(ranks, axis=1), axis=0, keepdims=True).astype(jnp.int32)
    rank_ref[...] = jnp.where((iota((128, atoms), 0) & 63) == rank, 1.0, 0.0).astype(BF)
    payload = jnp.concatenate([charge_ref[...], frac_ref[...], cell_ref[...].astype(jnp.float32)], axis=0)
    parts = double(payload)
    low_half = iota((8, 128), 1) < 64

    def sort(g, carry):
        rows = []
        for part in parts:
            rows += [jnp.where(target == g * 8 + t, part, 0.0) for t in range(8)]
        moved = dot_nt(jnp.concatenate(rows, axis=0).astype(BF), rank_ref[...])
        moved = moved[0:64] + moved[64:128]
        tiles = [
            jnp.where(low_half, moved[16 * t : 16 * t + 8], moved[16 * t + 8 : 16 * t + 16]) for t in range(4)
        ]
        sorted_ref[:, pl.ds(pl.multiple_of(g * 512, 512), 512)] = jnp.concatenate(tiles, axis=1)
        return carry

    lax.fori_loop(0, SLABS // 8, sort, 0, unroll=4)

    for j, weight in enumerate(spline_weights(sorted_ref[4:7, :])):
        spline_ref[j, 0:3, :] = weight

    def along(dim, g):
        return [spline_ref[j, dim : dim + 1, slot_lanes(g)] for j in range(4)]

    slab_of = iota((ROWS, LANES), 1) >> 6
    first_part = (iota((ROWS, LANES), 0) & 1) == 0
    x_of = row_x((BACK_ROWS, LANES))

    def line(held, g, p):
        return jnp.where(first_part, held[p : p + 1, :], held[2 + p : 3 + p, :]) * line_ref[g, 0:ROWS, :]

    rim_sums[...] = jnp.zeros(rim_sums.shape, jnp.float32)
    window_row = iota((WINDOW, LANES), 0)
    window_place = (window_row >> 4) * 16 + (window_row & 7) * 2 + ((window_row >> 3) & 1)
    slab_start = (iota((1, LANES), 1) >> 6) * 8

    def make_rims(g, carry):
        held = sorted_ref[:, slot_lanes(g)]
        code = held[7:8, :].astype(jnp.int32)
        line_ref[g] = dense((code >> 3) & 7, along(2, g), x_of)
        wz = dense((code & 7) + slab_start, along(0, g), window_place)
        lines = [line(held, g, p) for p in range(2)]
        blocks, columns = [], []
        for h, y in enumerate((64, 65, -1)):
            rim = (wz * dense((code >> 6) - 1, along(1, g), y)).astype(BF)
            rim_pairs[g, pl.ds(h * WINDOW, WINDOW), :] = rim
            blocks.append(rim)
            rows = []
            for p in range(2):
                if h:
                    rows.append(jnp.zeros((32 * h, LANES), jnp.float32))
                rows += [lines[p], jnp.zeros((128 - ROWS - 32 * h, LANES), jnp.float32)]
            columns.append(jnp.concatenate(rows, axis=0).astype(BF))
        at = pl.ds(pl.multiple_of(g * 32, 16), WINDOW)
        rim_sums[at, :] = rim_sums[at, :] + dot_nt(
            jnp.concatenate(blocks, axis=1), jnp.concatenate(columns, axis=1)
        )
        return carry

    lax.fori_loop(0, GROUPS, make_rims, 0, unroll=4)
    rim_sums[0:16, :] = rim_sums[0:16, :] + rim_sums[G : G + 16, :]
    near = {}
    for p in range(2):
        rim_out[p] = rim_sums[0:G, p * 128 : p * 128 + 128].astype(BF)
    pl.semaphore_wait(barrier, SLABS - 1 + BRICKS - 1)
    for p in range(2):
        near["up", p] = remote(rim_out.at[p], rim_in.at[p, 0], near_sems, 8 * p, up)
        near["down", p] = remote(rim_out.at[p], rim_in.at[p, 1], near_sems, 8 * p + 1, down)

    mesh[:, 0:2] = jnp.zeros((2, 2, ROWS, 128), jnp.float32)

    def spread(p):
        def one(g, carry):
            held = sorted_ref[:, slot_lanes(g)]
            if p == 0:
                code = held[7:8, :].astype(jnp.int32)
                wz = dense(code & 7, along(0, g), iota((16, LANES), 0))
                wy = dense((code >> 6) - 1, along(1, g), iota((64, LANES), 0))
            own = line(held, g, p)
            lines = jnp.concatenate([jnp.where(slab_of == i, own, 0.0) for i in range(4)], axis=0).astype(BF)
            for z in (4, 8, 0):
                if p == 0:
                    pairs[g, z // 4] = jnp.concatenate(
                        [wy * wz[z + k : z + k + 1, :] for k in range(4)], axis=0
                    ).astype(BF)
                tile = dot_nt(lines, pairs[g, z // 4])
                for i in range(4):
                    for side in range(2):
                        at = g * 16 + i * 4 + z // 2 + side
                        part = tile[i * ROWS : i * ROWS + ROWS, side * 128 : side * 128 + 128]
                        mesh[p, at] = part if z else mesh[p, at] + part
            return carry

        lax.fori_loop(0, GROUPS, one, 0, unroll=4)
        mesh[p, 0] = mesh[p, 0] + mesh[p, 128]
        mesh[p, 1] = mesh[p, 1] + mesh[p, 129]

    low_all = iota((G, 128), 1) < 64
    sign = jnp.where(low_all, 1.0, -1.0)

    def turn(values):
        return sign[0 : values.shape[0]] * pltpu.roll(values, 64, 1)

    def pack_rims(p, which):
        return dot_nt(
            jnp.concatenate([potential[p, x] for x in which], axis=1),
            jnp.concatenate([rim_ref[:, x * 128 : x * 128 + 128] for x in which], axis=1),
        )

    def both_rims(arrived, p):
        return jnp.where(low_all, arrived[p, 0].astype(jnp.float32), arrived[p, 1].astype(jnp.float32))

    def cut(p):
        near["up", p].wait_recv()
        near["down", p].wait_recv()
        added[...] = dot(both_rims(rim_in, p).astype(BF), rim_ref[...]).astype(BF)

        def one(step, carry):
            rows = pl.ds(pl.multiple_of(step * 16, 16), 16)
            for part in range(3):
                turned = jnp.swapaxes(mesh[p, pl.ds(step * 8, 8), pl.ds(part * 8, 8), :], 0, 1)
                for at, x in enumerate(ORDER[4 * part : 4 * part + 4]):
                    a, b = turned[2 * at], turned[2 * at + 1]
                    core = jnp.concatenate(
                        [
                            jnp.where(low_half, a, pltpu.roll(b, 64, 1)),
                            jnp.where(low_half, pltpu.roll(a, 64, 1), b),
                        ],
                        axis=0,
                    )
                    core = core + added[rows, pl.ds(x * 128, 128)].astype(jnp.float32)
                    if x in SIDES:
                        side_out[p, SIDES.index(x), rows, :] = core.astype(BF)
                    elif x in EDGES:
                        edges[p, EDGES.index(x), rows, :] = core
                    else:
                        slices[p, x, rows, :] = core.astype(BF)
            return carry

        lax.fori_loop(0, 16, one, 0, unroll=2)
        near["right", p] = remote(
            side_out.at[p, pl.ds(0, 2)], side_in.at[p, pl.ds(0, 2)], near_sems, 8 * p + 2, right
        )
        near["left", p] = remote(side_out.at[p, pl.ds(2, 1)], side_in.at[p, pl.ds(2, 1)], near_sems, 8 * p + 3, left)

    def signed(k):
        return jnp.where(k < G // 2, k, k - G).astype(jnp.float32)

    def make_gain():
        fx = signed(brick * 64 + iota((64, G), 0))
        fy = signed(iota((64, G), 1))
        flat = fx * fx + fy * fy

        def one(index, carry):
            fz = signed(slab * 8 + index)
            magnitude = jnp.sqrt(fz * fz + flat)
            scaled = magnitude * (1.0 / BIN) - 8.0
            middle = jnp.exp(-0.5 * scaled * scaled)
            sums = [amp_ref[p, 8] * middle for p in range(2)]
            for way in (1, -1):
                ratio = jnp.exp(way * scaled - 0.5)
                bump = middle
                for center in range(8 + way, 16 if way > 0 else -1, way):
                    bump = bump * ratio
                    ratio = ratio * math.exp(-1.0)
                    sums = [sums[p] + amp_ref[p, center] * bump for p in range(2)]
            for p in range(2):
                gain[p, pl.ds(pl.multiple_of(index * 64, 64), 64), :] = sums[p]
            return carry

        lax.fori_loop(0, 8, one, 0)

    def send(src, dst, u, axis, me, count, sems):
        def one(step, carry):
            peer = lax.rem(me + step, count)
            pltpu.make_async_remote_copy(
                src_ref=src.at[u, peer],
                dst_ref=dst.at[u, me],
                send_sem=sems.at[0, u],
                recv_sem=sems.at[1, u],
                device_id={axis: peer},
                device_id_type=MESH,
            ).start()
            return carry

        lax.fori_loop(1, count, one, 0)

    def send_slabs(make, src, dst, u, sems):
        def to(peer):
            pltpu.make_async_remote_copy(
                src_ref=src.at[u, peer],
                dst_ref=dst.at[u, slab],
                send_sem=sems.at[0, u],
                recv_sem=sems.at[1, u],
                device_id={"slab": peer},
                device_id_type=MESH,
            ).start()

        for dy, dz in CHIP_ORDER:
            pair = lax.rem(slab // 8 + dy, 4) * 4 + lax.rem(slab // 2 + dz, 4)
            make(pair)
            to(2 * pair)
            to(2 * pair + 1)
        make(slab // 2)
        to(slab + 1 - 2 * lax.rem(slab, 2))
        dst[u, slab] = src[u, slab]

    def wait(buf, u, count, sems, which):
        part = buf.at[u, pl.ds(0, count - 1)]
        pltpu.make_async_copy(part, part, sems.at[which, u]).wait()

    def z_pair(p, x):
        out = dot(zt[...], jnp.concatenate([slices[p, x], slices[p, x + 1]], axis=1))
        for half in range(HALVES):
            for k in range(2):
                lanes = slice(k * 128, k * 128 + 128)
                u = out[half * 256 : half * 256 + 128, lanes]
                v = out[half * 256 + 128 : half * 256 + 256, lanes]
                freq[half, x - 1 + k] = u + turn(v)

    def inner_z(p):
        z_pair(p, 3)
        z_pair(p, 5)

    def outer_z(p):
        near["right", p].wait_recv()
        for at in range(2):
            slices[p, EDGES[at]] = (edges[p, at] + side_in[p, at].astype(jnp.float32)).astype(BF)
        z_pair(p, 1)
        near["left", p].wait_recv()
        slices[p, EDGES[2]] = (edges[p, 2] + side_in[p, 2].astype(jnp.float32)).astype(BF)
        z_pair(p, 7)
        for half in range(HALVES):

            def pack(pair, half=half):
                turned = jnp.swapaxes(freq[half, :, pl.ds(pl.multiple_of(pair * 8, 8), 8), :], 0, 1)
                block[2 * p + half, pl.ds(2 * pair, 2)] = turned.reshape(2, 2, 16, 128).astype(BF)

            send_slabs(pack, block, from_slab, 2 * p + half, slab_sems)

    def x_stage(u):
        wait(from_slab, u, SLABS, slab_sems, 1)
        cols = []
        for two in range(2):
            held = from_slab[u, :, two].astype(jnp.float32)
            cols += [held[:, 0:8].reshape(G, 128), held[:, 8:16].reshape(G, 128)]
        out = dot(xt[...], jnp.concatenate(cols, axis=1).astype(BF))
        for k in range(4):
            lanes = slice(k * 128, k * 128 + 128)
            done = (out[0:G, lanes] + turn(out[G:, lanes])).astype(BF)
            to_brick[u, :, k] = done.reshape(BRICKS, 64, 128)
        send(to_brick, from_brick, u, "brick", brick, BRICKS, brick_sems)
        from_brick[u, brick] = to_brick[u, brick]

    def y_stage(u):
        wait(from_brick, u, BRICKS, brick_sems, 1)
        rows = jnp.concatenate([from_brick[u, b].reshape(G, 128) for b in range(BRICKS)], axis=1)
        spectrum = dot(rows, yt[...])
        weight = gain[u // 2, pl.ds(u % 2 * 256, 256), :]
        filtered = jnp.concatenate([spectrum[:, :G] * weight, spectrum[:, G:] * weight], axis=1)
        back = dot(filtered.astype(BF), iyt[...]).astype(BF)
        for b in range(BRICKS):
            back_brick[u, b] = back[:, b * 128 : b * 128 + 128].reshape(4, 64, 128)
        send(back_brick, got_brick, u, "brick", brick, BRICKS, brick_sems2)
        got_brick[u, brick] = back_brick[u, brick]

    def i_stage(u):
        wait(got_brick, u, BRICKS, brick_sems2, 1)
        after[...] = dot(ixt[...], jnp.concatenate([got_brick[u, :, k].reshape(G, 128) for k in range(4)], axis=1))

        def make(pair):
            at = pl.multiple_of(pair * 16, 16)
            done = []
            for k in range(4):
                lanes = pl.ds(k * 128, 128)
                values = after[pl.ds(at, 16), lanes] - turn(after[pl.ds(G + at, 16), lanes])
                done.append(values.reshape(2, 8, 128))
            for two in range(2):
                back_slab[u, pl.ds(2 * pair, 2), two] = jnp.concatenate(done[2 * two : 2 * two + 2], axis=1).astype(BF)

        send_slabs(make, back_slab, got_slab, u, slab_sems2)

    def home(p):
        for half in range(HALVES):
            wait(got_slab, 2 * p + half, SLABS, slab_sems2, 1)

            def unpack(s, carry, half=half):
                rows = []
                for eight in range(2):
                    held = got_slab[2 * p + half, pl.ds(4 * s + 2 * eight, 2)].astype(jnp.float32)
                    rows.append(jnp.swapaxes(held.reshape(8, 8, 128), 0, 1))
                at = pl.multiple_of(half * 128 + s * 16, 16)
                freq_back[:, pl.ds(at, 16), :] = jnp.concatenate(rows, axis=1).astype(BF)
                return carry

            lax.fori_loop(0, SLABS // 4, unpack, 0, unroll=4)

        def back_z(x):
            out = dot(izt[...], jnp.concatenate([freq_back[x - 1], freq_back[x]], axis=1))
            for k in range(2):
                lanes = slice(k * 128, k * 128 + 128)
                potential[p, x + k] = (out[0:G, lanes] - turn(out[G:, lanes])).astype(BF)

        back_z(1)
        near["left2", p] = remote(
            potential.at[p, pl.ds(1, 2)], potential.at[p, pl.ds(9, 2)], near_sems, 8 * p + 4, left
        )
        back_z(7)
        near["right2", p] = remote(
            potential.at[p, pl.ds(8, 1)], potential.at[p, pl.ds(0, 1)], near_sems, 8 * p + 5, right
        )
        back_z(3)
        back_z(5)
        rim_part[...] = pack_rims(p, range(1, 9))
        place(p, 0)

    def place(p, part):
        def one(step, carry):
            rows = pl.ds(pl.multiple_of(step * 16, 16), 16)
            blank = jnp.zeros((8, 128), jnp.float32)
            turned = []
            for four in range(2):
                if 8 * part + 4 * four >= WIDE:
                    turned.append(jnp.zeros((8, 8, 128), jnp.float32))
                    continue
                tiles = []
                for x in ORDER[8 * part + 4 * four : 8 * part + 4 * four + 4]:
                    held = potential[p, x, rows, :].astype(jnp.float32)
                    a, b = held[0:8], held[8:16]
                    tiles.append(jnp.where(low_half, a, pltpu.roll(b, 64, 1)))
                    tiles.append(jnp.where(low_half, pltpu.roll(a, 64, 1), b))
                tiles += [blank] * (8 - len(tiles))
                turned.append(jnp.swapaxes(jnp.stack(tiles, axis=0), 0, 1))
            mesh_back[p, pl.ds(step * 8, 8), pl.ds(part * 16, 16), :] = jnp.concatenate(turned, axis=1).astype(BF)
            return carry

        lax.fori_loop(0, 16, one, 0, unroll=4)

    def send_back_rims(p):
        near["left2", p].wait_recv()
        near["right2", p].wait_recv()
        rim_out2[p] = (rim_part[...] + pack_rims(p, (0, 9, 10))).astype(BF)
        near["down2", p] = remote(rim_out2.at[p], rim_in2.at[p, 0], near_sems, 8 * p + 6, down)
        near["up2", p] = remote(rim_out2.at[p], rim_in2.at[p, 1], near_sems, 8 * p + 7, up)
        place(p, 1)
        mesh_back[p, 128] = mesh_back[p, 0]
        mesh_back[p, 129] = mesh_back[p, 1]

    back_slab_of = iota((BACK_ROWS, LANES), 1) >> 6
    rim_of = iota((WINDOW, 128), 1) >> 5

    def reduce_x(own):
        return own[0:8] + own[8:16] + own[16:24] + own[24:32]

    def read_mesh(p):
        def one(g, carry):
            seen = jnp.zeros((4 * BACK_ROWS, LANES), jnp.float32)
            for z in range(0, 12, 4):
                rows = []
                for i in range(4):
                    at = g * 16 + i * 4 + z // 2
                    rows.append(jnp.concatenate([mesh_back[p, at + side] for side in range(2)], axis=1))
                seen = seen + dot(jnp.concatenate(rows, axis=0), pairs[g, z // 4])
            own = jnp.zeros((BACK_ROWS, LANES), jnp.float32)
            for i in range(4):
                own = own + jnp.where(back_slab_of == i, seen[i * BACK_ROWS : i * BACK_ROWS + BACK_ROWS], 0.0)
            read_ref[:, slot_lanes(g)] = reduce_x(own * line_ref[g])
            return carry

        lax.fori_loop(0, GROUPS, one, 0, unroll=4)

    def read_rims(p):
        near["down2", p].wait_recv()
        near["up2", p].wait_recv()
        rims = both_rims(rim_in2, p)
        rim_near[0:G, :] = rims
        rim_near[G : G + 16, :] = rims[0:16]

        def one(g, carry):
            window = rim_near[pl.ds(pl.multiple_of(g * 32, 16), WINDOW), :]
            window = jnp.concatenate([jnp.where(rim_of == h, window, 0.0) for h in range(3)], axis=0).astype(BF)
            rim = lax.dot_general(
                window, rim_pairs[g], (((0,), (0,)), ((), ())), preferred_element_type=jnp.float32
            )
            own = rim[0:32] + rim[32:64] + rim[64:96]
            readings = reduce_x(own * line_ref[g]) + read_ref[:, slot_lanes(g)]
            readings = readings + pltpu.roll(readings, 4, 0)
            read_ref[:, slot_lanes(g)] = readings + pltpu.roll(readings, 2, 0)
            return carry

        lax.fori_loop(0, GROUPS, one, 0, unroll=4)

        def unsort(g, total):
            rows = []
            for part in double(read_ref[:, pl.ds(pl.multiple_of(g * 512, 512), 512)]):
                for t in range(4):
                    tile = part[:, t * 128 : t * 128 + 128]
                    rows += [jnp.where(low_half, tile, 0.0), jnp.where(low_half, 0.0, tile)]
            moved = dot(jnp.concatenate(rows, axis=0).astype(BF), rank_ref[...])
            moved = moved[0:64] + moved[64:128]
            for t in range(8):
                total = total + jnp.where(target == g * 8 + t, moved[t * 8 : t * 8 + 8], 0.0)
            return total

        total = lax.fori_loop(0, SLABS // 8, unsort, jnp.zeros((8, atoms), jnp.float32), unroll=4)
        out_ref[p : p + 1, :] = total[0:1]
        out_ref[2 + p : 3 + p, :] = total[1:2]

    spread(0)
    loads[0].wait()
    cut(0)
    for load in loads[1:]:
        load.wait()
    inner_z(0)
    make_gain()
    outer_z(0)
    spread(1)
    cut(1)
    x_stage(0)
    x_stage(1)
    inner_z(1)
    outer_z(1)
    y_stage(0)
    y_stage(1)
    x_stage(2)
    x_stage(3)
    i_stage(0)
    i_stage(1)
    y_stage(2)
    y_stage(3)
    i_stage(2)
    i_stage(3)
    home(0)
    send_back_rims(0)
    home(1)
    read_mesh(0)
    send_back_rims(1)
    read_rims(0)
    read_mesh(1)
    read_rims(1)
    for copy in near.values():
        copy.wait_send()
    for u in range(UNITS):
        wait(block, u, SLABS, slab_sems, 0)
        wait(back_slab, u, SLABS, slab_sems2, 0)
        wait(to_brick, u, BRICKS, brick_sems, 0)
        wait(back_brick, u, BRICKS, brick_sems2, 0)


def body(charges, fractions, inner_cell, dest_slab, filter_amp):
    vmem = pl.BlockSpec(memory_space=pltpu.VMEM)
    anywhere = pl.BlockSpec(memory_space=pl.ANY)
    dma = pltpu.SemaphoreType.DMA
    atoms = charges.shape[1]
    tables = [jnp.asarray(table) for table in make_tables()]
    to_slab = (UNITS, SLABS, 2, 16, 128)
    to_brick = (UNITS, BRICKS, 4, 64, 128)
    return pl.pallas_call(
        kernel,
        out_shape=jax.ShapeDtypeStruct((4, atoms), jnp.float32),
        in_specs=[vmem] * 4 + [pl.BlockSpec(memory_space=pltpu.SMEM)] + [anywhere] * len(tables),
        out_specs=vmem,
        scratch_shapes=[pltpu.VMEM(table.shape, BF) for table in tables]
        + [
            pltpu.VMEM((8, SLABS * CAP), jnp.float32),
            pltpu.VMEM((4, 8, SLABS * CAP), jnp.float32),
            pltpu.VMEM((GROUPS, BACK_ROWS, LANES), jnp.float32),
            pltpu.VMEM((8, SLABS * CAP), jnp.float32),
            pltpu.VMEM((128, atoms), BF),
            pltpu.VMEM((GROUPS, 3, 256, LANES), BF),
            pltpu.VMEM((GROUPS, 3 * WINDOW, LANES), BF),
            pltpu.VMEM((G + 16, 256), jnp.float32),
            pltpu.VMEM((G + 16, 128), jnp.float32),
            pltpu.VMEM((G, 128), jnp.float32),
            pltpu.VMEM((2, PLACES, ROWS, 128), jnp.float32),
            pltpu.VMEM((2, PLACES, BACK_ROWS, 128), BF),
            pltpu.VMEM((G, WIDE * 128), BF),
            pltpu.VMEM((2, 3, G, 128), jnp.float32),
            pltpu.VMEM((2, WIDE, G, 128), BF),
            pltpu.VMEM((2, G, 128), BF),
            pltpu.VMEM((2, 2, G, 128), BF),
            pltpu.VMEM((2, G, 128), BF),
            pltpu.VMEM((2, 2, G, 128), BF),
            pltpu.VMEM((2, 3, G, 128), BF),
            pltpu.VMEM((2, 3, G, 128), BF),
            pltpu.VMEM((HALVES, 8, 128, 128), jnp.float32),
            pltpu.VMEM((8, G, 128), BF),
        ]
        + [pltpu.VMEM(to_slab, BF)] * 2
        + [pltpu.VMEM(to_brick, BF)] * 4
        + [pltpu.VMEM(to_slab, BF)] * 2
        + [
            pltpu.VMEM((512, 512), jnp.float32),
            pltpu.VMEM((2, WIDE, G, 128), BF),
            pltpu.VMEM((2, 512, G), jnp.float32),
            dma((len(tables),)),
            dma((2, 16)),
        ]
        + [dma((2, UNITS))] * 4,
        compiler_params=pltpu.CompilerParams(collective_id=0, has_side_effects=True, vmem_limit_bytes=VMEM_LIMIT),
    )(
        charges, fractions, inner_cell.reshape(1, -1), dest_slab.reshape(1, -1), filter_amp, *tables
    )


def solution(mesh):
    in_specs = (
        P(None, ("slab", "brick")),
        P(None, ("slab", "brick")),
        P(("slab", "brick")),
        P(("slab", "brick"), None),
        P(),
    )
    out_specs = P(None, ("slab", "brick"))
    return jax.shard_map(body, mesh=mesh, in_specs=in_specs, out_specs=out_specs, check_vma=False)
```

```python
import math

import numpy as np

import jax
import jax.numpy as jnp
import ml_dtypes
from jax import lax
from jax.experimental import pallas as pl
from jax.experimental.pallas import tpu as pltpu
from jax.sharding import PartitionSpec as P

G = 256
BIN = 16
SLABS = 32
BRICKS = 4
CAP = 64
BF = jnp.bfloat16
MESH = pl.DeviceIdType.MESH


def waves():
    places = np.arange(G)
    angles = 2.0 * np.pi * ((places[:, None] * places[None, :]) % G) / G
    return np.cos(angles), np.sin(angles)


def forward_table():
    cosine, sine = waves()
    return np.stack([np.stack([cosine, sine], 1), np.stack([-sine, cosine], 1)], 0)


def inverse_table():
    cosine, sine = waves()
    return np.stack([np.stack([cosine, -sine], 1), np.stack([sine, cosine], 1)], 0) / G


def spline_weights(fraction):
    remainder = 1.0 - fraction
    square = fraction * fraction
    cubed = square * fraction
    return (
        remainder * remainder * remainder / 6.0,
        (3.0 * cubed - 6.0 * square + 4.0) / 6.0,
        (-3.0 * cubed + 3.0 * square + 3.0 * fraction + 1.0) / 6.0,
        cubed / 6.0,
    )


GROUPS = 8
LANES = 256
PLACES = 132
WINDOW = 48
HALVES = 2
UNITS = 4
CHIP_ORDER = (
    (2, 2), (0, 1), (1, 0), (0, 3), (3, 0), (1, 2), (2, 1), (3, 2), (2, 3), (0, 2), (2, 0), (1, 1), (3, 3), (1, 3), (3, 1),
)
WIDE = 11
ORDER = (1, 2, 3, 4, 5, 6, 7, 8, 0, 9, 10)
SIDES = (9, 10, 0)
EDGES = (1, 2, 8)
ROWS = 24
BACK_ROWS = 32
VMEM_LIMIT = 56 * 1024 * 1024


def rounded_table(table):
    return np.ascontiguousarray(table).astype(ml_dtypes.bfloat16)


def rim_table():
    table = np.zeros((128, WIDE, 2, 64), np.float32)
    for at, x in enumerate(ORDER):
        for r in range(2):
            for start, y in ((0, 0), (32, 1), (64, 63)):
                table[start + at * 2 + r, x, r, y] = 1.0
    return table.reshape(128, WIDE * 128)


def make_tables():
    forward = forward_table()
    inverse = inverse_table()
    both = np.stack(waves())
    where = np.arange(G)
    where = (where // 16 * 16 + where % 8 * 2 + where // 8 % 2 - 1) % G
    order = np.arange(G).reshape(SLABS, HALVES, 4).transpose(1, 0, 2).reshape(G)
    tables = (
        rim_table(),
        both[:, order][:, :, where].reshape(2, HALVES, 128, G).transpose(1, 0, 2, 3).reshape(512, G),
        both.reshape(512, G),
        forward.reshape(2, G, 2, BRICKS, 64).transpose(3, 2, 4, 0, 1).reshape(512, 512),
        inverse.reshape(2, BRICKS, 64, 2, G).transpose(3, 4, 1, 0, 2).reshape(512, 512),
        both.reshape(512, G) / G,
        both[:, where][:, :, order].reshape(512, G) / G,
    )
    return [rounded_table(table) for table in tables]


def dot(a, b):
    return lax.dot_general(a, b, (((1,), (0,)), ((), ())), preferred_element_type=jnp.float32)


def dot_nt(a, b):
    return lax.dot_general(a, b, (((1,), (1,)), ((), ())), preferred_element_type=jnp.float32)


def iota(shape, dim):
    return lax.broadcasted_iota(jnp.int32, shape, dim)


def double(values):
    high = values.astype(BF).astype(jnp.float32)
    return high, values - high


def dense(cell, weights, places):
    total = 0.0
    for j in range(4):
        total = total + jnp.where(places == cell + j, weights[j], 0.0)
    return total


def slot_lanes(g):
    return pl.ds(pl.multiple_of(g * LANES, LANES), LANES)


def row_x(shape):
    at = iota(shape, 0) >> 1
    return jnp.where(at < 8, at + 1, jnp.where(at == 8, 0, jnp.where(at < WIDE, at, 99)))


def remote(src, dst, sems, at, target):
    copy = pltpu.make_async_remote_copy(
        src_ref=src,
        dst_ref=dst,
        send_sem=sems.at[0, at],
        recv_sem=sems.at[1, at],
        device_id=target,
        device_id_type=MESH,
    )
    copy.start()
    return copy


def kernel(
    charge_ref, frac_ref, cell_ref, target_ref, amp_ref,
    rim_far, zt_far, xt_far, yt_far, iyt_far, ixt_far, izt_far,
    out_ref,
    rim_ref, zt, xt, yt, iyt, ixt, izt,
    sorted_ref, spline_ref, line_ref, read_ref, rank_ref, pairs, rim_pairs, rim_sums, rim_near, rim_part, mesh, mesh_back, slices,
    rim_out, rim_in, rim_out2, rim_in2, side_out, side_in, freq, freq_back,
    block, from_slab, to_brick, from_brick, back_brick, got_brick, back_slab, got_slab, after, potential, gain,
    table_sems, near_sems, slab_sems, brick_sems, brick_sems2, slab_sems2,
):
    slab = lax.axis_index("slab")
    brick = lax.axis_index("brick")
    left = {"slab": lax.rem(slab + SLABS - 1, SLABS)}
    right = {"slab": lax.rem(slab + 1, SLABS)}
    down = {"brick": lax.rem(brick + BRICKS - 1, BRICKS)}
    up = {"brick": lax.rem(brick + 1, BRICKS)}

    barrier = pltpu.get_barrier_semaphore()

    for step in range(1, SLABS):
        pl.semaphore_signal(
            barrier, inc=1, device_id={"slab": lax.rem(slab + step, SLABS)}, device_id_type=MESH
        )
    for step in range(1, BRICKS):
        pl.semaphore_signal(
            barrier, inc=1, device_id={"brick": lax.rem(brick + step, BRICKS)}, device_id_type=MESH
        )

    loads = []
    for at, (far, near) in enumerate(
        ((rim_far, rim_ref), (zt_far, zt), (xt_far, xt), (yt_far, yt), (iyt_far, iyt), (ixt_far, ixt), (izt_far, izt))
    ):
        load = pltpu.make_async_copy(far, near, table_sems.at[at])
        load.start()
        loads.append(load)

    atoms = charge_ref.shape[1]
    blocks = atoms // 128
    target = target_ref[...]
    here = jnp.where(iota((SLABS, atoms), 0) == target, 1.0, 0.0)
    stacked = jnp.concatenate([here[:, b * 128 : b * 128 + 128] for b in range(blocks)], axis=0).astype(BF)
    earlier = jnp.where(iota((128, 128), 0) < iota((128, 128), 1), 1.0, 0.0)
    counts = dot(stacked, jnp.concatenate([earlier, jnp.ones((128, 128), jnp.float32)], axis=1).astype(BF))
    ahead = jnp.zeros((SLABS, 128), jnp.float32)
    ranks = []
    for b in range(blocks):
        rows = slice(b * SLABS, b * SLABS + SLABS)
        ranks.append(counts[rows, 0:128] + ahead)
        ahead = ahead + counts[rows, 128:]
    rank = jnp.sum(here * jnp.concatenate(ranks, axis=1), axis=0, keepdims=True).astype(jnp.int32)
    rank_ref[...] = jnp.where((iota((128, atoms), 0) & 63) == rank, 1.0, 0.0).astype(BF)
    payload = jnp.concatenate([charge_ref[...], frac_ref[...], cell_ref[...].astype(jnp.float32)], axis=0)
    parts = double(payload)
    low_half = iota((8, 128), 1) < 64

    def sort(g, carry):
        rows = []
        for part in parts:
            rows += [jnp.where(target == g * 8 + t, part, 0.0) for t in range(8)]
        moved = dot_nt(jnp.concatenate(rows, axis=0).astype(BF), rank_ref[...])
        moved = moved[0:64] + moved[64:128]
        tiles = [
            jnp.where(low_half, moved[16 * t : 16 * t + 8], moved[16 * t + 8 : 16 * t + 16]) for t in range(4)
        ]
        sorted_ref[:, pl.ds(pl.multiple_of(g * 512, 512), 512)] = jnp.concatenate(tiles, axis=1)
        return carry

    lax.fori_loop(0, SLABS // 8, sort, 0, unroll=4)

    for j, weight in enumerate(spline_weights(sorted_ref[4:7, :])):
        spline_ref[j, 0:3, :] = weight

    def along(dim, g):
        return [spline_ref[j, dim : dim + 1, slot_lanes(g)] for j in range(4)]

    slab_of = iota((ROWS, LANES), 1) >> 6
    first_part = (iota((ROWS, LANES), 0) & 1) == 0
    x_of = row_x((BACK_ROWS, LANES))

    def line(held, g, p):
        return jnp.where(first_part, held[p : p + 1, :], held[2 + p : 3 + p, :]) * line_ref[g, 0:ROWS, :]

    rim_sums[...] = jnp.zeros(rim_sums.shape, jnp.float32)
    window_row = iota((WINDOW, LANES), 0)
    window_place = (window_row >> 4) * 16 + (window_row & 7) * 2 + ((window_row >> 3) & 1)
    slab_start = (iota((1, LANES), 1) >> 6) * 8

    def make_rims(g, carry):
        held = sorted_ref[:, slot_lanes(g)]
        code = held[7:8, :].astype(jnp.int32)
        line_ref[g] = dense((code >> 3) & 7, along(2, g), x_of)
        wz = dense((code & 7) + slab_start, along(0, g), window_place)
        lines = [line(held, g, p) for p in range(2)]
        blocks, columns = [], []
        for h, y in enumerate((64, 65, -1)):
            rim = (wz * dense((code >> 6) - 1, along(1, g), y)).astype(BF)
            rim_pairs[g, pl.ds(h * WINDOW, WINDOW), :] = rim
            blocks.append(rim)
            rows = []
            for p in range(2):
                if h:
                    rows.append(jnp.zeros((32 * h, LANES), jnp.float32))
                rows += [lines[p], jnp.zeros((128 - ROWS - 32 * h, LANES), jnp.float32)]
            columns.append(jnp.concatenate(rows, axis=0).astype(BF))
        at = pl.ds(pl.multiple_of(g * 32, 16), WINDOW)
        rim_sums[at, :] = rim_sums[at, :] + dot_nt(
            jnp.concatenate(blocks, axis=1), jnp.concatenate(columns, axis=1)
        )
        return carry

    lax.fori_loop(0, GROUPS, make_rims, 0, unroll=8)
    rim_sums[0:16, :] = rim_sums[0:16, :] + rim_sums[G : G + 16, :]
    near = {}
    for p in range(2):
        rim_out[p] = rim_sums[0:G, p * 128 : p * 128 + 128].astype(BF)
    pl.semaphore_wait(barrier, SLABS - 1 + BRICKS - 1)
    for p in range(2):
        near["up", p] = remote(rim_out.at[p], rim_in.at[p, 0], near_sems, 8 * p, up)
        near["down", p] = remote(rim_out.at[p], rim_in.at[p, 1], near_sems, 8 * p + 1, down)

    mesh[:, 0:2] = jnp.zeros((2, 2, ROWS, 128), jnp.float32)

    def spread(p):
        def one(g, carry):
            held = sorted_ref[:, slot_lanes(g)]
            if p == 0:
                code = held[7:8, :].astype(jnp.int32)
                wz = dense(code & 7, along(0, g), iota((16, LANES), 0))
                wy = dense((code >> 6) - 1, along(1, g), iota((64, LANES), 0))
            own = line(held, g, p)
            lines = jnp.concatenate([jnp.where(slab_of == i, own, 0.0) for i in range(4)], axis=0).astype(BF)
            for z in (4, 8, 0):
                if p == 0:
                    pairs[g, z // 4] = jnp.concatenate(
                        [wy * wz[z + k : z + k + 1, :] for k in range(4)], axis=0
                    ).astype(BF)
                tile = dot_nt(lines, pairs[g, z // 4])
                for i in range(4):
                    for side in range(2):
                        at = g * 16 + i * 4 + z // 2 + side
                        part = tile[i * ROWS : i * ROWS + ROWS, side * 128 : side * 128 + 128]
                        mesh[p, at] = part if z else mesh[p, at] + part
            return carry

        lax.fori_loop(0, GROUPS, one, 0, unroll=8)
        mesh[p, 0] = mesh[p, 0] + mesh[p, 128]
        mesh[p, 1] = mesh[p, 1] + mesh[p, 129]

    low_all = iota((G, 128), 1) < 64
    sign = jnp.where(low_all, 1.0, -1.0)

    def turn(values):
        return sign[0 : values.shape[0]] * pltpu.roll(values, 64, 1)

    def pack_rims(p, which):
        return dot_nt(
            jnp.concatenate([potential[p, x] for x in which], axis=1),
            jnp.concatenate([rim_ref[:, x * 128 : x * 128 + 128] for x in which], axis=1),
        )

    def both_rims(arrived, p):
        return jnp.where(low_all, arrived[p, 0].astype(jnp.float32), arrived[p, 1].astype(jnp.float32))

    def cut(p):
        def one(step, carry):
            for part in range(3):
                turned = jnp.swapaxes(mesh[p, pl.ds(step * 8, 8), pl.ds(part * 8, 8), :], 0, 1)
                for at, x in enumerate(ORDER[4 * part : 4 * part + 4]):
                    a, b = turned[2 * at], turned[2 * at + 1]
                    slices[p, x, pl.ds(pl.multiple_of(step * 16, 16), 16), :] = jnp.concatenate(
                        [
                            jnp.where(low_half, a, pltpu.roll(b, 64, 1)),
                            jnp.where(low_half, pltpu.roll(a, 64, 1), b),
                        ],
                        axis=0,
                    )
            return carry

        lax.fori_loop(0, 16, one, 0, unroll=8)

    def send_sides(p):
        near["up", p].wait_recv()
        near["down", p].wait_recv()
        rims = both_rims(rim_in, p).astype(BF)
        added = dot(rims, jnp.concatenate([rim_ref[:, x * 128 : x * 128 + 128] for x in SIDES], axis=1))
        for at, x in enumerate(SIDES):
            side_out[p, at] = (slices[p, x] + added[:, at * 128 : at * 128 + 128]).astype(BF)
        near["right", p] = remote(
            side_out.at[p, pl.ds(0, 2)], side_in.at[p, pl.ds(0, 2)], near_sems, 8 * p + 2, right
        )
        near["left", p] = remote(side_out.at[p, pl.ds(2, 1)], side_in.at[p, pl.ds(2, 1)], near_sems, 8 * p + 3, left)
        added = dot(rims, rim_ref[:, 128 : 9 * 128])
        for x in range(1, 9):
            slices[p, x] = slices[p, x] + added[:, x * 128 - 128 : x * 128]

    def signed(k):
        return jnp.where(k < G // 2, k, k - G).astype(jnp.float32)

    def make_gain():
        fx = signed(brick * 64 + iota((64, G), 0))
        fy = signed(iota((64, G), 1))
        flat = fx * fx + fy * fy

        def one(index, carry):
            fz = signed(slab * 8 + index)
            magnitude = jnp.sqrt(fz * fz + flat)
            scaled = magnitude * (1.0 / BIN) - 8.0
            middle = jnp.exp(-0.5 * scaled * scaled)
            sums = [amp_ref[p, 8] * middle for p in range(2)]
            for way in (1, -1):
                ratio = jnp.exp(way * scaled - 0.5)
                bump = middle
                for center in range(8 + way, 16 if way > 0 else -1, way):
                    bump = bump * ratio
                    ratio = ratio * math.exp(-1.0)
                    sums = [sums[p] + amp_ref[p, center] * bump for p in range(2)]
            for p in range(2):
                gain[p, pl.ds(pl.multiple_of(index * 64, 64), 64), :] = sums[p]
            return carry

        lax.fori_loop(0, 8, one, 0, unroll=2)

    def send(src, dst, u, axis, me, count, sems):
        def one(step, carry):
            peer = lax.rem(me + step, count)
            pltpu.make_async_remote_copy(
                src_ref=src.at[u, peer],
                dst_ref=dst.at[u, me],
                send_sem=sems.at[0, u],
                recv_sem=sems.at[1, u],
                device_id={axis: peer},
                device_id_type=MESH,
            ).start()
            return carry

        lax.fori_loop(1, count, one, 0)

    def send_slabs(make, src, dst, u, sems):
        def to(peer):
            pltpu.make_async_remote_copy(
                src_ref=src.at[u, peer],
                dst_ref=dst.at[u, slab],
                send_sem=sems.at[0, u],
                recv_sem=sems.at[1, u],
                device_id={"slab": peer},
                device_id_type=MESH,
            ).start()

        for dy, dz in CHIP_ORDER:
            pair = lax.rem(slab // 8 + dy, 4) * 4 + lax.rem(slab // 2 + dz, 4)
            make(pair)
            to(2 * pair)
            to(2 * pair + 1)
        make(slab // 2)
        to(slab + 1 - 2 * lax.rem(slab, 2))
        dst[u, slab] = src[u, slab]

    def wait(buf, u, count, sems, which):
        part = buf.at[u, pl.ds(0, count - 1)]
        pltpu.make_async_copy(part, part, sems.at[which, u]).wait()

    def z_pair(p, x):
        out = dot(zt[...], jnp.concatenate([slices[p, x], slices[p, x + 1]], axis=1).astype(BF))
        for half in range(HALVES):
            for k in range(2):
                lanes = slice(k * 128, k * 128 + 128)
                u = out[half * 256 : half * 256 + 128, lanes]
                v = out[half * 256 + 128 : half * 256 + 256, lanes]
                freq[half, x - 1 + k] = u + turn(v)

    def inner_z(p):
        z_pair(p, 3)
        z_pair(p, 5)

    def outer_z(p):
        near["right", p].wait_recv()
        for at in range(2):
            slices[p, EDGES[at]] = slices[p, EDGES[at]] + side_in[p, at].astype(jnp.float32)
        z_pair(p, 1)
        near["left", p].wait_recv()
        slices[p, EDGES[2]] = slices[p, EDGES[2]] + side_in[p, 2].astype(jnp.float32)
        z_pair(p, 7)
        for half in range(HALVES):

            def pack(pair, half=half):
                turned = jnp.swapaxes(freq[half, :, pl.ds(pl.multiple_of(pair * 8, 8), 8), :], 0, 1)
                block[2 * p + half, pl.ds(2 * pair, 2)] = turned.reshape(2, 2, 16, 128).astype(BF)

            send_slabs(pack, block, from_slab, 2 * p + half, slab_sems)

    def x_stage(u):
        wait(from_slab, u, SLABS, slab_sems, 1)
        cols = []
        for two in range(2):
            held = from_slab[u, :, two].astype(jnp.float32)
            cols += [held[:, 0:8].reshape(G, 128), held[:, 8:16].reshape(G, 128)]
        out = dot(xt[...], jnp.concatenate(cols, axis=1).astype(BF))
        for k in range(4):
            lanes = slice(k * 128, k * 128 + 128)
            done = (out[0:G, lanes] + turn(out[G:, lanes])).astype(BF)
            to_brick[u, :, k] = done.reshape(BRICKS, 64, 128)
        send(to_brick, from_brick, u, "brick", brick, BRICKS, brick_sems)
        from_brick[u, brick] = to_brick[u, brick]

    def y_stage(u):
        wait(from_brick, u, BRICKS, brick_sems, 1)
        rows = jnp.concatenate([from_brick[u, b].reshape(G, 128) for b in range(BRICKS)], axis=1)
        spectrum = dot(rows, yt[...])
        weight = gain[u // 2, pl.ds(u % 2 * 256, 256), :]
        filtered = jnp.concatenate([spectrum[:, :G] * weight, spectrum[:, G:] * weight], axis=1)
        back = dot(filtered.astype(BF), iyt[...]).astype(BF)
        for b in range(BRICKS):
            back_brick[u, b] = back[:, b * 128 : b * 128 + 128].reshape(4, 64, 128)
        send(back_brick, got_brick, u, "brick", brick, BRICKS, brick_sems2)
        got_brick[u, brick] = back_brick[u, brick]

    def i_stage(u):
        wait(got_brick, u, BRICKS, brick_sems2, 1)
        after[...] = dot(ixt[...], jnp.concatenate([got_brick[u, :, k].reshape(G, 128) for k in range(4)], axis=1))

        def make(pair):
            at = pl.multiple_of(pair * 16, 16)
            done = []
            for k in range(4):
                lanes = pl.ds(k * 128, 128)
                values = after[pl.ds(at, 16), lanes] - turn(after[pl.ds(G + at, 16), lanes])
                done.append(values.reshape(2, 8, 128))
            for two in range(2):
                back_slab[u, pl.ds(2 * pair, 2), two] = jnp.concatenate(done[2 * two : 2 * two + 2], axis=1).astype(BF)

        send_slabs(make, back_slab, got_slab, u, slab_sems2)

    def home(p):
        for half in range(HALVES):
            wait(got_slab, 2 * p + half, SLABS, slab_sems2, 1)

            def unpack(s, carry, half=half):
                rows = []
                for eight in range(2):
                    held = got_slab[2 * p + half, pl.ds(4 * s + 2 * eight, 2)].astype(jnp.float32)
                    rows.append(jnp.swapaxes(held.reshape(8, 8, 128), 0, 1))
                at = pl.multiple_of(half * 128 + s * 16, 16)
                freq_back[:, pl.ds(at, 16), :] = jnp.concatenate(rows, axis=1).astype(BF)
                return carry

            lax.fori_loop(0, SLABS // 4, unpack, 0, unroll=8)

        def back_z(x):
            out = dot(izt[...], jnp.concatenate([freq_back[x - 1], freq_back[x]], axis=1))
            for k in range(2):
                lanes = slice(k * 128, k * 128 + 128)
                potential[p, x + k] = (out[0:G, lanes] - turn(out[G:, lanes])).astype(BF)

        back_z(1)
        near["left2", p] = remote(
            potential.at[p, pl.ds(1, 2)], potential.at[p, pl.ds(9, 2)], near_sems, 8 * p + 4, left
        )
        back_z(7)
        near["right2", p] = remote(
            potential.at[p, pl.ds(8, 1)], potential.at[p, pl.ds(0, 1)], near_sems, 8 * p + 5, right
        )
        back_z(3)
        back_z(5)
        rim_part[...] = pack_rims(p, range(1, 9))
        place(p, 0)

    def place(p, part):
        def one(step, carry):
            rows = pl.ds(pl.multiple_of(step * 16, 16), 16)
            blank = jnp.zeros((8, 128), jnp.float32)
            turned = []
            for four in range(2):
                if 8 * part + 4 * four >= WIDE:
                    turned.append(jnp.zeros((8, 8, 128), jnp.float32))
                    continue
                tiles = []
                for x in ORDER[8 * part + 4 * four : 8 * part + 4 * four + 4]:
                    held = potential[p, x, rows, :].astype(jnp.float32)
                    a, b = held[0:8], held[8:16]
                    tiles.append(jnp.where(low_half, a, pltpu.roll(b, 64, 1)))
                    tiles.append(jnp.where(low_half, pltpu.roll(a, 64, 1), b))
                tiles += [blank] * (8 - len(tiles))
                turned.append(jnp.swapaxes(jnp.stack(tiles, axis=0), 0, 1))
            mesh_back[p, pl.ds(step * 8, 8), pl.ds(part * 16, 16), :] = jnp.concatenate(turned, axis=1).astype(BF)
            return carry

        lax.fori_loop(0, 16, one, 0, unroll=8)

    def send_back_rims(p):
        near["left2", p].wait_recv()
        near["right2", p].wait_recv()
        rim_out2[p] = (rim_part[...] + pack_rims(p, (0, 9, 10))).astype(BF)
        near["down2", p] = remote(rim_out2.at[p], rim_in2.at[p, 0], near_sems, 8 * p + 6, down)
        near["up2", p] = remote(rim_out2.at[p], rim_in2.at[p, 1], near_sems, 8 * p + 7, up)
        place(p, 1)
        mesh_back[p, 128] = mesh_back[p, 0]
        mesh_back[p, 129] = mesh_back[p, 1]

    back_slab_of = iota((BACK_ROWS, LANES), 1) >> 6
    rim_of = iota((WINDOW, 128), 1) >> 5

    def reduce_x(own):
        return own[0:8] + own[8:16] + own[16:24] + own[24:32]

    def read_mesh(p):
        def one(g, carry):
            seen = jnp.zeros((4 * BACK_ROWS, LANES), jnp.float32)
            for z in range(0, 12, 4):
                rows = []
                for i in range(4):
                    at = g * 16 + i * 4 + z // 2
                    rows.append(jnp.concatenate([mesh_back[p, at + side] for side in range(2)], axis=1))
                seen = seen + dot(jnp.concatenate(rows, axis=0), pairs[g, z // 4])
            own = jnp.zeros((BACK_ROWS, LANES), jnp.float32)
            for i in range(4):
                own = own + jnp.where(back_slab_of == i, seen[i * BACK_ROWS : i * BACK_ROWS + BACK_ROWS], 0.0)
            read_ref[:, slot_lanes(g)] = reduce_x(own * line_ref[g])
            return carry

        lax.fori_loop(0, GROUPS, one, 0, unroll=8)

    def read_rims(p):
        near["down2", p].wait_recv()
        near["up2", p].wait_recv()
        rims = both_rims(rim_in2, p)
        rim_near[0:G, :] = rims
        rim_near[G : G + 16, :] = rims[0:16]

        def one(g, carry):
            window = rim_near[pl.ds(pl.multiple_of(g * 32, 16), WINDOW), :]
            window = jnp.concatenate([jnp.where(rim_of == h, window, 0.0) for h in range(3)], axis=0).astype(BF)
            rim = lax.dot_general(
                window, rim_pairs[g], (((0,), (0,)), ((), ())), preferred_element_type=jnp.float32
            )
            own = rim[0:32] + rim[32:64] + rim[64:96]
            readings = reduce_x(own * line_ref[g]) + read_ref[:, slot_lanes(g)]
            readings = readings + pltpu.roll(readings, 4, 0)
            read_ref[:, slot_lanes(g)] = readings + pltpu.roll(readings, 2, 0)
            return carry

        lax.fori_loop(0, GROUPS, one, 0, unroll=8)

        def unsort(g, total):
            rows = []
            for part in double(read_ref[:, pl.ds(pl.multiple_of(g * 512, 512), 512)]):
                for t in range(4):
                    tile = part[:, t * 128 : t * 128 + 128]
                    rows += [jnp.where(low_half, tile, 0.0), jnp.where(low_half, 0.0, tile)]
            moved = dot(jnp.concatenate(rows, axis=0).astype(BF), rank_ref[...])
            moved = moved[0:64] + moved[64:128]
            for t in range(8):
                total = total + jnp.where(target == g * 8 + t, moved[t * 8 : t * 8 + 8], 0.0)
            return total

        total = lax.fori_loop(0, SLABS // 8, unsort, jnp.zeros((8, atoms), jnp.float32), unroll=4)
        out_ref[p : p + 1, :] = total[0:1]
        out_ref[2 + p : 3 + p, :] = total[1:2]

    spread(0)
    cut(0)
    loads[0].wait()
    send_sides(0)
    for load in loads[1:]:
        load.wait()
    inner_z(0)
    make_gain()
    outer_z(0)
    spread(1)
    cut(1)
    send_sides(1)
    x_stage(0)
    x_stage(1)
    inner_z(1)
    outer_z(1)
    y_stage(0)
    y_stage(1)
    x_stage(2)
    x_stage(3)
    i_stage(0)
    i_stage(1)
    y_stage(2)
    y_stage(3)
    i_stage(2)
    i_stage(3)
    home(0)
    send_back_rims(0)
    home(1)
    read_mesh(0)
    send_back_rims(1)
    read_rims(0)
    read_mesh(1)
    read_rims(1)
    for copy in near.values():
        copy.wait_send()
    for u in range(UNITS):
        wait(block, u, SLABS, slab_sems, 0)
        wait(back_slab, u, SLABS, slab_sems2, 0)
        wait(to_brick, u, BRICKS, brick_sems, 0)
        wait(back_brick, u, BRICKS, brick_sems2, 0)


def body(charges, fractions, inner_cell, dest_slab, filter_amp):
    vmem = pl.BlockSpec(memory_space=pltpu.VMEM)
    anywhere = pl.BlockSpec(memory_space=pl.ANY)
    dma = pltpu.SemaphoreType.DMA
    atoms = charges.shape[1]
    tables = [jnp.asarray(table) for table in make_tables()]
    to_slab = (UNITS, SLABS, 2, 16, 128)
    to_brick = (UNITS, BRICKS, 4, 64, 128)
    return pl.pallas_call(
        kernel,
        out_shape=jax.ShapeDtypeStruct((4, atoms), jnp.float32),
        in_specs=[vmem] * 4 + [pl.BlockSpec(memory_space=pltpu.SMEM)] + [anywhere] * len(tables),
        out_specs=vmem,
        scratch_shapes=[pltpu.VMEM(table.shape, BF) for table in tables]
        + [
            pltpu.VMEM((8, SLABS * CAP), jnp.float32),
            pltpu.VMEM((4, 8, SLABS * CAP), jnp.float32),
            pltpu.VMEM((GROUPS, BACK_ROWS, LANES), jnp.float32),
            pltpu.VMEM((8, SLABS * CAP), jnp.float32),
            pltpu.VMEM((128, atoms), BF),
            pltpu.VMEM((GROUPS, 3, 256, LANES), BF),
            pltpu.VMEM((GROUPS, 3 * WINDOW, LANES), BF),
            pltpu.VMEM((G + 16, 256), jnp.float32),
            pltpu.VMEM((G + 16, 128), jnp.float32),
            pltpu.VMEM((G, 128), jnp.float32),
            pltpu.VMEM((2, PLACES, ROWS, 128), jnp.float32),
            pltpu.VMEM((2, PLACES, BACK_ROWS, 128), BF),
            pltpu.VMEM((2, WIDE, G, 128), jnp.float32),
            pltpu.VMEM((2, G, 128), BF),
            pltpu.VMEM((2, 2, G, 128), BF),
            pltpu.VMEM((2, G, 128), BF),
            pltpu.VMEM((2, 2, G, 128), BF),
            pltpu.VMEM((2, 3, G, 128), BF),
            pltpu.VMEM((2, 3, G, 128), BF),
            pltpu.VMEM((HALVES, 8, 128, 128), jnp.float32),
            pltpu.VMEM((8, G, 128), BF),
        ]
        + [pltpu.VMEM(to_slab, BF)] * 2
        + [pltpu.VMEM(to_brick, BF)] * 4
        + [pltpu.VMEM(to_slab, BF)] * 2
        + [
            pltpu.VMEM((512, 512), jnp.float32),
            pltpu.VMEM((2, WIDE, G, 128), BF),
            pltpu.VMEM((2, 512, G), jnp.float32),
            dma((len(tables),)),
            dma((2, 16)),
        ]
        + [dma((2, UNITS))] * 4,
        compiler_params=pltpu.CompilerParams(collective_id=0, has_side_effects=True, vmem_limit_bytes=VMEM_LIMIT),
    )(
        charges, fractions, inner_cell.reshape(1, -1), dest_slab.reshape(1, -1), filter_amp, *tables
    )


def solution(mesh):
    in_specs = (
        P(None, ("slab", "brick")),
        P(None, ("slab", "brick")),
        P(("slab", "brick")),
        P(("slab", "brick"), None),
        P(),
    )
    out_specs = P(None, ("slab", "brick"))
    return jax.shard_map(body, mesh=mesh, in_specs=in_specs, out_specs=out_specs, check_vma=False)
```

```python
import math

import numpy as np

import jax
import jax.numpy as jnp
import ml_dtypes
from jax import lax
from jax.experimental import pallas as pl
from jax.experimental.pallas import tpu as pltpu
from jax.sharding import PartitionSpec as P

G = 256
BIN = 16
SLABS = 32
BRICKS = 4
CAP = 64
BF = jnp.bfloat16
MESH = pl.DeviceIdType.MESH


def waves():
    places = np.arange(G)
    angles = 2.0 * np.pi * ((places[:, None] * places[None, :]) % G) / G
    return np.cos(angles), np.sin(angles)


def forward_table():
    cosine, sine = waves()
    return np.stack([np.stack([cosine, sine], 1), np.stack([-sine, cosine], 1)], 0)


def inverse_table():
    cosine, sine = waves()
    return np.stack([np.stack([cosine, -sine], 1), np.stack([sine, cosine], 1)], 0) / G


def spline_weights(fraction):
    remainder = 1.0 - fraction
    square = fraction * fraction
    cubed = square * fraction
    return (
        remainder * remainder * remainder / 6.0,
        (3.0 * cubed - 6.0 * square + 4.0) / 6.0,
        (-3.0 * cubed + 3.0 * square + 3.0 * fraction + 1.0) / 6.0,
        cubed / 6.0,
    )


GROUPS = 8
LANES = 256
PLACES = 132
WINDOW = 48
HALVES = 2
UNITS = 6
PAIR_OF = (0, 0, 0, 1, 1, 1)
TILES = ((0, 1), (1, 2), (2, 4), (0, 2), (2, 3), (3, 4))
UNITS_OF = ((0, 1, 2), (3, 4, 5))
CHIP_ORDER = (
    (2, 2), (0, 1), (1, 0), (0, 3), (3, 0), (1, 2), (2, 1), (3, 2), (2, 3), (0, 2), (2, 0), (1, 1), (3, 3), (1, 3), (3, 1),
)
WIDE = 11
ORDER = (1, 2, 3, 4, 5, 6, 7, 8, 0, 9, 10)
SIDES = (9, 10, 0)
EDGES = (1, 2, 8)
ROWS = 24
BACK_ROWS = 32
VMEM_LIMIT = 56 * 1024 * 1024


def rounded_table(table):
    return np.ascontiguousarray(table).astype(ml_dtypes.bfloat16)


def rim_table():
    table = np.zeros((128, WIDE, 2, 64), np.float32)
    for at, x in enumerate(ORDER):
        for r in range(2):
            for start, y in ((0, 0), (32, 1), (64, 63)):
                table[start + at * 2 + r, x, r, y] = 1.0
    return table.reshape(128, WIDE * 128)


def make_tables():
    forward = forward_table()
    inverse = inverse_table()
    both = np.stack(waves())
    where = np.arange(G)
    where = (where // 16 * 16 + where % 8 * 2 + where // 8 % 2 - 1) % G
    order = np.arange(G).reshape(SLABS, HALVES, 4).transpose(1, 0, 2).reshape(G)
    tables = (
        rim_table(),
        both[:, order][:, :, where].reshape(2, HALVES, 128, G).transpose(1, 0, 2, 3).reshape(512, G),
        both.reshape(512, G),
        forward.reshape(2, G, 2, BRICKS, 64).transpose(3, 2, 4, 0, 1).reshape(512, 512),
        inverse.reshape(2, BRICKS, 64, 2, G).transpose(3, 4, 1, 0, 2).reshape(512, 512),
        both.reshape(512, G) / G,
        both[:, where][:, :, order].reshape(512, G) / G,
    )
    return [rounded_table(table) for table in tables]


def dot(a, b):
    return lax.dot_general(a, b, (((1,), (0,)), ((), ())), preferred_element_type=jnp.float32)


def dot_nt(a, b):
    return lax.dot_general(a, b, (((1,), (1,)), ((), ())), preferred_element_type=jnp.float32)


def iota(shape, dim):
    return lax.broadcasted_iota(jnp.int32, shape, dim)


def double(values):
    high = values.astype(BF).astype(jnp.float32)
    return high, values - high


def dense(cell, weights, places):
    total = 0.0
    for j in range(4):
        total = total + jnp.where(places == cell + j, weights[j], 0.0)
    return total


def slot_lanes(g):
    return pl.ds(pl.multiple_of(g * LANES, LANES), LANES)


def row_x(shape):
    at = iota(shape, 0) >> 1
    return jnp.where(at < 8, at + 1, jnp.where(at == 8, 0, jnp.where(at < WIDE, at, 99)))


def remote(src, dst, sems, at, target):
    copy = pltpu.make_async_remote_copy(
        src_ref=src,
        dst_ref=dst,
        send_sem=sems.at[0, at],
        recv_sem=sems.at[1, at],
        device_id=target,
        device_id_type=MESH,
    )
    copy.start()
    return copy


def kernel(
    charge_ref, frac_ref, cell_ref, target_ref, amp_ref,
    rim_far, zt_far, xt_far, yt_far, iyt_far, ixt_far, izt_far,
    out_ref,
    rim_ref, zt, xt, yt, iyt, ixt, izt,
    sorted_ref, spline_ref, line_ref, read_ref, rank_ref, pairs, rim_pairs, rim_sums, rim_near, rim_part, mesh, mesh_back, slices,
    rim_out, rim_in, rim_out2, rim_in2, side_out, side_in, freq, freq_back,
    block, from_slab, to_brick, from_brick, back_brick, got_brick, back_slab, got_slab, after, potential, gain,
    table_sems, near_sems, slab_sems, brick_sems, brick_sems2, slab_sems2,
):
    slab = lax.axis_index("slab")
    brick = lax.axis_index("brick")
    left = {"slab": lax.rem(slab + SLABS - 1, SLABS)}
    right = {"slab": lax.rem(slab + 1, SLABS)}
    down = {"brick": lax.rem(brick + BRICKS - 1, BRICKS)}
    up = {"brick": lax.rem(brick + 1, BRICKS)}

    barrier = pltpu.get_barrier_semaphore()

    for step in range(1, SLABS):
        pl.semaphore_signal(
            barrier, inc=1, device_id={"slab": lax.rem(slab + step, SLABS)}, device_id_type=MESH
        )
    for step in range(1, BRICKS):
        pl.semaphore_signal(
            barrier, inc=1, device_id={"brick": lax.rem(brick + step, BRICKS)}, device_id_type=MESH
        )

    loads = []
    for at, (far, near) in enumerate(
        ((rim_far, rim_ref), (zt_far, zt), (xt_far, xt), (yt_far, yt), (iyt_far, iyt), (ixt_far, ixt), (izt_far, izt))
    ):
        load = pltpu.make_async_copy(far, near, table_sems.at[at])
        load.start()
        loads.append(load)

    atoms = charge_ref.shape[1]
    blocks = atoms // 128
    target = target_ref[...]
    here = jnp.where(iota((SLABS, atoms), 0) == target, 1.0, 0.0)
    stacked = jnp.concatenate([here[:, b * 128 : b * 128 + 128] for b in range(blocks)], axis=0).astype(BF)
    earlier = jnp.where(iota((128, 128), 0) < iota((128, 128), 1), 1.0, 0.0)
    counts = dot(stacked, jnp.concatenate([earlier, jnp.ones((128, 128), jnp.float32)], axis=1).astype(BF))
    ahead = jnp.zeros((SLABS, 128), jnp.float32)
    ranks = []
    for b in range(blocks):
        rows = slice(b * SLABS, b * SLABS + SLABS)
        ranks.append(counts[rows, 0:128] + ahead)
        ahead = ahead + counts[rows, 128:]
    rank = jnp.sum(here * jnp.concatenate(ranks, axis=1), axis=0, keepdims=True).astype(jnp.int32)
    rank_ref[...] = jnp.where((iota((128, atoms), 0) & 63) == rank, 1.0, 0.0).astype(BF)
    payload = jnp.concatenate([charge_ref[...], frac_ref[...], cell_ref[...].astype(jnp.float32)], axis=0)
    parts = double(payload)
    low_half = iota((8, 128), 1) < 64

    def sort(g, carry):
        rows = []
        for part in parts:
            rows += [jnp.where(target == g * 8 + t, part, 0.0) for t in range(8)]
        moved = dot_nt(jnp.concatenate(rows, axis=0).astype(BF), rank_ref[...])
        moved = moved[0:64] + moved[64:128]
        tiles = [
            jnp.where(low_half, moved[16 * t : 16 * t + 8], moved[16 * t + 8 : 16 * t + 16]) for t in range(4)
        ]
        sorted_ref[:, pl.ds(pl.multiple_of(g * 512, 512), 512)] = jnp.concatenate(tiles, axis=1)
        return carry

    lax.fori_loop(0, SLABS // 8, sort, 0, unroll=4)

    for j, weight in enumerate(spline_weights(sorted_ref[4:7, :])):
        spline_ref[j, 0:3, :] = weight

    def along(dim, g):
        return [spline_ref[j, dim : dim + 1, slot_lanes(g)] for j in range(4)]

    slab_of = iota((ROWS, LANES), 1) >> 6
    first_part = (iota((ROWS, LANES), 0) & 1) == 0
    x_of = row_x((BACK_ROWS, LANES))

    def line(held, g, p):
        return jnp.where(first_part, held[p : p + 1, :], held[2 + p : 3 + p, :]) * line_ref[g, 0:ROWS, :]

    rim_sums[...] = jnp.zeros(rim_sums.shape, jnp.float32)
    window_row = iota((WINDOW, LANES), 0)
    window_place = (window_row >> 4) * 16 + (window_row & 7) * 2 + ((window_row >> 3) & 1)
    slab_start = (iota((1, LANES), 1) >> 6) * 8

    def make_rims(g, carry):
        held = sorted_ref[:, slot_lanes(g)]
        code = held[7:8, :].astype(jnp.int32)
        line_ref[g] = dense((code >> 3) & 7, along(2, g), x_of)
        wz = dense((code & 7) + slab_start, along(0, g), window_place)
        lines = [line(held, g, p) for p in range(2)]
        blocks, columns = [], []
        for h, y in enumerate((64, 65, -1)):
            rim = (wz * dense((code >> 6) - 1, along(1, g), y)).astype(BF)
            rim_pairs[g, pl.ds(h * WINDOW, WINDOW), :] = rim
            blocks.append(rim)
            rows = []
            for p in range(2):
                if h:
                    rows.append(jnp.zeros((32 * h, LANES), jnp.float32))
                rows += [lines[p], jnp.zeros((128 - ROWS - 32 * h, LANES), jnp.float32)]
            columns.append(jnp.concatenate(rows, axis=0).astype(BF))
        at = pl.ds(pl.multiple_of(g * 32, 16), WINDOW)
        rim_sums[at, :] = rim_sums[at, :] + dot_nt(
            jnp.concatenate(blocks, axis=1), jnp.concatenate(columns, axis=1)
        )
        return carry

    lax.fori_loop(0, GROUPS, make_rims, 0, unroll=8)
    rim_sums[0:16, :] = rim_sums[0:16, :] + rim_sums[G : G + 16, :]
    near = {}
    for p in range(2):
        rim_out[p] = rim_sums[0:G, p * 128 : p * 128 + 128].astype(BF)
    pl.semaphore_wait(barrier, SLABS - 1 + BRICKS - 1)
    for p in range(2):
        near["up", p] = remote(rim_out.at[p], rim_in.at[p, 0], near_sems, 8 * p, up)
        near["down", p] = remote(rim_out.at[p], rim_in.at[p, 1], near_sems, 8 * p + 1, down)

    mesh[:, 0:2] = jnp.zeros((2, 2, ROWS, 128), jnp.float32)

    def spread(p):
        def one(g, carry):
            held = sorted_ref[:, slot_lanes(g)]
            if p == 0:
                code = held[7:8, :].astype(jnp.int32)
                wz = dense(code & 7, along(0, g), iota((16, LANES), 0))
                wy = dense((code >> 6) - 1, along(1, g), iota((64, LANES), 0))
            own = line(held, g, p)
            lines = jnp.concatenate([jnp.where(slab_of == i, own, 0.0) for i in range(4)], axis=0).astype(BF)
            for z in (4, 8, 0):
                if p == 0:
                    pairs[g, z // 4] = jnp.concatenate(
                        [wy * wz[z + k : z + k + 1, :] for k in range(4)], axis=0
                    ).astype(BF)
                tile = dot_nt(lines, pairs[g, z // 4])
                for i in range(4):
                    for side in range(2):
                        at = g * 16 + i * 4 + z // 2 + side
                        part = tile[i * ROWS : i * ROWS + ROWS, side * 128 : side * 128 + 128]
                        mesh[p, at] = part if z else mesh[p, at] + part
            return carry

        lax.fori_loop(0, GROUPS, one, 0, unroll=8)
        mesh[p, 0] = mesh[p, 0] + mesh[p, 128]
        mesh[p, 1] = mesh[p, 1] + mesh[p, 129]

    low_all = iota((G, 128), 1) < 64
    sign = jnp.where(low_all, 1.0, -1.0)

    def turn(values):
        return sign[0 : values.shape[0]] * pltpu.roll(values, 64, 1)

    def pack_rims(p, which):
        return dot_nt(
            jnp.concatenate([potential[p, x] for x in which], axis=1),
            jnp.concatenate([rim_ref[:, x * 128 : x * 128 + 128] for x in which], axis=1),
        )

    def both_rims(arrived, p):
        return jnp.where(low_all, arrived[p, 0].astype(jnp.float32), arrived[p, 1].astype(jnp.float32))

    def cut(p):
        def one(step, carry):
            for part in range(3):
                turned = jnp.swapaxes(mesh[p, pl.ds(step * 8, 8), pl.ds(part * 8, 8), :], 0, 1)
                for at, x in enumerate(ORDER[4 * part : 4 * part + 4]):
                    a, b = turned[2 * at], turned[2 * at + 1]
                    slices[p, x, pl.ds(pl.multiple_of(step * 16, 16), 16), :] = jnp.concatenate(
                        [
                            jnp.where(low_half, a, pltpu.roll(b, 64, 1)),
                            jnp.where(low_half, pltpu.roll(a, 64, 1), b),
                        ],
                        axis=0,
                    )
            return carry

        lax.fori_loop(0, 16, one, 0, unroll=8)

    def send_sides(p):
        near["up", p].wait_recv()
        near["down", p].wait_recv()
        rims = both_rims(rim_in, p).astype(BF)
        added = dot(rims, jnp.concatenate([rim_ref[:, x * 128 : x * 128 + 128] for x in SIDES], axis=1))
        for at, x in enumerate(SIDES):
            side_out[p, at] = (slices[p, x] + added[:, at * 128 : at * 128 + 128]).astype(BF)
        near["right", p] = remote(
            side_out.at[p, pl.ds(0, 2)], side_in.at[p, pl.ds(0, 2)], near_sems, 8 * p + 2, right
        )
        near["left", p] = remote(side_out.at[p, pl.ds(2, 1)], side_in.at[p, pl.ds(2, 1)], near_sems, 8 * p + 3, left)
        added = dot(rims, rim_ref[:, 128 : 9 * 128])
        for x in range(1, 9):
            slices[p, x] = slices[p, x] + added[:, x * 128 - 128 : x * 128]

    def signed(k):
        return jnp.where(k < G // 2, k, k - G).astype(jnp.float32)

    def make_gain():
        fx = signed(brick * 64 + iota((64, G), 0))
        fy = signed(iota((64, G), 1))
        flat = fx * fx + fy * fy

        def one(index, carry):
            fz = signed(slab * 8 + index)
            magnitude = jnp.sqrt(fz * fz + flat)
            scaled = magnitude * (1.0 / BIN) - 8.0
            middle = jnp.exp(-0.5 * scaled * scaled)
            sums = [amp_ref[p, 8] * middle for p in range(2)]
            for way in (1, -1):
                ratio = jnp.exp(way * scaled - 0.5)
                bump = middle
                for center in range(8 + way, 16 if way > 0 else -1, way):
                    bump = bump * ratio
                    ratio = ratio * math.exp(-1.0)
                    sums = [sums[p] + amp_ref[p, center] * bump for p in range(2)]
            for p in range(2):
                gain[p, pl.ds(pl.multiple_of(index * 64, 64), 64), :] = sums[p]
            return carry

        lax.fori_loop(0, 8, one, 0, unroll=2)

    def tiles_of(u):
        return pl.ds(TILES[u][0], TILES[u][1] - TILES[u][0])

    def freqs_of(u):
        return pl.ds(2 * TILES[u][0], 2 * (TILES[u][1] - TILES[u][0]))

    def send_bricks(src, dst, u, sems):
        p = PAIR_OF[u]
        for step in range(1, BRICKS):
            peer = lax.rem(brick + step, BRICKS)
            pltpu.make_async_remote_copy(
                src_ref=src.at[p, peer, freqs_of(u)],
                dst_ref=dst.at[p, brick, freqs_of(u)],
                send_sem=sems.at[0, u],
                recv_sem=sems.at[1, u],
                device_id={"brick": peer},
                device_id_type=MESH,
            ).start()
        dst[p, brick, freqs_of(u)] = src[p, brick, freqs_of(u)]

    def wait_bricks(buf, u, sem):
        part = buf.at[PAIR_OF[u], pl.ds(0, BRICKS - 1), freqs_of(u)]
        pltpu.make_async_copy(part, part, sem).wait()

    def wait_slabs(buf, u, sem):
        part = buf.at[PAIR_OF[u], pl.ds(0, SLABS - 1), tiles_of(u)]
        pltpu.make_async_copy(part, part, sem).wait()

    def send_slabs(make, src, dst, u, sems):
        def to(peer):
            pltpu.make_async_remote_copy(
                src_ref=src.at[PAIR_OF[u], peer, tiles_of(u)],
                dst_ref=dst.at[PAIR_OF[u], slab, tiles_of(u)],
                send_sem=sems.at[0, u],
                recv_sem=sems.at[1, u],
                device_id={"slab": peer},
                device_id_type=MESH,
            ).start()

        for dy, dz in CHIP_ORDER:
            pair = lax.rem(slab // 8 + dy, 4) * 4 + lax.rem(slab // 2 + dz, 4)
            make(pair)
            to(2 * pair)
            to(2 * pair + 1)
        make(slab // 2)
        to(slab + 1 - 2 * lax.rem(slab, 2))
        dst[PAIR_OF[u], slab, tiles_of(u)] = src[PAIR_OF[u], slab, tiles_of(u)]

    def z_pair(p, x):
        out = dot(zt[...], jnp.concatenate([slices[p, x], slices[p, x + 1]], axis=1).astype(BF))
        for half in range(HALVES):
            for k in range(2):
                lanes = slice(k * 128, k * 128 + 128)
                u = out[half * 256 : half * 256 + 128, lanes]
                v = out[half * 256 + 128 : half * 256 + 256, lanes]
                freq[half, x - 1 + k] = u + turn(v)

    def inner_z(p):
        z_pair(p, 3)
        z_pair(p, 5)

    def outer_z(p):
        near["right", p].wait_recv()
        for at in range(2):
            slices[p, EDGES[at]] = slices[p, EDGES[at]] + side_in[p, at].astype(jnp.float32)
        z_pair(p, 1)
        near["left", p].wait_recv()
        slices[p, EDGES[2]] = slices[p, EDGES[2]] + side_in[p, 2].astype(jnp.float32)
        z_pair(p, 7)

        def pack(halves):
            def one(pair):
                for half in halves:
                    turned = jnp.swapaxes(freq[half, :, pl.ds(pl.multiple_of(pair * 8, 8), 8), :], 0, 1)
                    block[p, pl.ds(2 * pair, 2), pl.ds(2 * half, 2)] = turned.reshape(2, 2, 16, 128).astype(BF)

            return one

        made = 0
        for u in UNITS_OF[p]:
            needed = (TILES[u][1] + 1) // 2
            send_slabs(pack(range(made, needed)), block, from_slab, u, slab_sems)
            made = needed

    def x_stage(u):
        wait_slabs(from_slab, u, slab_sems.at[1, u])
        p = PAIR_OF[u]
        cols = []
        for tile in range(*TILES[u]):
            held = from_slab[p, :, tile].astype(jnp.float32)
            cols += [held[:, 0:8].reshape(G, 128), held[:, 8:16].reshape(G, 128)]
        out = dot(xt[...], jnp.concatenate(cols, axis=1).astype(BF))
        for k in range(len(cols)):
            lanes = slice(k * 128, k * 128 + 128)
            done = (out[0:G, lanes] + turn(out[G:, lanes])).astype(BF)
            to_brick[p, :, 2 * TILES[u][0] + k] = done.reshape(BRICKS, 64, 128)
        send_bricks(to_brick, from_brick, u, brick_sems)

    def y_stage(u):
        wait_bricks(from_brick, u, brick_sems.at[1, u])
        p = PAIR_OF[u]
        first, count = 2 * TILES[u][0], 2 * (TILES[u][1] - TILES[u][0])
        rows = jnp.concatenate(
            [from_brick[p, b, freqs_of(u)].reshape(count * 64, 128) for b in range(BRICKS)], axis=1
        )
        spectrum = dot(rows, yt[...])
        weight = gain[p, pl.ds(first * 64, count * 64), :]
        filtered = jnp.concatenate([spectrum[:, :G] * weight, spectrum[:, G:] * weight], axis=1)
        back = dot(filtered.astype(BF), iyt[...]).astype(BF)
        for b in range(BRICKS):
            back_brick[p, b, freqs_of(u)] = back[:, b * 128 : b * 128 + 128].reshape(count, 64, 128)
        send_bricks(back_brick, got_brick, u, brick_sems2)

    def i_stage(u):
        wait_bricks(got_brick, u, brick_sems2.at[1, u])
        p = PAIR_OF[u]
        first, last = 2 * TILES[u][0], 2 * TILES[u][1]
        after[:, 0 : (last - first) * 128] = dot(
            ixt[...], jnp.concatenate([got_brick[p, :, k].reshape(G, 128) for k in range(first, last)], axis=1)
        )

        def make(pair):
            at = pl.multiple_of(pair * 16, 16)
            done = []
            for k in range(last - first):
                lanes = pl.ds(k * 128, 128)
                values = after[pl.ds(at, 16), lanes] - turn(after[pl.ds(G + at, 16), lanes])
                done.append(values.reshape(2, 8, 128))
            for tile in range(*TILES[u]):
                two = 2 * tile - first
                back_slab[p, pl.ds(2 * pair, 2), tile] = jnp.concatenate(done[two : two + 2], axis=1).astype(BF)

        send_slabs(make, back_slab, got_slab, u, slab_sems2)

    def home(p):
        there = 0
        for half in range(HALVES):
            for u in UNITS_OF[p]:
                if there < 2 * half + 2 and there == TILES[u][0]:
                    wait_slabs(got_slab, u, slab_sems2.at[1, u])
                    there = TILES[u][1]

            def unpack(s, carry, half=half):
                rows = []
                for eight in range(2):
                    held = got_slab[p, pl.ds(4 * s + 2 * eight, 2), pl.ds(2 * half, 2)].astype(jnp.float32)
                    rows.append(jnp.swapaxes(held.reshape(8, 8, 128), 0, 1))
                at = pl.multiple_of(half * 128 + s * 16, 16)
                freq_back[:, pl.ds(at, 16), :] = jnp.concatenate(rows, axis=1).astype(BF)
                return carry

            lax.fori_loop(0, SLABS // 4, unpack, 0, unroll=8)

        def back_z(x):
            out = dot(izt[...], jnp.concatenate([freq_back[x - 1], freq_back[x]], axis=1))
            for k in range(2):
                lanes = slice(k * 128, k * 128 + 128)
                potential[p, x + k] = (out[0:G, lanes] - turn(out[G:, lanes])).astype(BF)

        back_z(1)
        near["left2", p] = remote(
            potential.at[p, pl.ds(1, 2)], potential.at[p, pl.ds(9, 2)], near_sems, 8 * p + 4, left
        )
        back_z(7)
        near["right2", p] = remote(
            potential.at[p, pl.ds(8, 1)], potential.at[p, pl.ds(0, 1)], near_sems, 8 * p + 5, right
        )
        back_z(3)
        back_z(5)
        rim_part[...] = pack_rims(p, range(1, 9))
        place(p, 0)

    def place(p, part):
        def one(step, carry):
            rows = pl.ds(pl.multiple_of(step * 16, 16), 16)
            blank = jnp.zeros((8, 128), jnp.float32)
            turned = []
            for four in range(2):
                if 8 * part + 4 * four >= WIDE:
                    turned.append(jnp.zeros((8, 8, 128), jnp.float32))
                    continue
                tiles = []
                for x in ORDER[8 * part + 4 * four : 8 * part + 4 * four + 4]:
                    held = potential[p, x, rows, :].astype(jnp.float32)
                    a, b = held[0:8], held[8:16]
                    tiles.append(jnp.where(low_half, a, pltpu.roll(b, 64, 1)))
                    tiles.append(jnp.where(low_half, pltpu.roll(a, 64, 1), b))
                tiles += [blank] * (8 - len(tiles))
                turned.append(jnp.swapaxes(jnp.stack(tiles, axis=0), 0, 1))
            mesh_back[p, pl.ds(step * 8, 8), pl.ds(part * 16, 16), :] = jnp.concatenate(turned, axis=1).astype(BF)
            return carry

        lax.fori_loop(0, 16, one, 0, unroll=8)

    def send_back_rims(p):
        near["left2", p].wait_recv()
        near["right2", p].wait_recv()
        rim_out2[p] = (rim_part[...] + pack_rims(p, (0, 9, 10))).astype(BF)
        near["down2", p] = remote(rim_out2.at[p], rim_in2.at[p, 0], near_sems, 8 * p + 6, down)
        near["up2", p] = remote(rim_out2.at[p], rim_in2.at[p, 1], near_sems, 8 * p + 7, up)
        place(p, 1)
        mesh_back[p, 128] = mesh_back[p, 0]
        mesh_back[p, 129] = mesh_back[p, 1]

    back_slab_of = iota((BACK_ROWS, LANES), 1) >> 6
    rim_of = iota((WINDOW, 128), 1) >> 5

    def reduce_x(own):
        return own[0:8] + own[8:16] + own[16:24] + own[24:32]

    def read_mesh(p):
        def one(g, carry):
            seen = jnp.zeros((4 * BACK_ROWS, LANES), jnp.float32)
            for z in range(0, 12, 4):
                rows = []
                for i in range(4):
                    at = g * 16 + i * 4 + z // 2
                    rows.append(jnp.concatenate([mesh_back[p, at + side] for side in range(2)], axis=1))
                seen = seen + dot(jnp.concatenate(rows, axis=0), pairs[g, z // 4])
            own = jnp.zeros((BACK_ROWS, LANES), jnp.float32)
            for i in range(4):
                own = own + jnp.where(back_slab_of == i, seen[i * BACK_ROWS : i * BACK_ROWS + BACK_ROWS], 0.0)
            read_ref[:, slot_lanes(g)] = reduce_x(own * line_ref[g])
            return carry

        lax.fori_loop(0, GROUPS, one, 0, unroll=8)

    def read_rims(p):
        near["down2", p].wait_recv()
        near["up2", p].wait_recv()
        rims = both_rims(rim_in2, p)
        rim_near[0:G, :] = rims
        rim_near[G : G + 16, :] = rims[0:16]

        def one(g, carry):
            window = rim_near[pl.ds(pl.multiple_of(g * 32, 16), WINDOW), :]
            window = jnp.concatenate([jnp.where(rim_of == h, window, 0.0) for h in range(3)], axis=0).astype(BF)
            rim = lax.dot_general(
                window, rim_pairs[g], (((0,), (0,)), ((), ())), preferred_element_type=jnp.float32
            )
            own = rim[0:32] + rim[32:64] + rim[64:96]
            readings = reduce_x(own * line_ref[g]) + read_ref[:, slot_lanes(g)]
            readings = readings + pltpu.roll(readings, 4, 0)
            read_ref[:, slot_lanes(g)] = readings + pltpu.roll(readings, 2, 0)
            return carry

        lax.fori_loop(0, GROUPS, one, 0, unroll=8)

        def unsort(g, total):
            rows = []
            for part in double(read_ref[:, pl.ds(pl.multiple_of(g * 512, 512), 512)]):
                for t in range(4):
                    tile = part[:, t * 128 : t * 128 + 128]
                    rows += [jnp.where(low_half, tile, 0.0), jnp.where(low_half, 0.0, tile)]
            moved = dot(jnp.concatenate(rows, axis=0).astype(BF), rank_ref[...])
            moved = moved[0:64] + moved[64:128]
            for t in range(8):
                total = total + jnp.where(target == g * 8 + t, moved[t * 8 : t * 8 + 8], 0.0)
            return total

        total = lax.fori_loop(0, SLABS // 8, unsort, jnp.zeros((8, atoms), jnp.float32), unroll=4)
        out_ref[p : p + 1, :] = total[0:1]
        out_ref[2 + p : 3 + p, :] = total[1:2]

    spread(0)
    cut(0)
    loads[0].wait()
    send_sides(0)
    for load in loads[1:]:
        load.wait()
    inner_z(0)
    make_gain()
    outer_z(0)
    spread(1)
    cut(1)
    send_sides(1)
    for u in UNITS_OF[0]:
        x_stage(u)
    inner_z(1)
    outer_z(1)
    for u in UNITS_OF[0]:
        y_stage(u)
    for u in UNITS_OF[1]:
        x_stage(u)
    for u in UNITS_OF[0]:
        i_stage(u)
    for u in UNITS_OF[1]:
        y_stage(u)
    for u in UNITS_OF[1]:
        i_stage(u)
    home(0)
    send_back_rims(0)
    home(1)
    read_mesh(0)
    send_back_rims(1)
    read_rims(0)
    read_mesh(1)
    read_rims(1)
    for copy in near.values():
        copy.wait_send()
    for u in range(UNITS):
        wait_slabs(block, u, slab_sems.at[0, u])
        wait_bricks(to_brick, u, brick_sems.at[0, u])
        wait_bricks(back_brick, u, brick_sems2.at[0, u])
        wait_slabs(back_slab, u, slab_sems2.at[0, u])


def body(charges, fractions, inner_cell, dest_slab, filter_amp):
    vmem = pl.BlockSpec(memory_space=pltpu.VMEM)
    anywhere = pl.BlockSpec(memory_space=pl.ANY)
    dma = pltpu.SemaphoreType.DMA
    atoms = charges.shape[1]
    tables = [jnp.asarray(table) for table in make_tables()]
    to_slab = (2, SLABS, 4, 16, 128)
    to_brick = (2, BRICKS, 8, 64, 128)
    return pl.pallas_call(
        kernel,
        out_shape=jax.ShapeDtypeStruct((4, atoms), jnp.float32),
        in_specs=[vmem] * 4 + [pl.BlockSpec(memory_space=pltpu.SMEM)] + [anywhere] * len(tables),
        out_specs=vmem,
        scratch_shapes=[pltpu.VMEM(table.shape, BF) for table in tables]
        + [
            pltpu.VMEM((8, SLABS * CAP), jnp.float32),
            pltpu.VMEM((4, 8, SLABS * CAP), jnp.float32),
            pltpu.VMEM((GROUPS, BACK_ROWS, LANES), jnp.float32),
            pltpu.VMEM((8, SLABS * CAP), jnp.float32),
            pltpu.VMEM((128, atoms), BF),
            pltpu.VMEM((GROUPS, 3, 256, LANES), BF),
            pltpu.VMEM((GROUPS, 3 * WINDOW, LANES), BF),
            pltpu.VMEM((G + 16, 256), jnp.float32),
            pltpu.VMEM((G + 16, 128), jnp.float32),
            pltpu.VMEM((G, 128), jnp.float32),
            pltpu.VMEM((2, PLACES, ROWS, 128), jnp.float32),
            pltpu.VMEM((2, PLACES, BACK_ROWS, 128), BF),
            pltpu.VMEM((2, WIDE, G, 128), jnp.float32),
            pltpu.VMEM((2, G, 128), BF),
            pltpu.VMEM((2, 2, G, 128), BF),
            pltpu.VMEM((2, G, 128), BF),
            pltpu.VMEM((2, 2, G, 128), BF),
            pltpu.VMEM((2, 3, G, 128), BF),
            pltpu.VMEM((2, 3, G, 128), BF),
            pltpu.VMEM((HALVES, 8, 128, 128), jnp.float32),
            pltpu.VMEM((8, G, 128), BF),
        ]
        + [pltpu.VMEM(to_slab, BF)] * 2
        + [pltpu.VMEM(to_brick, BF)] * 4
        + [pltpu.VMEM(to_slab, BF)] * 2
        + [
            pltpu.VMEM((512, 4 * 128), jnp.float32),
            pltpu.VMEM((2, WIDE, G, 128), BF),
            pltpu.VMEM((2, 512, G), jnp.float32),
            dma((len(tables),)),
            dma((2, 16)),
        ]
        + [dma((2, UNITS))] * 4,
        compiler_params=pltpu.CompilerParams(collective_id=0, has_side_effects=True, vmem_limit_bytes=VMEM_LIMIT),
    )(
        charges, fractions, inner_cell.reshape(1, -1), dest_slab.reshape(1, -1), filter_amp, *tables
    )


def solution(mesh):
    in_specs = (
        P(None, ("slab", "brick")),
        P(None, ("slab", "brick")),
        P(("slab", "brick")),
        P(("slab", "brick"), None),
        P(),
    )
    out_specs = P(None, ("slab", "brick"))
    return jax.shard_map(body, mesh=mesh, in_specs=in_specs, out_specs=out_specs, check_vma=False)
```

```python
import math

import numpy as np

import jax
import jax.numpy as jnp
import ml_dtypes
from jax import lax
from jax.experimental import pallas as pl
from jax.experimental.pallas import tpu as pltpu
from jax.sharding import PartitionSpec as P

G = 256
BIN = 16
SLABS = 32
BRICKS = 4
CAP = 64
BF = jnp.bfloat16
MESH = pl.DeviceIdType.MESH


def waves():
    places = np.arange(G)
    angles = 2.0 * np.pi * ((places[:, None] * places[None, :]) % G) / G
    return np.cos(angles), np.sin(angles)


def forward_table():
    cosine, sine = waves()
    return np.stack([np.stack([cosine, sine], 1), np.stack([-sine, cosine], 1)], 0)


def inverse_table():
    cosine, sine = waves()
    return np.stack([np.stack([cosine, -sine], 1), np.stack([sine, cosine], 1)], 0) / G


def spline_weights(fraction):
    remainder = 1.0 - fraction
    square = fraction * fraction
    cubed = square * fraction
    return (
        remainder * remainder * remainder / 6.0,
        (3.0 * cubed - 6.0 * square + 4.0) / 6.0,
        (-3.0 * cubed + 3.0 * square + 3.0 * fraction + 1.0) / 6.0,
        cubed / 6.0,
    )


GROUPS = 8
LANES = 256
PLACES = 132
WINDOW = 48
HALVES = 2
UNITS = 6
PAIR_OF = (0, 0, 0, 1, 1, 1)
TILES = ((0, 1), (1, 2), (2, 4), (0, 2), (2, 3), (3, 4))
UNITS_OF = ((0, 1, 2), (3, 4, 5))
CHIP_ORDER = (
    (2, 2), (0, 1), (1, 0), (0, 3), (3, 0), (1, 2), (2, 1), (3, 2), (2, 3), (0, 2), (2, 0), (1, 1), (3, 3), (1, 3), (3, 1),
)
WIDE = 11
ORDER = (1, 2, 3, 4, 5, 6, 7, 8, 0, 9, 10)
SIDES = (9, 10, 0)
EDGES = (1, 2, 8)
ROWS = 24
BACK_ROWS = 32
VMEM_LIMIT = 56 * 1024 * 1024


def rounded_table(table):
    return np.ascontiguousarray(table).astype(ml_dtypes.bfloat16)


def rim_table():
    table = np.zeros((128, WIDE, 2, 64), np.float32)
    for at, x in enumerate(ORDER):
        for r in range(2):
            for start, y in ((0, 0), (32, 1), (64, 63)):
                table[start + at * 2 + r, x, r, y] = 1.0
    return table.reshape(128, WIDE * 128)


def make_tables():
    forward = forward_table()
    inverse = inverse_table()
    both = np.stack(waves())
    where = np.arange(G)
    where = (where // 16 * 16 + where % 8 * 2 + where // 8 % 2 - 1) % G
    order = np.arange(G).reshape(SLABS, HALVES, 4).transpose(1, 0, 2).reshape(G)
    tables = (
        rim_table(),
        both[:, order][:, :, where].reshape(2, HALVES, 128, G).transpose(1, 0, 2, 3).reshape(512, G),
        both.reshape(512, G),
        forward.reshape(2, G, 2, BRICKS, 64).transpose(3, 2, 4, 0, 1).reshape(512, 512),
        inverse.reshape(2, BRICKS, 64, 2, G).transpose(3, 4, 1, 0, 2).reshape(512, 512),
        both.reshape(512, G) / G,
        both[:, where][:, :, order].reshape(512, G) / G,
    )
    return [rounded_table(table) for table in tables]


def dot(a, b):
    return lax.dot_general(a, b, (((1,), (0,)), ((), ())), preferred_element_type=jnp.float32)


def dot_nt(a, b):
    return lax.dot_general(a, b, (((1,), (1,)), ((), ())), preferred_element_type=jnp.float32)


def iota(shape, dim):
    return lax.broadcasted_iota(jnp.int32, shape, dim)


def double(values):
    high = values.astype(BF).astype(jnp.float32)
    return high, values - high


def dense(cell, weights, places):
    total = 0.0
    for j in range(4):
        total = total + jnp.where(places == cell + j, weights[j], 0.0)
    return total


def slot_lanes(g):
    return pl.ds(pl.multiple_of(g * LANES, LANES), LANES)


def row_x(shape):
    at = iota(shape, 0) >> 1
    return jnp.where(at < 8, at + 1, jnp.where(at == 8, 0, jnp.where(at < WIDE, at, 99)))


def remote(src, dst, sems, at, target):
    copy = pltpu.make_async_remote_copy(
        src_ref=src,
        dst_ref=dst,
        send_sem=sems.at[0, at],
        recv_sem=sems.at[1, at],
        device_id=target,
        device_id_type=MESH,
    )
    copy.start()
    return copy


def kernel(
    charge_ref, frac_ref, cell_ref, target_ref, amp_ref,
    rim_far, zt_far, xt_far, yt_far, iyt_far, ixt_far, izt_far,
    out_ref,
    rim_ref, zt, xt, yt, iyt, ixt, izt,
    sorted_ref, spline_ref, line_ref, read_ref, rank_ref, pairs, rim_pairs, rim_sums, rim_near, rim_part, mesh, mesh_back, slices,
    rim_out, rim_in, rim_out2, rim_in2, side_out, side_in, freq, freq_back,
    block, from_slab, to_brick, from_brick, back_brick, got_brick, back_slab, got_slab, after, potential, gain,
    table_sems, near_sems, slab_sems, brick_sems, brick_sems2, slab_sems2,
):
    slab = lax.axis_index("slab")
    brick = lax.axis_index("brick")
    left = {"slab": lax.rem(slab + SLABS - 1, SLABS)}
    right = {"slab": lax.rem(slab + 1, SLABS)}
    down = {"brick": lax.rem(brick + BRICKS - 1, BRICKS)}
    up = {"brick": lax.rem(brick + 1, BRICKS)}

    barrier = pltpu.get_barrier_semaphore()

    for step in range(1, SLABS):
        pl.semaphore_signal(
            barrier, inc=1, device_id={"slab": lax.rem(slab + step, SLABS)}, device_id_type=MESH
        )
    for step in range(1, BRICKS):
        pl.semaphore_signal(
            barrier, inc=1, device_id={"brick": lax.rem(brick + step, BRICKS)}, device_id_type=MESH
        )

    loads = []
    for at, (far, near) in enumerate(
        ((rim_far, rim_ref), (zt_far, zt), (xt_far, xt), (yt_far, yt), (iyt_far, iyt), (ixt_far, ixt), (izt_far, izt))
    ):
        load = pltpu.make_async_copy(far, near, table_sems.at[at])
        load.start()
        loads.append(load)

    atoms = charge_ref.shape[1]
    blocks = atoms // 128
    target = target_ref[...]
    here = jnp.where(iota((SLABS, atoms), 0) == target, 1.0, 0.0)
    stacked = jnp.concatenate([here[:, b * 128 : b * 128 + 128] for b in range(blocks)], axis=0).astype(BF)
    earlier = jnp.where(iota((128, 128), 0) < iota((128, 128), 1), 1.0, 0.0)
    counts = dot(stacked, jnp.concatenate([earlier, jnp.ones((128, 128), jnp.float32)], axis=1).astype(BF))
    ahead = jnp.zeros((SLABS, 128), jnp.float32)
    ranks = []
    for b in range(blocks):
        rows = slice(b * SLABS, b * SLABS + SLABS)
        ranks.append(counts[rows, 0:128] + ahead)
        ahead = ahead + counts[rows, 128:]
    rank = jnp.sum(here * jnp.concatenate(ranks, axis=1), axis=0, keepdims=True).astype(jnp.int32)
    rank_ref[...] = jnp.where((iota((128, atoms), 0) & 63) == rank, 1.0, 0.0).astype(BF)
    payload = jnp.concatenate([charge_ref[...], frac_ref[...], cell_ref[...].astype(jnp.float32)], axis=0)
    parts = double(payload)
    low_half = iota((8, 128), 1) < 64

    def sort(g, carry):
        rows = []
        for part in parts:
            rows += [jnp.where(target == g * 8 + t, part, 0.0) for t in range(8)]
        moved = dot_nt(jnp.concatenate(rows, axis=0).astype(BF), rank_ref[...])
        moved = moved[0:64] + moved[64:128]
        tiles = [
            jnp.where(low_half, moved[16 * t : 16 * t + 8], moved[16 * t + 8 : 16 * t + 16]) for t in range(4)
        ]
        sorted_ref[:, pl.ds(pl.multiple_of(g * 512, 512), 512)] = jnp.concatenate(tiles, axis=1)
        return carry

    lax.fori_loop(0, SLABS // 8, sort, 0, unroll=4)

    for j, weight in enumerate(spline_weights(sorted_ref[4:7, :])):
        spline_ref[j, 0:3, :] = weight

    def along(dim, g):
        return [spline_ref[j, dim : dim + 1, slot_lanes(g)] for j in range(4)]

    slab_of = iota((ROWS, LANES), 1) >> 6
    first_part = (iota((ROWS, LANES), 0) & 1) == 0
    x_of = row_x((BACK_ROWS, LANES))

    def line(held, g, p):
        return jnp.where(first_part, held[p : p + 1, :], held[2 + p : 3 + p, :]) * line_ref[g, 0:ROWS, :]

    rim_sums[...] = jnp.zeros(rim_sums.shape, jnp.float32)
    window_row = iota((WINDOW, LANES), 0)
    window_place = (window_row >> 4) * 16 + (window_row & 7) * 2 + ((window_row >> 3) & 1)
    slab_start = (iota((1, LANES), 1) >> 6) * 8

    def make_rims(g, carry):
        held = sorted_ref[:, slot_lanes(g)]
        code = held[7:8, :].astype(jnp.int32)
        line_ref[g] = dense((code >> 3) & 7, along(2, g), x_of)
        wz = dense((code & 7) + slab_start, along(0, g), window_place)
        lines = [line(held, g, p) for p in range(2)]
        blocks, columns = [], []
        for h, y in enumerate((64, 65, -1)):
            rim = (wz * dense((code >> 6) - 1, along(1, g), y)).astype(BF)
            rim_pairs[g, pl.ds(h * WINDOW, WINDOW), :] = rim
            blocks.append(rim)
            rows = []
            for p in range(2):
                if h:
                    rows.append(jnp.zeros((32 * h, LANES), jnp.float32))
                rows += [lines[p], jnp.zeros((128 - ROWS - 32 * h, LANES), jnp.float32)]
            columns.append(jnp.concatenate(rows, axis=0).astype(BF))
        at = pl.ds(pl.multiple_of(g * 32, 16), WINDOW)
        rim_sums[at, :] = rim_sums[at, :] + dot_nt(
            jnp.concatenate(blocks, axis=1), jnp.concatenate(columns, axis=1)
        )
        return carry

    lax.fori_loop(0, GROUPS, make_rims, 0, unroll=8)
    rim_sums[0:16, :] = rim_sums[0:16, :] + rim_sums[G : G + 16, :]
    near = {}
    for p in range(2):
        rim_out[p] = rim_sums[0:G, p * 128 : p * 128 + 128].astype(BF)
    pl.semaphore_wait(barrier, SLABS - 1 + BRICKS - 1)
    for p in range(2):
        near["up", p] = remote(rim_out.at[p], rim_in.at[p, 0], near_sems, 8 * p, up)
        near["down", p] = remote(rim_out.at[p], rim_in.at[p, 1], near_sems, 8 * p + 1, down)

    mesh[:, 0:2] = jnp.zeros((2, 2, ROWS, 128), jnp.float32)

    def spread(p):
        def one(g, carry):
            held = sorted_ref[:, slot_lanes(g)]
            if p == 0:
                code = held[7:8, :].astype(jnp.int32)
                wz = dense(code & 7, along(0, g), iota((16, LANES), 0))
                wy = dense((code >> 6) - 1, along(1, g), iota((64, LANES), 0))
            own = line(held, g, p)
            lines = jnp.concatenate([jnp.where(slab_of == i, own, 0.0) for i in range(4)], axis=0).astype(BF)
            for z in (4, 8, 0):
                if p == 0:
                    pairs[g, z // 4] = jnp.concatenate(
                        [wy * wz[z + k : z + k + 1, :] for k in range(4)], axis=0
                    ).astype(BF)
                tile = dot_nt(lines, pairs[g, z // 4])
                for i in range(4):
                    for side in range(2):
                        at = g * 16 + i * 4 + z // 2 + side
                        part = tile[i * ROWS : i * ROWS + ROWS, side * 128 : side * 128 + 128]
                        mesh[p, at] = part if z else mesh[p, at] + part
            return carry

        lax.fori_loop(0, GROUPS, one, 0, unroll=8)
        mesh[p, 0] = mesh[p, 0] + mesh[p, 128]
        mesh[p, 1] = mesh[p, 1] + mesh[p, 129]

    low_all = iota((G, 128), 1) < 64
    sign = jnp.where(low_all, 1.0, -1.0)

    def turn(values):
        return sign[0 : values.shape[0]] * pltpu.roll(values, 64, 1)

    def pack_rims(p, which):
        return dot_nt(
            jnp.concatenate([potential[p, x] for x in which], axis=1),
            jnp.concatenate([rim_ref[:, x * 128 : x * 128 + 128] for x in which], axis=1),
        )

    def both_rims(arrived, p):
        return jnp.where(low_all, arrived[p, 0].astype(jnp.float32), arrived[p, 1].astype(jnp.float32))

    def cut(p):
        def one(step, carry):
            for part in range(3):
                turned = jnp.swapaxes(mesh[p, pl.ds(step * 8, 8), pl.ds(part * 8, 8), :], 0, 1)
                for at, x in enumerate(ORDER[4 * part : 4 * part + 4]):
                    a, b = turned[2 * at], turned[2 * at + 1]
                    slices[p, x, pl.ds(pl.multiple_of(step * 16, 16), 16), :] = jnp.concatenate(
                        [
                            jnp.where(low_half, a, pltpu.roll(b, 64, 1)),
                            jnp.where(low_half, pltpu.roll(a, 64, 1), b),
                        ],
                        axis=0,
                    )
            return carry

        lax.fori_loop(0, 16, one, 0, unroll=8)

    def send_sides(p):
        near["up", p].wait_recv()
        near["down", p].wait_recv()
        rims = both_rims(rim_in, p).astype(BF)
        added = dot(rims, jnp.concatenate([rim_ref[:, x * 128 : x * 128 + 128] for x in SIDES], axis=1))
        for at, x in enumerate(SIDES):
            side_out[p, at] = (slices[p, x] + added[:, at * 128 : at * 128 + 128]).astype(BF)
        near["right", p] = remote(
            side_out.at[p, pl.ds(0, 2)], side_in.at[p, pl.ds(0, 2)], near_sems, 8 * p + 2, right
        )
        near["left", p] = remote(side_out.at[p, pl.ds(2, 1)], side_in.at[p, pl.ds(2, 1)], near_sems, 8 * p + 3, left)
        added = dot(rims, rim_ref[:, 128 : 9 * 128])
        for x in range(1, 9):
            slices[p, x] = slices[p, x] + added[:, x * 128 - 128 : x * 128]

    def signed(k):
        return jnp.where(k < G // 2, k, k - G).astype(jnp.float32)

    def make_gain():
        fx = signed(brick * 64 + iota((64, G), 0))
        fy = signed(iota((64, G), 1))
        flat = fx * fx + fy * fy

        def one(index, carry):
            fz = signed(slab * 8 + index)
            magnitude = jnp.sqrt(fz * fz + flat)
            scaled = magnitude * (1.0 / BIN) - 8.0
            middle = jnp.exp(-0.5 * scaled * scaled)
            sums = [amp_ref[p, 8] * middle for p in range(2)]
            for way in (1, -1):
                ratio = jnp.exp(way * scaled - 0.5)
                bump = middle
                for center in range(8 + way, 16 if way > 0 else -1, way):
                    bump = bump * ratio
                    ratio = ratio * math.exp(-1.0)
                    sums = [sums[p] + amp_ref[p, center] * bump for p in range(2)]
            for p in range(2):
                gain[p, pl.ds(pl.multiple_of(index * 64, 64), 64), :] = sums[p]
            return carry

        lax.fori_loop(0, 8, one, 0, unroll=2)

    def tiles_of(u):
        return pl.ds(TILES[u][0], TILES[u][1] - TILES[u][0])

    def freqs_of(u):
        return pl.ds(2 * TILES[u][0], 2 * (TILES[u][1] - TILES[u][0]))

    def send_bricks(src, dst, u, sems):
        p = PAIR_OF[u]
        for step in range(1, BRICKS):
            peer = lax.rem(brick + step, BRICKS)
            pltpu.make_async_remote_copy(
                src_ref=src.at[p, peer, freqs_of(u)],
                dst_ref=dst.at[p, brick, freqs_of(u)],
                send_sem=sems.at[0, u],
                recv_sem=sems.at[1, u],
                device_id={"brick": peer},
                device_id_type=MESH,
            ).start()
        dst[p, brick, freqs_of(u)] = src[p, brick, freqs_of(u)]

    def wait_bricks(buf, u, sem):
        part = buf.at[PAIR_OF[u], pl.ds(0, BRICKS - 1), freqs_of(u)]
        pltpu.make_async_copy(part, part, sem).wait()

    def wait_slabs(buf, u, sem):
        part = buf.at[PAIR_OF[u], pl.ds(0, SLABS - 1), tiles_of(u)]
        pltpu.make_async_copy(part, part, sem).wait()

    def send_slabs(make, src, dst, u, sems):
        def to(peer):
            pltpu.make_async_remote_copy(
                src_ref=src.at[PAIR_OF[u], peer, tiles_of(u)],
                dst_ref=dst.at[PAIR_OF[u], slab, tiles_of(u)],
                send_sem=sems.at[0, u],
                recv_sem=sems.at[1, u],
                device_id={"slab": peer},
                device_id_type=MESH,
            ).start()

        for dy, dz in CHIP_ORDER:
            pair = lax.rem(slab // 8 + dy, 4) * 4 + lax.rem(slab // 2 + dz, 4)
            make(pair)
            to(2 * pair)
            to(2 * pair + 1)
        make(slab // 2)
        to(slab + 1 - 2 * lax.rem(slab, 2))
        dst[PAIR_OF[u], slab, tiles_of(u)] = src[PAIR_OF[u], slab, tiles_of(u)]

    def z_pair(p, x):
        out = dot(zt[...], jnp.concatenate([slices[p, x], slices[p, x + 1]], axis=1).astype(BF))
        for half in range(HALVES):
            for k in range(2):
                lanes = slice(k * 128, k * 128 + 128)
                u = out[half * 256 : half * 256 + 128, lanes]
                v = out[half * 256 + 128 : half * 256 + 256, lanes]
                freq[half, x - 1 + k] = u + turn(v)

    def inner_z(p):
        z_pair(p, 3)
        z_pair(p, 5)

    def outer_z(p):
        near["right", p].wait_recv()
        for at in range(2):
            slices[p, EDGES[at]] = slices[p, EDGES[at]] + side_in[p, at].astype(jnp.float32)
        z_pair(p, 1)
        near["left", p].wait_recv()
        slices[p, EDGES[2]] = slices[p, EDGES[2]] + side_in[p, 2].astype(jnp.float32)
        z_pair(p, 7)

        def pack(halves):
            def one(pair):
                for half in halves:
                    turned = jnp.swapaxes(freq[half, :, pl.ds(pl.multiple_of(pair * 8, 8), 8), :], 0, 1)
                    block[p, pl.ds(2 * pair, 2), pl.ds(2 * half, 2)] = turned.reshape(2, 2, 16, 128).astype(BF)

            return one

        made = 0
        for u in UNITS_OF[p]:
            needed = (TILES[u][1] + 1) // 2
            send_slabs(pack(range(made, needed)), block, from_slab, u, slab_sems)
            made = needed

    def x_stage(u):
        wait_slabs(from_slab, u, slab_sems.at[1, u])
        p = PAIR_OF[u]
        cols = []
        for tile in range(*TILES[u]):
            held = from_slab[p, :, tile].astype(jnp.float32)
            cols += [held[:, 0:8].reshape(G, 128), held[:, 8:16].reshape(G, 128)]
        out = dot(xt[...], jnp.concatenate(cols, axis=1).astype(BF))
        for k in range(len(cols)):
            lanes = slice(k * 128, k * 128 + 128)
            done = (out[0:G, lanes] + turn(out[G:, lanes])).astype(BF)
            to_brick[p, :, 2 * TILES[u][0] + k] = done.reshape(BRICKS, 64, 128)
        send_bricks(to_brick, from_brick, u, brick_sems)

    def y_stage(u):
        wait_bricks(from_brick, u, brick_sems.at[1, u])
        p = PAIR_OF[u]
        first, count = 2 * TILES[u][0], 2 * (TILES[u][1] - TILES[u][0])
        rows = jnp.concatenate(
            [from_brick[p, b, freqs_of(u)].reshape(count * 64, 128) for b in range(BRICKS)], axis=1
        )
        spectrum = dot(rows, yt[...])
        weight = gain[p, pl.ds(first * 64, count * 64), :]
        filtered = jnp.concatenate([spectrum[:, :G] * weight, spectrum[:, G:] * weight], axis=1)
        back = dot(filtered.astype(BF), iyt[...]).astype(BF)
        for b in range(BRICKS):
            back_brick[p, b, freqs_of(u)] = back[:, b * 128 : b * 128 + 128].reshape(count, 64, 128)
        send_bricks(back_brick, got_brick, u, brick_sems2)

    def i_stage(u):
        wait_bricks(got_brick, u, brick_sems2.at[1, u])
        p = PAIR_OF[u]
        first, last = 2 * TILES[u][0], 2 * TILES[u][1]
        after[:, 0 : (last - first) * 128] = dot(
            ixt[...], jnp.concatenate([got_brick[p, :, k].reshape(G, 128) for k in range(first, last)], axis=1)
        )

        def make(pair):
            at = pl.multiple_of(pair * 16, 16)
            done = []
            for k in range(last - first):
                lanes = pl.ds(k * 128, 128)
                values = after[pl.ds(at, 16), lanes] - turn(after[pl.ds(G + at, 16), lanes])
                done.append(values.reshape(2, 8, 128))
            for tile in range(*TILES[u]):
                two = 2 * tile - first
                back_slab[p, pl.ds(2 * pair, 2), tile] = jnp.concatenate(done[two : two + 2], axis=1).astype(BF)

        send_slabs(make, back_slab, got_slab, u, slab_sems2)

    def home(p):
        there = 0
        for half in range(HALVES):
            for u in UNITS_OF[p]:
                if there < 2 * half + 2 and there == TILES[u][0]:
                    wait_slabs(got_slab, u, slab_sems2.at[1, u])
                    there = TILES[u][1]

            def unpack(s, carry, half=half):
                rows = []
                for eight in range(2):
                    held = got_slab[p, pl.ds(4 * s + 2 * eight, 2), pl.ds(2 * half, 2)].astype(jnp.float32)
                    rows.append(jnp.swapaxes(held.reshape(8, 8, 128), 0, 1))
                at = pl.multiple_of(half * 128 + s * 16, 16)
                freq_back[:, pl.ds(at, 16), :] = jnp.concatenate(rows, axis=1).astype(BF)
                return carry

            lax.fori_loop(0, SLABS // 4, unpack, 0, unroll=8)

        def back_z(x):
            out = dot(izt[...], jnp.concatenate([freq_back[x - 1], freq_back[x]], axis=1))
            for k in range(2):
                lanes = slice(k * 128, k * 128 + 128)
                potential[p, x + k] = (out[0:G, lanes] - turn(out[G:, lanes])).astype(BF)

        back_z(1)
        near["left2", p] = remote(
            potential.at[p, pl.ds(1, 2)], potential.at[p, pl.ds(9, 2)], near_sems, 8 * p + 4, left
        )
        back_z(7)
        near["right2", p] = remote(
            potential.at[p, pl.ds(8, 1)], potential.at[p, pl.ds(0, 1)], near_sems, 8 * p + 5, right
        )
        back_z(3)
        back_z(5)
        rim_part[...] = pack_rims(p, range(1, 9))
        place(p, 0)

    def place(p, part):
        def one(step, carry):
            rows = pl.ds(pl.multiple_of(step * 16, 16), 16)
            blank = jnp.zeros((8, 128), jnp.float32)
            turned = []
            for four in range(2):
                if 8 * part + 4 * four >= WIDE:
                    turned.append(jnp.zeros((8, 8, 128), jnp.float32))
                    continue
                tiles = []
                for x in ORDER[8 * part + 4 * four : 8 * part + 4 * four + 4]:
                    held = potential[p, x, rows, :].astype(jnp.float32)
                    a, b = held[0:8], held[8:16]
                    tiles.append(jnp.where(low_half, a, pltpu.roll(b, 64, 1)))
                    tiles.append(jnp.where(low_half, pltpu.roll(a, 64, 1), b))
                tiles += [blank] * (8 - len(tiles))
                turned.append(jnp.swapaxes(jnp.stack(tiles, axis=0), 0, 1))
            mesh_back[p, pl.ds(step * 8, 8), pl.ds(part * 16, 16), :] = jnp.concatenate(turned, axis=1).astype(BF)
            return carry

        lax.fori_loop(0, 16, one, 0, unroll=8)

    def send_back_rims(p):
        near["left2", p].wait_recv()
        near["right2", p].wait_recv()
        rim_out2[p] = (rim_part[...] + pack_rims(p, (0, 9, 10))).astype(BF)
        near["down2", p] = remote(rim_out2.at[p], rim_in2.at[p, 0], near_sems, 8 * p + 6, down)
        near["up2", p] = remote(rim_out2.at[p], rim_in2.at[p, 1], near_sems, 8 * p + 7, up)
        place(p, 1)
        mesh_back[p, 128] = mesh_back[p, 0]
        mesh_back[p, 129] = mesh_back[p, 1]

    back_slab_of = iota((BACK_ROWS, LANES), 1) >> 6
    rim_of = iota((WINDOW, 128), 1) >> 5

    def reduce_x(own):
        return own[0:8] + own[8:16] + own[16:24] + own[24:32]

    def read_mesh(p):
        def one(g, carry):
            seen = jnp.zeros((4 * BACK_ROWS, LANES), jnp.float32)
            for z in range(0, 12, 4):
                rows = []
                for i in range(4):
                    at = g * 16 + i * 4 + z // 2
                    rows.append(jnp.concatenate([mesh_back[p, at + side] for side in range(2)], axis=1))
                seen = seen + dot(jnp.concatenate(rows, axis=0), pairs[g, z // 4])
            own = jnp.zeros((BACK_ROWS, LANES), jnp.float32)
            for i in range(4):
                own = own + jnp.where(back_slab_of == i, seen[i * BACK_ROWS : i * BACK_ROWS + BACK_ROWS], 0.0)
            read_ref[:, slot_lanes(g)] = reduce_x(own * line_ref[g])
            return carry

        lax.fori_loop(0, GROUPS, one, 0, unroll=8)

    def read_rims(p):
        near["down2", p].wait_recv()
        near["up2", p].wait_recv()
        rims = both_rims(rim_in2, p)
        rim_near[0:G, :] = rims
        rim_near[G : G + 16, :] = rims[0:16]

        def one(g, carry):
            window = rim_near[pl.ds(pl.multiple_of(g * 32, 16), WINDOW), :]
            window = jnp.concatenate([jnp.where(rim_of == h, window, 0.0) for h in range(3)], axis=0).astype(BF)
            rim = lax.dot_general(
                window, rim_pairs[g], (((0,), (0,)), ((), ())), preferred_element_type=jnp.float32
            )
            own = rim[0:32] + rim[32:64] + rim[64:96]
            readings = reduce_x(own * line_ref[g]) + read_ref[:, slot_lanes(g)]
            readings = readings + pltpu.roll(readings, 4, 0)
            read_ref[:, slot_lanes(g)] = readings + pltpu.roll(readings, 2, 0)
            return carry

        lax.fori_loop(0, GROUPS, one, 0, unroll=8)

        def unsort(g, total):
            rows = []
            for part in double(read_ref[:, pl.ds(pl.multiple_of(g * 512, 512), 512)]):
                for t in range(4):
                    tile = part[:, t * 128 : t * 128 + 128]
                    rows += [jnp.where(low_half, tile, 0.0), jnp.where(low_half, 0.0, tile)]
            moved = dot(jnp.concatenate(rows, axis=0).astype(BF), rank_ref[...])
            moved = moved[0:64] + moved[64:128]
            for t in range(8):
                total = total + jnp.where(target == g * 8 + t, moved[t * 8 : t * 8 + 8], 0.0)
            return total

        total = lax.fori_loop(0, SLABS // 8, unsort, jnp.zeros((8, atoms), jnp.float32), unroll=4)
        out_ref[p : p + 1, :] = total[0:1]
        out_ref[2 + p : 3 + p, :] = total[1:2]

    spread(0)
    cut(0)
    loads[0].wait()
    send_sides(0)
    for load in loads[1:]:
        load.wait()
    inner_z(0)
    make_gain()
    outer_z(0)
    spread(1)
    x_stage(0)
    cut(1)
    x_stage(1)
    send_sides(1)
    x_stage(2)
    inner_z(1)
    y_stage(0)
    outer_z(1)
    y_stage(1)
    y_stage(2)
    i_stage(0)
    x_stage(3)
    x_stage(4)
    x_stage(5)
    i_stage(1)
    y_stage(3)
    i_stage(2)
    y_stage(4)
    y_stage(5)
    i_stage(3)
    i_stage(4)
    i_stage(5)
    home(0)
    send_back_rims(0)
    home(1)
    read_mesh(0)
    send_back_rims(1)
    read_rims(0)
    read_mesh(1)
    read_rims(1)
    for copy in near.values():
        copy.wait_send()
    for u in range(UNITS):
        wait_slabs(block, u, slab_sems.at[0, u])
        wait_bricks(to_brick, u, brick_sems.at[0, u])
        wait_bricks(back_brick, u, brick_sems2.at[0, u])
        wait_slabs(back_slab, u, slab_sems2.at[0, u])


def body(charges, fractions, inner_cell, dest_slab, filter_amp):
    vmem = pl.BlockSpec(memory_space=pltpu.VMEM)
    anywhere = pl.BlockSpec(memory_space=pl.ANY)
    dma = pltpu.SemaphoreType.DMA
    atoms = charges.shape[1]
    tables = [jnp.asarray(table) for table in make_tables()]
    to_slab = (2, SLABS, 4, 16, 128)
    to_brick = (2, BRICKS, 8, 64, 128)
    return pl.pallas_call(
        kernel,
        out_shape=jax.ShapeDtypeStruct((4, atoms), jnp.float32),
        in_specs=[vmem] * 4 + [pl.BlockSpec(memory_space=pltpu.SMEM)] + [anywhere] * len(tables),
        out_specs=vmem,
        scratch_shapes=[pltpu.VMEM(table.shape, BF) for table in tables]
        + [
            pltpu.VMEM((8, SLABS * CAP), jnp.float32),
            pltpu.VMEM((4, 8, SLABS * CAP), jnp.float32),
            pltpu.VMEM((GROUPS, BACK_ROWS, LANES), jnp.float32),
            pltpu.VMEM((8, SLABS * CAP), jnp.float32),
            pltpu.VMEM((128, atoms), BF),
            pltpu.VMEM((GROUPS, 3, 256, LANES), BF),
            pltpu.VMEM((GROUPS, 3 * WINDOW, LANES), BF),
            pltpu.VMEM((G + 16, 256), jnp.float32),
            pltpu.VMEM((G + 16, 128), jnp.float32),
            pltpu.VMEM((G, 128), jnp.float32),
            pltpu.VMEM((2, PLACES, ROWS, 128), jnp.float32),
            pltpu.VMEM((2, PLACES, BACK_ROWS, 128), BF),
            pltpu.VMEM((2, WIDE, G, 128), jnp.float32),
            pltpu.VMEM((2, G, 128), BF),
            pltpu.VMEM((2, 2, G, 128), BF),
            pltpu.VMEM((2, G, 128), BF),
            pltpu.VMEM((2, 2, G, 128), BF),
            pltpu.VMEM((2, 3, G, 128), BF),
            pltpu.VMEM((2, 3, G, 128), BF),
            pltpu.VMEM((HALVES, 8, 128, 128), jnp.float32),
            pltpu.VMEM((8, G, 128), BF),
        ]
        + [pltpu.VMEM(to_slab, BF)] * 2
        + [pltpu.VMEM(to_brick, BF)] * 4
        + [pltpu.VMEM(to_slab, BF)] * 2
        + [
            pltpu.VMEM((512, 4 * 128), jnp.float32),
            pltpu.VMEM((2, WIDE, G, 128), BF),
            pltpu.VMEM((2, 512, G), jnp.float32),
            dma((len(tables),)),
            dma((2, 16)),
        ]
        + [dma((2, UNITS))] * 4,
        compiler_params=pltpu.CompilerParams(collective_id=0, has_side_effects=True, vmem_limit_bytes=VMEM_LIMIT),
    )(
        charges, fractions, inner_cell.reshape(1, -1), dest_slab.reshape(1, -1), filter_amp, *tables
    )


def solution(mesh):
    in_specs = (
        P(None, ("slab", "brick")),
        P(None, ("slab", "brick")),
        P(("slab", "brick")),
        P(("slab", "brick"), None),
        P(),
    )
    out_specs = P(None, ("slab", "brick"))
    return jax.shard_map(body, mesh=mesh, in_specs=in_specs, out_specs=out_specs, check_vma=False)
```

```python
import math

import numpy as np

import jax
import jax.numpy as jnp
import ml_dtypes
from jax import lax
from jax.experimental import pallas as pl
from jax.experimental.pallas import tpu as pltpu
from jax.sharding import PartitionSpec as P

G = 256
BIN = 16
SLABS = 32
BRICKS = 4
CAP = 64
BF = jnp.bfloat16
MESH = pl.DeviceIdType.MESH


def waves():
    places = np.arange(G)
    angles = 2.0 * np.pi * ((places[:, None] * places[None, :]) % G) / G
    return np.cos(angles), np.sin(angles)


def forward_table():
    cosine, sine = waves()
    return np.stack([np.stack([cosine, sine], 1), np.stack([-sine, cosine], 1)], 0)


def inverse_table():
    cosine, sine = waves()
    return np.stack([np.stack([cosine, -sine], 1), np.stack([sine, cosine], 1)], 0) / G


def spline_weights(fraction):
    remainder = 1.0 - fraction
    square = fraction * fraction
    cubed = square * fraction
    return (
        remainder * remainder * remainder / 6.0,
        (3.0 * cubed - 6.0 * square + 4.0) / 6.0,
        (-3.0 * cubed + 3.0 * square + 3.0 * fraction + 1.0) / 6.0,
        cubed / 6.0,
    )


GROUPS = 8
LANES = 256
PLACES = 132
WINDOW = 48
HALVES = 2
UNITS = 6
PAIR_OF = (0, 0, 0, 1, 1, 1)
TILES = ((0, 1), (1, 2), (2, 4), (0, 2), (2, 3), (3, 4))
UNITS_OF = ((0, 1, 2), (3, 4, 5))
CHIP_ORDER = (
    (2, 2), (0, 1), (1, 0), (0, 3), (3, 0), (1, 2), (2, 1), (3, 2), (2, 3), (0, 2), (2, 0), (1, 1), (3, 3), (1, 3), (3, 1),
)
WIDE = 11
ORDER = (1, 2, 3, 4, 5, 6, 7, 8, 0, 9, 10)
SIDES = (9, 10, 0)
EDGES = (1, 2, 8)
ROWS = 24
BACK_ROWS = 32
VMEM_LIMIT = 56 * 1024 * 1024


def rounded_table(table):
    return np.ascontiguousarray(table).astype(ml_dtypes.bfloat16)


def rim_table():
    table = np.zeros((128, WIDE, 2, 64), np.float32)
    for at, x in enumerate(ORDER):
        for r in range(2):
            for start, y in ((0, 0), (32, 1), (64, 63)):
                table[start + at * 2 + r, x, r, y] = 1.0
    return table.reshape(128, WIDE * 128)


def make_tables():
    forward = forward_table()
    inverse = inverse_table()
    both = np.stack(waves())
    where = np.arange(G)
    where = (where // 16 * 16 + where % 8 * 2 + where // 8 % 2 - 1) % G
    order = np.arange(G).reshape(SLABS, HALVES, 4).transpose(1, 0, 2).reshape(G)
    tables = (
        rim_table(),
        both[:, order][:, :, where].reshape(2, HALVES, 128, G).transpose(1, 0, 2, 3).reshape(512, G),
        both.reshape(512, G),
        forward.reshape(2, G, 2, BRICKS, 64).transpose(3, 2, 4, 0, 1).reshape(512, 512),
        inverse.reshape(2, BRICKS, 64, 2, G).transpose(3, 4, 1, 0, 2).reshape(512, 512),
        both.reshape(512, G) / G,
        both[:, where][:, :, order].reshape(512, G) / G,
    )
    return [rounded_table(table) for table in tables]


def dot(a, b):
    return lax.dot_general(a, b, (((1,), (0,)), ((), ())), preferred_element_type=jnp.float32)


def dot_nt(a, b):
    return lax.dot_general(a, b, (((1,), (1,)), ((), ())), preferred_element_type=jnp.float32)


def iota(shape, dim):
    return lax.broadcasted_iota(jnp.int32, shape, dim)


def double(values):
    high = values.astype(BF).astype(jnp.float32)
    return high, values - high


def dense(cell, weights, places):
    total = 0.0
    for j in range(4):
        total = total + jnp.where(places == cell + j, weights[j], 0.0)
    return total


def slot_lanes(g):
    return pl.ds(pl.multiple_of(g * LANES, LANES), LANES)


def row_x(shape):
    at = iota(shape, 0) >> 1
    return jnp.where(at < 8, at + 1, jnp.where(at == 8, 0, jnp.where(at < WIDE, at, 99)))


def remote(src, dst, sems, at, target):
    copy = pltpu.make_async_remote_copy(
        src_ref=src,
        dst_ref=dst,
        send_sem=sems.at[0, at],
        recv_sem=sems.at[1, at],
        device_id=target,
        device_id_type=MESH,
    )
    copy.start()
    return copy


def kernel(
    charge_ref, frac_ref, cell_ref, target_ref, amp_ref,
    rim_far, zt_far, xt_far, yt_far, iyt_far, ixt_far, izt_far,
    out_ref,
    rim_ref, zt, xt, yt, iyt, ixt, izt,
    sorted_ref, spline_ref, line_ref, read_ref, rank_ref, pairs, rim_pairs, rim_sums, rim_near, rim_part, mesh, mesh_back, slices,
    rim_out, rim_in, rim_out2, rim_in2, side_out, side_in, freq, freq_back,
    block, from_slab, to_brick, from_brick, back_brick, got_brick, back_slab, got_slab, after, potential, gain,
    table_sems, near_sems, slab_sems, brick_sems, brick_sems2, slab_sems2,
):
    slab = lax.axis_index("slab")
    brick = lax.axis_index("brick")
    left = {"slab": lax.rem(slab + SLABS - 1, SLABS)}
    right = {"slab": lax.rem(slab + 1, SLABS)}
    down = {"brick": lax.rem(brick + BRICKS - 1, BRICKS)}
    up = {"brick": lax.rem(brick + 1, BRICKS)}

    barrier = pltpu.get_barrier_semaphore()

    for step in range(1, SLABS):
        pl.semaphore_signal(
            barrier, inc=1, device_id={"slab": lax.rem(slab + step, SLABS)}, device_id_type=MESH
        )
    for step in range(1, BRICKS):
        pl.semaphore_signal(
            barrier, inc=1, device_id={"brick": lax.rem(brick + step, BRICKS)}, device_id_type=MESH
        )

    loads = []
    for at, (far, near) in enumerate(
        ((rim_far, rim_ref), (zt_far, zt), (xt_far, xt), (yt_far, yt), (iyt_far, iyt), (ixt_far, ixt), (izt_far, izt))
    ):
        load = pltpu.make_async_copy(far, near, table_sems.at[at])
        load.start()
        loads.append(load)

    atoms = charge_ref.shape[1]
    blocks = atoms // 128
    target = target_ref[...]
    here = jnp.where(iota((SLABS, atoms), 0) == target, 1.0, 0.0)
    stacked = jnp.concatenate([here[:, b * 128 : b * 128 + 128] for b in range(blocks)], axis=0).astype(BF)
    earlier = jnp.where(iota((128, 128), 0) < iota((128, 128), 1), 1.0, 0.0)
    counts = dot(stacked, jnp.concatenate([earlier, jnp.ones((128, 128), jnp.float32)], axis=1).astype(BF))
    ahead = jnp.zeros((SLABS, 128), jnp.float32)
    ranks = []
    for b in range(blocks):
        rows = slice(b * SLABS, b * SLABS + SLABS)
        ranks.append(counts[rows, 0:128] + ahead)
        ahead = ahead + counts[rows, 128:]
    rank = jnp.sum(here * jnp.concatenate(ranks, axis=1), axis=0, keepdims=True).astype(jnp.int32)
    rank_ref[...] = jnp.where((iota((128, atoms), 0) & 63) == rank, 1.0, 0.0).astype(BF)
    payload = jnp.concatenate([charge_ref[...], frac_ref[...], cell_ref[...].astype(jnp.float32)], axis=0)
    parts = double(payload)
    low_half = iota((8, 128), 1) < 64

    def sort(g, carry):
        rows = []
        for part in parts:
            rows += [jnp.where(target == g * 8 + t, part, 0.0) for t in range(8)]
        moved = dot_nt(jnp.concatenate(rows, axis=0).astype(BF), rank_ref[...])
        moved = moved[0:64] + moved[64:128]
        tiles = [
            jnp.where(low_half, moved[16 * t : 16 * t + 8], moved[16 * t + 8 : 16 * t + 16]) for t in range(4)
        ]
        sorted_ref[:, pl.ds(pl.multiple_of(g * 512, 512), 512)] = jnp.concatenate(tiles, axis=1)
        return carry

    lax.fori_loop(0, SLABS // 8, sort, 0, unroll=4)

    for j, weight in enumerate(spline_weights(sorted_ref[4:7, :])):
        spline_ref[j, 0:3, :] = weight

    def along(dim, g):
        return [spline_ref[j, dim : dim + 1, slot_lanes(g)] for j in range(4)]

    slab_of = iota((ROWS, LANES), 1) >> 6
    first_part = (iota((ROWS, LANES), 0) & 1) == 0
    x_of = row_x((BACK_ROWS, LANES))

    def line(held, g, p):
        return jnp.where(first_part, held[p : p + 1, :], held[2 + p : 3 + p, :]) * line_ref[g, 0:ROWS, :]

    rim_sums[...] = jnp.zeros(rim_sums.shape, jnp.float32)
    window_row = iota((WINDOW, LANES), 0)
    window_place = (window_row >> 4) * 16 + (window_row & 7) * 2 + ((window_row >> 3) & 1)
    slab_start = (iota((1, LANES), 1) >> 6) * 8

    def make_rims(g, carry):
        held = sorted_ref[:, slot_lanes(g)]
        code = held[7:8, :].astype(jnp.int32)
        line_ref[g] = dense((code >> 3) & 7, along(2, g), x_of)
        wz = dense((code & 7) + slab_start, along(0, g), window_place)
        lines = [line(held, g, p) for p in range(2)]
        blocks, columns = [], []
        for h, y in enumerate((64, 65, -1)):
            rim = (wz * dense((code >> 6) - 1, along(1, g), y)).astype(BF)
            rim_pairs[g, pl.ds(h * WINDOW, WINDOW), :] = rim
            blocks.append(rim)
            rows = []
            for p in range(2):
                if h:
                    rows.append(jnp.zeros((32 * h, LANES), jnp.float32))
                rows += [lines[p], jnp.zeros((128 - ROWS - 32 * h, LANES), jnp.float32)]
            columns.append(jnp.concatenate(rows, axis=0).astype(BF))
        at = pl.ds(pl.multiple_of(g * 32, 16), WINDOW)
        rim_sums[at, :] = rim_sums[at, :] + dot_nt(
            jnp.concatenate(blocks, axis=1), jnp.concatenate(columns, axis=1)
        )
        return carry

    lax.fori_loop(0, GROUPS, make_rims, 0, unroll=8)
    rim_sums[0:16, :] = rim_sums[0:16, :] + rim_sums[G : G + 16, :]
    near = {}
    for p in range(2):
        rim_out[p] = rim_sums[0:G, p * 128 : p * 128 + 128].astype(BF)
    pl.semaphore_wait(barrier, SLABS - 1 + BRICKS - 1)
    for p in range(2):
        near["up", p] = remote(rim_out.at[p], rim_in.at[p, 0], near_sems, 8 * p, up)
        near["down", p] = remote(rim_out.at[p], rim_in.at[p, 1], near_sems, 8 * p + 1, down)

    mesh[:, 0:2] = jnp.zeros((2, 2, ROWS, 128), jnp.float32)

    def spread(p):
        def one(g, carry):
            held = sorted_ref[:, slot_lanes(g)]
            if p == 0:
                code = held[7:8, :].astype(jnp.int32)
                wz = dense(code & 7, along(0, g), iota((16, LANES), 0))
                wy = dense((code >> 6) - 1, along(1, g), iota((64, LANES), 0))
            own = line(held, g, p)
            lines = jnp.concatenate([jnp.where(slab_of == i, own, 0.0) for i in range(4)], axis=0).astype(BF)
            for z in (4, 8, 0):
                if p == 0:
                    pairs[g, z // 4] = jnp.concatenate(
                        [wy * wz[z + k : z + k + 1, :] for k in range(4)], axis=0
                    ).astype(BF)
                tile = dot_nt(lines, pairs[g, z // 4])
                for i in range(4):
                    for side in range(2):
                        at = g * 16 + i * 4 + z // 2 + side
                        part = tile[i * ROWS : i * ROWS + ROWS, side * 128 : side * 128 + 128]
                        mesh[p, at] = part if z else mesh[p, at] + part
            return carry

        lax.fori_loop(0, GROUPS, one, 0, unroll=8)
        mesh[p, 0] = mesh[p, 0] + mesh[p, 128]
        mesh[p, 1] = mesh[p, 1] + mesh[p, 129]

    low_all = iota((G, 128), 1) < 64
    sign = jnp.where(low_all, 1.0, -1.0)

    def turn(values):
        return sign[0 : values.shape[0]] * pltpu.roll(values, 64, 1)

    def pack_rims(p, which):
        return dot_nt(
            jnp.concatenate([potential[p, x] for x in which], axis=1),
            jnp.concatenate([rim_ref[:, x * 128 : x * 128 + 128] for x in which], axis=1),
        )

    def both_rims(arrived, p):
        return jnp.where(low_all, arrived[p, 0].astype(jnp.float32), arrived[p, 1].astype(jnp.float32))

    def cut(p):
        def one(step, carry):
            for part in range(3):
                turned = jnp.swapaxes(mesh[p, pl.ds(step * 8, 8), pl.ds(part * 8, 8), :], 0, 1)
                for at, x in enumerate(ORDER[4 * part : 4 * part + 4]):
                    a, b = turned[2 * at], turned[2 * at + 1]
                    slices[p, x, pl.ds(pl.multiple_of(step * 16, 16), 16), :] = jnp.concatenate(
                        [
                            jnp.where(low_half, a, pltpu.roll(b, 64, 1)),
                            jnp.where(low_half, pltpu.roll(a, 64, 1), b),
                        ],
                        axis=0,
                    )
            return carry

        lax.fori_loop(0, 16, one, 0, unroll=8)

    def send_sides(p):
        near["up", p].wait_recv()
        near["down", p].wait_recv()
        rims = both_rims(rim_in, p).astype(BF)
        added = dot(rims, jnp.concatenate([rim_ref[:, x * 128 : x * 128 + 128] for x in SIDES], axis=1))
        for at, x in enumerate(SIDES):
            side_out[p, at] = (slices[p, x] + added[:, at * 128 : at * 128 + 128]).astype(BF)
        near["right", p] = remote(
            side_out.at[p, pl.ds(0, 2)], side_in.at[p, pl.ds(0, 2)], near_sems, 8 * p + 2, right
        )
        near["left", p] = remote(side_out.at[p, pl.ds(2, 1)], side_in.at[p, pl.ds(2, 1)], near_sems, 8 * p + 3, left)
        added = dot(rims, rim_ref[:, 128 : 9 * 128])
        for x in range(1, 9):
            slices[p, x] = slices[p, x] + added[:, x * 128 - 128 : x * 128]

    def signed(k):
        return jnp.where(k < G // 2, k, k - G).astype(jnp.float32)

    def make_gain():
        fx = signed(brick * 64 + iota((64, G), 0))
        fy = signed(iota((64, G), 1))
        flat = fx * fx + fy * fy

        def one(index, carry):
            fz = signed(slab * 8 + index)
            magnitude = jnp.sqrt(fz * fz + flat)
            scaled = magnitude * (1.0 / BIN) - 8.0
            middle = jnp.exp(-0.5 * scaled * scaled)
            sums = [amp_ref[p, 8] * middle for p in range(2)]
            for way in (1, -1):
                ratio = jnp.exp(way * scaled - 0.5)
                bump = middle
                for center in range(8 + way, 16 if way > 0 else -1, way):
                    bump = bump * ratio
                    ratio = ratio * math.exp(-1.0)
                    sums = [sums[p] + amp_ref[p, center] * bump for p in range(2)]
            for p in range(2):
                gain[p, pl.ds(pl.multiple_of(index * 64, 64), 64), :] = sums[p]
            return carry

        lax.fori_loop(0, 8, one, 0, unroll=2)

    def tiles_of(u):
        return pl.ds(TILES[u][0], TILES[u][1] - TILES[u][0])

    def freqs_of(u):
        return pl.ds(2 * TILES[u][0], 2 * (TILES[u][1] - TILES[u][0]))

    def send_bricks(src, dst, u, sems):
        p = PAIR_OF[u]
        for step in range(1, BRICKS):
            peer = lax.rem(brick + step, BRICKS)
            pltpu.make_async_remote_copy(
                src_ref=src.at[p, peer, freqs_of(u)],
                dst_ref=dst.at[p, brick, freqs_of(u)],
                send_sem=sems.at[0, u],
                recv_sem=sems.at[1, u],
                device_id={"brick": peer},
                device_id_type=MESH,
            ).start()
        dst[p, brick, freqs_of(u)] = src[p, brick, freqs_of(u)]

    def wait_bricks(buf, u, sem):
        part = buf.at[PAIR_OF[u], pl.ds(0, BRICKS - 1), freqs_of(u)]
        pltpu.make_async_copy(part, part, sem).wait()

    def wait_slabs(buf, u, sem):
        part = buf.at[PAIR_OF[u], pl.ds(0, SLABS - 1), tiles_of(u)]
        pltpu.make_async_copy(part, part, sem).wait()

    def send_slabs(make, src, dst, u, sems):
        def to(peer):
            pltpu.make_async_remote_copy(
                src_ref=src.at[PAIR_OF[u], peer, tiles_of(u)],
                dst_ref=dst.at[PAIR_OF[u], slab, tiles_of(u)],
                send_sem=sems.at[0, u],
                recv_sem=sems.at[1, u],
                device_id={"slab": peer},
                device_id_type=MESH,
            ).start()

        for dy, dz in CHIP_ORDER:
            pair = lax.rem(slab // 8 + dy, 4) * 4 + lax.rem(slab // 2 + dz, 4)
            make(pair)
            to(2 * pair)
            to(2 * pair + 1)
        make(slab // 2)
        to(slab + 1 - 2 * lax.rem(slab, 2))
        dst[PAIR_OF[u], slab, tiles_of(u)] = src[PAIR_OF[u], slab, tiles_of(u)]

    def z_pair(p, x):
        out = dot(zt[...], jnp.concatenate([slices[p, x], slices[p, x + 1]], axis=1).astype(BF))
        for half in range(HALVES):
            for k in range(2):
                lanes = slice(k * 128, k * 128 + 128)
                u = out[half * 256 : half * 256 + 128, lanes]
                v = out[half * 256 + 128 : half * 256 + 256, lanes]
                freq[half, x - 1 + k] = u + turn(v)

    def inner_z(p):
        z_pair(p, 3)
        z_pair(p, 5)

    def outer_z(p):
        near["right", p].wait_recv()
        for at in range(2):
            slices[p, EDGES[at]] = slices[p, EDGES[at]] + side_in[p, at].astype(jnp.float32)
        z_pair(p, 1)
        near["left", p].wait_recv()
        slices[p, EDGES[2]] = slices[p, EDGES[2]] + side_in[p, 2].astype(jnp.float32)
        z_pair(p, 7)

        def pack(halves):
            def one(pair):
                for half in halves:
                    turned = jnp.swapaxes(freq[half, :, pl.ds(pl.multiple_of(pair * 8, 8), 8), :], 0, 1)
                    block[p, pl.ds(2 * pair, 2), pl.ds(2 * half, 2)] = turned.reshape(2, 2, 16, 128).astype(BF)

            return one

        made = 0
        for u in UNITS_OF[p]:
            needed = (TILES[u][1] + 1) // 2
            send_slabs(pack(range(made, needed)), block, from_slab, u, slab_sems)
            made = needed

    def x_stage(u):
        wait_slabs(from_slab, u, slab_sems.at[1, u])
        p = PAIR_OF[u]
        cols = []
        for tile in range(*TILES[u]):
            held = from_slab[p, :, tile].astype(jnp.float32)
            cols += [held[:, 0:8].reshape(G, 128), held[:, 8:16].reshape(G, 128)]
        out = dot(xt[...], jnp.concatenate(cols, axis=1).astype(BF))
        for k in range(len(cols)):
            lanes = slice(k * 128, k * 128 + 128)
            done = (out[0:G, lanes] + turn(out[G:, lanes])).astype(BF)
            to_brick[p, :, 2 * TILES[u][0] + k] = done.reshape(BRICKS, 64, 128)
        send_bricks(to_brick, from_brick, u, brick_sems)

    def y_stage(u):
        wait_bricks(from_brick, u, brick_sems.at[1, u])
        p = PAIR_OF[u]
        first, count = 2 * TILES[u][0], 2 * (TILES[u][1] - TILES[u][0])
        rows = jnp.concatenate(
            [from_brick[p, b, freqs_of(u)].reshape(count * 64, 128) for b in range(BRICKS)], axis=1
        )
        spectrum = dot(rows, yt[...])
        weight = gain[p, pl.ds(first * 64, count * 64), :]
        filtered = jnp.concatenate([spectrum[:, :G] * weight, spectrum[:, G:] * weight], axis=1)
        back = dot(filtered.astype(BF), iyt[...]).astype(BF)
        for b in range(BRICKS):
            back_brick[p, b, freqs_of(u)] = back[:, b * 128 : b * 128 + 128].reshape(count, 64, 128)
        send_bricks(back_brick, got_brick, u, brick_sems2)

    def i_stage(u):
        wait_bricks(got_brick, u, brick_sems2.at[1, u])
        p = PAIR_OF[u]
        first, last = 2 * TILES[u][0], 2 * TILES[u][1]
        after[:, 0 : (last - first) * 128] = dot(
            ixt[...], jnp.concatenate([got_brick[p, :, k].reshape(G, 128) for k in range(first, last)], axis=1)
        )

        def make(pair):
            at = pl.multiple_of(pair * 16, 16)
            done = []
            for k in range(last - first):
                lanes = pl.ds(k * 128, 128)
                values = after[pl.ds(at, 16), lanes] - turn(after[pl.ds(G + at, 16), lanes])
                done.append(values.reshape(2, 8, 128))
            for tile in range(*TILES[u]):
                two = 2 * tile - first
                back_slab[p, pl.ds(2 * pair, 2), tile] = jnp.concatenate(done[two : two + 2], axis=1).astype(BF)

        send_slabs(make, back_slab, got_slab, u, slab_sems2)

    def home(p):
        there = 0
        for half in range(HALVES):
            for u in UNITS_OF[p]:
                if there < 2 * half + 2 and there == TILES[u][0]:
                    wait_slabs(got_slab, u, slab_sems2.at[1, u])
                    there = TILES[u][1]

            def unpack(s, carry, half=half):
                rows = []
                for eight in range(2):
                    held = got_slab[p, pl.ds(4 * s + 2 * eight, 2), pl.ds(2 * half, 2)].astype(jnp.float32)
                    rows.append(jnp.swapaxes(held.reshape(8, 8, 128), 0, 1))
                at = pl.multiple_of(half * 128 + s * 16, 16)
                freq_back[:, pl.ds(at, 16), :] = jnp.concatenate(rows, axis=1).astype(BF)
                return carry

            lax.fori_loop(0, SLABS // 4, unpack, 0, unroll=8)

        def back_z(x):
            out = dot(izt[...], jnp.concatenate([freq_back[x - 1], freq_back[x]], axis=1))
            for k in range(2):
                lanes = slice(k * 128, k * 128 + 128)
                potential[p, x + k] = (out[0:G, lanes] - turn(out[G:, lanes])).astype(BF)

        back_z(1)
        near["left2", p] = remote(
            potential.at[p, pl.ds(1, 2)], potential.at[p, pl.ds(9, 2)], near_sems, 8 * p + 4, left
        )
        back_z(7)
        near["right2", p] = remote(
            potential.at[p, pl.ds(8, 1)], potential.at[p, pl.ds(0, 1)], near_sems, 8 * p + 5, right
        )
        back_z(3)
        back_z(5)
        rim_part[...] = pack_rims(p, range(1, 9))
        place(p, 0)

    def place(p, part):
        def one(step, carry):
            rows = pl.ds(pl.multiple_of(step * 16, 16), 16)
            blank = jnp.zeros((8, 128), jnp.float32)
            turned = []
            for four in range(2):
                if 8 * part + 4 * four >= WIDE:
                    turned.append(jnp.zeros((8, 8, 128), jnp.float32))
                    continue
                tiles = []
                for x in ORDER[8 * part + 4 * four : 8 * part + 4 * four + 4]:
                    held = potential[p, x, rows, :].astype(jnp.float32)
                    a, b = held[0:8], held[8:16]
                    tiles.append(jnp.where(low_half, a, pltpu.roll(b, 64, 1)))
                    tiles.append(jnp.where(low_half, pltpu.roll(a, 64, 1), b))
                tiles += [blank] * (8 - len(tiles))
                turned.append(jnp.swapaxes(jnp.stack(tiles, axis=0), 0, 1))
            mesh_back[p, pl.ds(step * 8, 8), pl.ds(part * 16, 16), :] = jnp.concatenate(turned, axis=1).astype(BF)
            return carry

        lax.fori_loop(0, 16, one, 0, unroll=8)

    def send_back_rims(p):
        near["left2", p].wait_recv()
        near["right2", p].wait_recv()
        rim_out2[p] = (rim_part[...] + pack_rims(p, (0, 9, 10))).astype(BF)
        near["down2", p] = remote(rim_out2.at[p], rim_in2.at[p, 0], near_sems, 8 * p + 6, down)
        near["up2", p] = remote(rim_out2.at[p], rim_in2.at[p, 1], near_sems, 8 * p + 7, up)
        place(p, 1)
        mesh_back[p, 128] = mesh_back[p, 0]
        mesh_back[p, 129] = mesh_back[p, 1]

    back_slab_of = iota((BACK_ROWS, LANES), 1) >> 6
    rim_of = iota((WINDOW, 128), 1) >> 5

    def reduce_x(own):
        return own[0:8] + own[8:16] + own[16:24] + own[24:32]

    def read_mesh(p):
        def one(g, carry):
            seen = jnp.zeros((4 * BACK_ROWS, LANES), jnp.float32)
            for z in range(0, 12, 4):
                rows = []
                for i in range(4):
                    at = g * 16 + i * 4 + z // 2
                    rows.append(jnp.concatenate([mesh_back[p, at + side] for side in range(2)], axis=1))
                seen = seen + dot(jnp.concatenate(rows, axis=0), pairs[g, z // 4])
            own = jnp.zeros((BACK_ROWS, LANES), jnp.float32)
            for i in range(4):
                own = own + jnp.where(back_slab_of == i, seen[i * BACK_ROWS : i * BACK_ROWS + BACK_ROWS], 0.0)
            read_ref[:, slot_lanes(g)] = reduce_x(own * line_ref[g])
            return carry

        lax.fori_loop(0, GROUPS, one, 0, unroll=8)

    def read_rims(p):
        near["down2", p].wait_recv()
        near["up2", p].wait_recv()
        rims = both_rims(rim_in2, p)
        rim_near[0:G, :] = rims
        rim_near[G : G + 16, :] = rims[0:16]

        def one(g, carry):
            window = rim_near[pl.ds(pl.multiple_of(g * 32, 16), WINDOW), :]
            window = jnp.concatenate([jnp.where(rim_of == h, window, 0.0) for h in range(3)], axis=0).astype(BF)
            rim = lax.dot_general(
                window, rim_pairs[g], (((0,), (0,)), ((), ())), preferred_element_type=jnp.float32
            )
            own = rim[0:32] + rim[32:64] + rim[64:96]
            readings = reduce_x(own * line_ref[g]) + read_ref[:, slot_lanes(g)]
            readings = readings + pltpu.roll(readings, 4, 0)
            read_ref[:, slot_lanes(g)] = readings + pltpu.roll(readings, 2, 0)
            return carry

        lax.fori_loop(0, GROUPS, one, 0, unroll=8)

        def unsort(g, total):
            rows = []
            for part in double(read_ref[:, pl.ds(pl.multiple_of(g * 512, 512), 512)]):
                for t in range(4):
                    tile = part[:, t * 128 : t * 128 + 128]
                    rows += [jnp.where(low_half, tile, 0.0), jnp.where(low_half, 0.0, tile)]
            moved = dot(jnp.concatenate(rows, axis=0).astype(BF), rank_ref[...])
            moved = moved[0:64] + moved[64:128]
            for t in range(8):
                total = total + jnp.where(target == g * 8 + t, moved[t * 8 : t * 8 + 8], 0.0)
            return total

        total = lax.fori_loop(0, SLABS // 8, unsort, jnp.zeros((8, atoms), jnp.float32), unroll=4)
        out_ref[p : p + 1, :] = total[0:1]
        out_ref[2 + p : 3 + p, :] = total[1:2]

    spread(0)
    cut(0)
    loads[0].wait()
    send_sides(0)
    for load in loads[1:]:
        load.wait()
    inner_z(0)
    make_gain()
    outer_z(0)
    spread(1)
    cut(1)
    send_sides(1)
    for u in UNITS_OF[0]:
        x_stage(u)
    inner_z(1)
    outer_z(1)
    for u in UNITS_OF[0]:
        y_stage(u)
    for u in UNITS_OF[1]:
        x_stage(u)
    for u in UNITS_OF[0]:
        i_stage(u)
    for u in UNITS_OF[1]:
        y_stage(u)
    home(0)
    for u in UNITS_OF[1]:
        i_stage(u)
    send_back_rims(0)
    home(1)
    read_mesh(0)
    send_back_rims(1)
    read_rims(0)
    read_mesh(1)
    read_rims(1)
    for copy in near.values():
        copy.wait_send()
    for u in range(UNITS):
        wait_slabs(block, u, slab_sems.at[0, u])
        wait_bricks(to_brick, u, brick_sems.at[0, u])
        wait_bricks(back_brick, u, brick_sems2.at[0, u])
        wait_slabs(back_slab, u, slab_sems2.at[0, u])


def body(charges, fractions, inner_cell, dest_slab, filter_amp):
    vmem = pl.BlockSpec(memory_space=pltpu.VMEM)
    anywhere = pl.BlockSpec(memory_space=pl.ANY)
    dma = pltpu.SemaphoreType.DMA
    atoms = charges.shape[1]
    tables = [jnp.asarray(table) for table in make_tables()]
    to_slab = (2, SLABS, 4, 16, 128)
    to_brick = (2, BRICKS, 8, 64, 128)
    return pl.pallas_call(
        kernel,
        out_shape=jax.ShapeDtypeStruct((4, atoms), jnp.float32),
        in_specs=[vmem] * 4 + [pl.BlockSpec(memory_space=pltpu.SMEM)] + [anywhere] * len(tables),
        out_specs=vmem,
        scratch_shapes=[pltpu.VMEM(table.shape, BF) for table in tables]
        + [
            pltpu.VMEM((8, SLABS * CAP), jnp.float32),
            pltpu.VMEM((4, 8, SLABS * CAP), jnp.float32),
            pltpu.VMEM((GROUPS, BACK_ROWS, LANES), jnp.float32),
            pltpu.VMEM((8, SLABS * CAP), jnp.float32),
            pltpu.VMEM((128, atoms), BF),
            pltpu.VMEM((GROUPS, 3, 256, LANES), BF),
            pltpu.VMEM((GROUPS, 3 * WINDOW, LANES), BF),
            pltpu.VMEM((G + 16, 256), jnp.float32),
            pltpu.VMEM((G + 16, 128), jnp.float32),
            pltpu.VMEM((G, 128), jnp.float32),
            pltpu.VMEM((2, PLACES, ROWS, 128), jnp.float32),
            pltpu.VMEM((2, PLACES, BACK_ROWS, 128), BF),
            pltpu.VMEM((2, WIDE, G, 128), jnp.float32),
            pltpu.VMEM((2, G, 128), BF),
            pltpu.VMEM((2, 2, G, 128), BF),
            pltpu.VMEM((2, G, 128), BF),
            pltpu.VMEM((2, 2, G, 128), BF),
            pltpu.VMEM((2, 3, G, 128), BF),
            pltpu.VMEM((2, 3, G, 128), BF),
            pltpu.VMEM((HALVES, 8, 128, 128), jnp.float32),
            pltpu.VMEM((8, G, 128), BF),
        ]
        + [pltpu.VMEM(to_slab, BF)] * 2
        + [pltpu.VMEM(to_brick, BF)] * 4
        + [pltpu.VMEM(to_slab, BF)] * 2
        + [
            pltpu.VMEM((512, 4 * 128), jnp.float32),
            pltpu.VMEM((2, WIDE, G, 128), BF),
            pltpu.VMEM((2, 512, G), jnp.float32),
            dma((len(tables),)),
            dma((2, 16)),
        ]
        + [dma((2, UNITS))] * 4,
        compiler_params=pltpu.CompilerParams(collective_id=0, has_side_effects=True, vmem_limit_bytes=VMEM_LIMIT),
    )(
        charges, fractions, inner_cell.reshape(1, -1), dest_slab.reshape(1, -1), filter_amp, *tables
    )


def solution(mesh):
    in_specs = (
        P(None, ("slab", "brick")),
        P(None, ("slab", "brick")),
        P(("slab", "brick")),
        P(("slab", "brick"), None),
        P(),
    )
    out_specs = P(None, ("slab", "brick"))
    return jax.shard_map(body, mesh=mesh, in_specs=in_specs, out_specs=out_specs, check_vma=False)
```

```python
import math

import numpy as np

import jax
import jax.numpy as jnp
import ml_dtypes
from jax import lax
from jax.experimental import pallas as pl
from jax.experimental.pallas import tpu as pltpu
from jax.sharding import PartitionSpec as P

G = 256
BIN = 16
SLABS = 32
BRICKS = 4
CAP = 64
BF = jnp.bfloat16
MESH = pl.DeviceIdType.MESH


def waves():
    places = np.arange(G)
    angles = 2.0 * np.pi * ((places[:, None] * places[None, :]) % G) / G
    return np.cos(angles), np.sin(angles)


def forward_table():
    cosine, sine = waves()
    return np.stack([np.stack([cosine, sine], 1), np.stack([-sine, cosine], 1)], 0)


def inverse_table():
    cosine, sine = waves()
    return np.stack([np.stack([cosine, -sine], 1), np.stack([sine, cosine], 1)], 0) / G


def spline_weights(fraction):
    remainder = 1.0 - fraction
    square = fraction * fraction
    cubed = square * fraction
    return (
        remainder * remainder * remainder / 6.0,
        (3.0 * cubed - 6.0 * square + 4.0) / 6.0,
        (-3.0 * cubed + 3.0 * square + 3.0 * fraction + 1.0) / 6.0,
        cubed / 6.0,
    )


GROUPS = 8
LANES = 256
PLACES = 132
WINDOW = 48
HALVES = 2
UNITS = 6
PAIR_OF = (0, 0, 0, 1, 1, 1)
TILES = ((0, 1), (1, 2), (2, 4), (0, 2), (2, 3), (3, 4))
UNITS_OF = ((0, 1, 2), (3, 4, 5))
CHIP_ORDER = (
    (2, 2), (0, 1), (1, 0), (0, 3), (3, 0), (1, 2), (2, 1), (3, 2), (2, 3), (0, 2), (2, 0), (1, 1), (3, 3), (1, 3), (3, 1),
)
WIDE = 11
ORDER = (1, 2, 3, 4, 5, 6, 7, 8, 0, 9, 10)
SIDES = (9, 10, 0)
EDGES = (1, 2, 8)
ROWS = 24
BACK_ROWS = 32
VMEM_LIMIT = 56 * 1024 * 1024


def rounded_table(table):
    return np.ascontiguousarray(table).astype(ml_dtypes.bfloat16)


def rim_table():
    table = np.zeros((128, WIDE, 2, 64), np.float32)
    for at, x in enumerate(ORDER):
        for r in range(2):
            for start, y in ((0, 0), (32, 1), (64, 63)):
                table[start + at * 2 + r, x, r, y] = 1.0
    return table.reshape(128, WIDE * 128)


def make_tables():
    forward = forward_table()
    inverse = inverse_table()
    both = np.stack(waves())
    where = np.arange(G)
    where = (where // 16 * 16 + where % 8 * 2 + where // 8 % 2 - 1) % G
    order = np.arange(G).reshape(SLABS, HALVES, 4).transpose(1, 0, 2).reshape(G)
    tables = (
        rim_table(),
        both[:, order][:, :, where].reshape(2, HALVES, 128, G).transpose(1, 0, 2, 3).reshape(512, G),
        both.reshape(512, G),
        forward.reshape(2, G, 2, BRICKS, 64).transpose(3, 2, 4, 0, 1).reshape(512, 512),
        inverse.reshape(2, BRICKS, 64, 2, G).transpose(3, 4, 1, 0, 2).reshape(512, 512),
        both.reshape(512, G) / G,
        both[:, where][:, :, order].reshape(512, G) / G,
    )
    return [rounded_table(table) for table in tables]


def dot(a, b):
    return lax.dot_general(a, b, (((1,), (0,)), ((), ())), preferred_element_type=jnp.float32)


def dot_nt(a, b):
    return lax.dot_general(a, b, (((1,), (1,)), ((), ())), preferred_element_type=jnp.float32)


def iota(shape, dim):
    return lax.broadcasted_iota(jnp.int32, shape, dim)


def double(values):
    high = values.astype(BF).astype(jnp.float32)
    return high, values - high


def dense(cell, weights, places):
    total = 0.0
    for j in range(4):
        total = total + jnp.where(places == cell + j, weights[j], 0.0)
    return total


def slot_lanes(g):
    return pl.ds(pl.multiple_of(g * LANES, LANES), LANES)


def row_x(shape):
    at = iota(shape, 0) >> 1
    return jnp.where(at < 8, at + 1, jnp.where(at == 8, 0, jnp.where(at < WIDE, at, 99)))


def remote(src, dst, sems, at, target):
    copy = pltpu.make_async_remote_copy(
        src_ref=src,
        dst_ref=dst,
        send_sem=sems.at[0, at],
        recv_sem=sems.at[1, at],
        device_id=target,
        device_id_type=MESH,
    )
    copy.start()
    return copy


def kernel(
    charge_ref, frac_ref, cell_ref, target_ref, amp_ref,
    rim_far, zt_far, xt_far, yt_far, iyt_far, ixt_far, izt_far,
    out_ref,
    rim_ref, zt, xt, yt, iyt, ixt, izt,
    sorted_ref, spline_ref, line_ref, read_ref, rank_ref, pairs, rim_pairs, rim_sums, rim_near, rim_part, mesh, mesh_back, slices,
    rim_out, rim_in, rim_out2, rim_in2, side_out, side_in, freq, freq_back,
    block, from_slab, to_brick, from_brick, back_brick, got_brick, back_slab, got_slab, after, potential, gain,
    table_sems, near_sems, slab_sems, brick_sems, brick_sems2, slab_sems2,
):
    slab = lax.axis_index("slab")
    brick = lax.axis_index("brick")
    left = {"slab": lax.rem(slab + SLABS - 1, SLABS)}
    right = {"slab": lax.rem(slab + 1, SLABS)}
    down = {"brick": lax.rem(brick + BRICKS - 1, BRICKS)}
    up = {"brick": lax.rem(brick + 1, BRICKS)}

    barrier = pltpu.get_barrier_semaphore()

    for step in range(1, SLABS):
        pl.semaphore_signal(
            barrier, inc=1, device_id={"slab": lax.rem(slab + step, SLABS)}, device_id_type=MESH
        )
    for step in range(1, BRICKS):
        pl.semaphore_signal(
            barrier, inc=1, device_id={"brick": lax.rem(brick + step, BRICKS)}, device_id_type=MESH
        )

    loads = []
    for at, (far, near) in enumerate(
        ((rim_far, rim_ref), (zt_far, zt), (xt_far, xt), (yt_far, yt), (iyt_far, iyt), (ixt_far, ixt), (izt_far, izt))
    ):
        load = pltpu.make_async_copy(far, near, table_sems.at[at])
        load.start()
        loads.append(load)

    atoms = charge_ref.shape[1]
    blocks = atoms // 128
    target = target_ref[...]
    here = jnp.where(iota((SLABS, atoms), 0) == target, 1.0, 0.0)
    stacked = jnp.concatenate([here[:, b * 128 : b * 128 + 128] for b in range(blocks)], axis=0).astype(BF)
    earlier = jnp.where(iota((128, 128), 0) < iota((128, 128), 1), 1.0, 0.0)
    counts = dot(stacked, jnp.concatenate([earlier, jnp.ones((128, 128), jnp.float32)], axis=1).astype(BF))
    ahead = jnp.zeros((SLABS, 128), jnp.float32)
    ranks = []
    for b in range(blocks):
        rows = slice(b * SLABS, b * SLABS + SLABS)
        ranks.append(counts[rows, 0:128] + ahead)
        ahead = ahead + counts[rows, 128:]
    rank = jnp.sum(here * jnp.concatenate(ranks, axis=1), axis=0, keepdims=True).astype(jnp.int32)
    rank_ref[...] = jnp.where((iota((128, atoms), 0) & 63) == rank, 1.0, 0.0).astype(BF)
    payload = jnp.concatenate([charge_ref[...], frac_ref[...], cell_ref[...].astype(jnp.float32)], axis=0)
    parts = double(payload)
    low_half = iota((8, 128), 1) < 64

    def sort(g, carry):
        rows = []
        for part in parts:
            rows += [jnp.where(target == g * 8 + t, part, 0.0) for t in range(8)]
        moved = dot_nt(jnp.concatenate(rows, axis=0).astype(BF), rank_ref[...])
        moved = moved[0:64] + moved[64:128]
        tiles = [
            jnp.where(low_half, moved[16 * t : 16 * t + 8], moved[16 * t + 8 : 16 * t + 16]) for t in range(4)
        ]
        sorted_ref[:, pl.ds(pl.multiple_of(g * 512, 512), 512)] = jnp.concatenate(tiles, axis=1)
        return carry

    lax.fori_loop(0, SLABS // 8, sort, 0, unroll=4)

    for j, weight in enumerate(spline_weights(sorted_ref[4:7, :])):
        spline_ref[j, 0:3, :] = weight

    def along(dim, g):
        return [spline_ref[j, dim : dim + 1, slot_lanes(g)] for j in range(4)]

    slab_of = iota((ROWS, LANES), 1) >> 6
    first_part = (iota((ROWS, LANES), 0) & 1) == 0
    x_of = row_x((BACK_ROWS, LANES))

    def line(held, g, p):
        return jnp.where(first_part, held[p : p + 1, :], held[2 + p : 3 + p, :]) * line_ref[g, 0:ROWS, :]

    rim_sums[...] = jnp.zeros(rim_sums.shape, jnp.float32)
    window_row = iota((WINDOW, LANES), 0)
    window_place = (window_row >> 4) * 16 + (window_row & 7) * 2 + ((window_row >> 3) & 1)
    slab_start = (iota((1, LANES), 1) >> 6) * 8

    def make_rims(g, carry):
        held = sorted_ref[:, slot_lanes(g)]
        code = held[7:8, :].astype(jnp.int32)
        line_ref[g] = dense((code >> 3) & 7, along(2, g), x_of)
        wz = dense((code & 7) + slab_start, along(0, g), window_place)
        lines = [line(held, g, p) for p in range(2)]
        blocks, columns = [], []
        for h, y in enumerate((64, 65, -1)):
            rim = (wz * dense((code >> 6) - 1, along(1, g), y)).astype(BF)
            rim_pairs[g, pl.ds(h * WINDOW, WINDOW), :] = rim
            blocks.append(rim)
            rows = []
            for p in range(2):
                if h:
                    rows.append(jnp.zeros((32 * h, LANES), jnp.float32))
                rows += [lines[p], jnp.zeros((128 - ROWS - 32 * h, LANES), jnp.float32)]
            columns.append(jnp.concatenate(rows, axis=0).astype(BF))
        at = pl.ds(pl.multiple_of(g * 32, 16), WINDOW)
        rim_sums[at, :] = rim_sums[at, :] + dot_nt(
            jnp.concatenate(blocks, axis=1), jnp.concatenate(columns, axis=1)
        )
        return carry

    lax.fori_loop(0, GROUPS, make_rims, 0, unroll=8)
    rim_sums[0:16, :] = rim_sums[0:16, :] + rim_sums[G : G + 16, :]
    near = {}
    for p in range(2):
        rim_out[p] = rim_sums[0:G, p * 128 : p * 128 + 128].astype(BF)
    pl.semaphore_wait(barrier, SLABS - 1 + BRICKS - 1)
    for p in range(2):
        near["up", p] = remote(rim_out.at[p], rim_in.at[p, 0], near_sems, 8 * p, up)
        near["down", p] = remote(rim_out.at[p], rim_in.at[p, 1], near_sems, 8 * p + 1, down)

    mesh[:, 0:2] = jnp.zeros((2, 2, ROWS, 128), jnp.float32)

    def spread(p):
        def one(g, carry):
            held = sorted_ref[:, slot_lanes(g)]
            if p == 0:
                code = held[7:8, :].astype(jnp.int32)
                wz = dense(code & 7, along(0, g), iota((16, LANES), 0))
                wy = dense((code >> 6) - 1, along(1, g), iota((64, LANES), 0))
            own = line(held, g, p)
            lines = jnp.concatenate([jnp.where(slab_of == i, own, 0.0) for i in range(4)], axis=0).astype(BF)
            for z in (4, 8, 0):
                if p == 0:
                    pairs[g, z // 4] = jnp.concatenate(
                        [wy * wz[z + k : z + k + 1, :] for k in range(4)], axis=0
                    ).astype(BF)
                tile = dot_nt(lines, pairs[g, z // 4])
                for i in range(4):
                    for side in range(2):
                        at = g * 16 + i * 4 + z // 2 + side
                        part = tile[i * ROWS : i * ROWS + ROWS, side * 128 : side * 128 + 128]
                        mesh[p, at] = part if z else mesh[p, at] + part
            return carry

        lax.fori_loop(0, GROUPS, one, 0, unroll=8)
        mesh[p, 0] = mesh[p, 0] + mesh[p, 128]
        mesh[p, 1] = mesh[p, 1] + mesh[p, 129]

    low_all = iota((G, 128), 1) < 64
    sign = jnp.where(low_all, 1.0, -1.0)

    def turn(values):
        return sign[0 : values.shape[0]] * pltpu.roll(values, 64, 1)

    def pack_rims(p, which):
        return dot_nt(
            jnp.concatenate([potential[p, x] for x in which], axis=1),
            jnp.concatenate([rim_ref[:, x * 128 : x * 128 + 128] for x in which], axis=1),
        )

    def both_rims(arrived, p):
        return jnp.where(low_all, arrived[p, 0].astype(jnp.float32), arrived[p, 1].astype(jnp.float32))

    def cut(p):
        def one(step, carry):
            for part in range(3):
                turned = jnp.swapaxes(mesh[p, pl.ds(step * 8, 8), pl.ds(part * 8, 8), :], 0, 1)
                for at, x in enumerate(ORDER[4 * part : 4 * part + 4]):
                    a, b = turned[2 * at], turned[2 * at + 1]
                    slices[p, x, pl.ds(pl.multiple_of(step * 16, 16), 16), :] = jnp.concatenate(
                        [
                            jnp.where(low_half, a, pltpu.roll(b, 64, 1)),
                            jnp.where(low_half, pltpu.roll(a, 64, 1), b),
                        ],
                        axis=0,
                    )
            return carry

        lax.fori_loop(0, 16, one, 0, unroll=8)

    def send_sides(p):
        near["up", p].wait_recv()
        near["down", p].wait_recv()
        rims = both_rims(rim_in, p).astype(BF)
        added = dot(rims, jnp.concatenate([rim_ref[:, x * 128 : x * 128 + 128] for x in SIDES], axis=1))
        for at, x in enumerate(SIDES):
            side_out[p, at] = (slices[p, x] + added[:, at * 128 : at * 128 + 128]).astype(BF)
        near["right", p] = remote(
            side_out.at[p, pl.ds(0, 2)], side_in.at[p, pl.ds(0, 2)], near_sems, 8 * p + 2, right
        )
        near["left", p] = remote(side_out.at[p, pl.ds(2, 1)], side_in.at[p, pl.ds(2, 1)], near_sems, 8 * p + 3, left)
        added = dot(rims, rim_ref[:, 128 : 9 * 128])
        for x in range(1, 9):
            slices[p, x] = slices[p, x] + added[:, x * 128 - 128 : x * 128]

    def signed(k):
        return jnp.where(k < G // 2, k, k - G).astype(jnp.float32)

    def make_gain():
        fx = signed(brick * 64 + iota((64, G), 0))
        fy = signed(iota((64, G), 1))
        flat = fx * fx + fy * fy

        def one(index, carry):
            fz = signed(slab * 8 + index)
            magnitude = jnp.sqrt(fz * fz + flat)
            scaled = magnitude * (1.0 / BIN) - 8.0
            middle = jnp.exp(-0.5 * scaled * scaled)
            sums = [amp_ref[p, 8] * middle for p in range(2)]
            for way in (1, -1):
                ratio = jnp.exp(way * scaled - 0.5)
                bump = middle
                for center in range(8 + way, 16 if way > 0 else -1, way):
                    bump = bump * ratio
                    ratio = ratio * math.exp(-1.0)
                    sums = [sums[p] + amp_ref[p, center] * bump for p in range(2)]
            for p in range(2):
                gain[p, pl.ds(pl.multiple_of(index * 64, 64), 64), :] = sums[p]
            return carry

        lax.fori_loop(0, 8, one, 0, unroll=2)

    def tiles_of(u):
        return pl.ds(TILES[u][0], TILES[u][1] - TILES[u][0])

    def freqs_of(u):
        return pl.ds(2 * TILES[u][0], 2 * (TILES[u][1] - TILES[u][0]))

    def send_bricks(src, dst, u, sems):
        p = PAIR_OF[u]
        for step in range(1, BRICKS):
            peer = lax.rem(brick + step, BRICKS)
            pltpu.make_async_remote_copy(
                src_ref=src.at[p, peer, freqs_of(u)],
                dst_ref=dst.at[p, brick, freqs_of(u)],
                send_sem=sems.at[0, u],
                recv_sem=sems.at[1, u],
                device_id={"brick": peer},
                device_id_type=MESH,
            ).start()
        dst[p, brick, freqs_of(u)] = src[p, brick, freqs_of(u)]

    def wait_bricks(buf, u, sem):
        part = buf.at[PAIR_OF[u], pl.ds(0, BRICKS - 1), freqs_of(u)]
        pltpu.make_async_copy(part, part, sem).wait()

    def wait_slabs(buf, u, sem):
        part = buf.at[PAIR_OF[u], pl.ds(0, SLABS - 1), tiles_of(u)]
        pltpu.make_async_copy(part, part, sem).wait()

    def send_slabs(make, src, dst, u, sems):
        def to(peer):
            pltpu.make_async_remote_copy(
                src_ref=src.at[PAIR_OF[u], peer, tiles_of(u)],
                dst_ref=dst.at[PAIR_OF[u], slab, tiles_of(u)],
                send_sem=sems.at[0, u],
                recv_sem=sems.at[1, u],
                device_id={"slab": peer},
                device_id_type=MESH,
            ).start()

        for dy, dz in CHIP_ORDER:
            pair = lax.rem(slab // 8 + dy, 4) * 4 + lax.rem(slab // 2 + dz, 4)
            make(pair)
            to(2 * pair)
            to(2 * pair + 1)
        make(slab // 2)
        to(slab + 1 - 2 * lax.rem(slab, 2))
        dst[PAIR_OF[u], slab, tiles_of(u)] = src[PAIR_OF[u], slab, tiles_of(u)]

    def z_pair(p, x):
        out = dot(zt[...], jnp.concatenate([slices[p, x], slices[p, x + 1]], axis=1).astype(BF))
        for half in range(HALVES):
            for k in range(2):
                lanes = slice(k * 128, k * 128 + 128)
                u = out[half * 256 : half * 256 + 128, lanes]
                v = out[half * 256 + 128 : half * 256 + 256, lanes]
                freq[half, x - 1 + k] = u + turn(v)

    def inner_z(p):
        z_pair(p, 3)
        z_pair(p, 5)

    def outer_z(p):
        near["right", p].wait_recv()
        for at in range(2):
            slices[p, EDGES[at]] = slices[p, EDGES[at]] + side_in[p, at].astype(jnp.float32)
        z_pair(p, 1)
        near["left", p].wait_recv()
        slices[p, EDGES[2]] = slices[p, EDGES[2]] + side_in[p, 2].astype(jnp.float32)
        z_pair(p, 7)

        def pack(halves):
            def one(pair):
                for half in halves:
                    turned = jnp.swapaxes(freq[half, :, pl.ds(pl.multiple_of(pair * 8, 8), 8), :], 0, 1)
                    block[p, pl.ds(2 * pair, 2), pl.ds(2 * half, 2)] = turned.reshape(2, 2, 16, 128).astype(BF)

            return one

        made = 0
        for u in UNITS_OF[p]:
            needed = (TILES[u][1] + 1) // 2
            send_slabs(pack(range(made, needed)), block, from_slab, u, slab_sems)
            made = needed

    def x_stage(u):
        wait_slabs(from_slab, u, slab_sems.at[1, u])
        p = PAIR_OF[u]
        cols = []
        for tile in range(*TILES[u]):
            held = from_slab[p, :, tile].astype(jnp.float32)
            cols += [held[:, 0:8].reshape(G, 128), held[:, 8:16].reshape(G, 128)]
        out = dot(xt[...], jnp.concatenate(cols, axis=1).astype(BF))
        for k in range(len(cols)):
            lanes = slice(k * 128, k * 128 + 128)
            done = (out[0:G, lanes] + turn(out[G:, lanes])).astype(BF)
            to_brick[p, :, 2 * TILES[u][0] + k] = done.reshape(BRICKS, 64, 128)
        send_bricks(to_brick, from_brick, u, brick_sems)

    def y_stage(u):
        wait_bricks(from_brick, u, brick_sems.at[1, u])
        p = PAIR_OF[u]
        first, count = 2 * TILES[u][0], 2 * (TILES[u][1] - TILES[u][0])
        rows = jnp.concatenate(
            [from_brick[p, b, freqs_of(u)].reshape(count * 64, 128) for b in range(BRICKS)], axis=1
        )
        spectrum = dot(rows, yt[...])
        weight = gain[p, pl.ds(first * 64, count * 64), :]
        filtered = jnp.concatenate([spectrum[:, :G] * weight, spectrum[:, G:] * weight], axis=1)
        back = dot(filtered.astype(BF), iyt[...]).astype(BF)
        for b in range(BRICKS):
            back_brick[p, b, freqs_of(u)] = back[:, b * 128 : b * 128 + 128].reshape(count, 64, 128)
        send_bricks(back_brick, got_brick, u, brick_sems2)

    def i_stage(u):
        wait_bricks(got_brick, u, brick_sems2.at[1, u])
        p = PAIR_OF[u]
        first, last = 2 * TILES[u][0], 2 * TILES[u][1]
        after[:, 0 : (last - first) * 128] = dot(
            ixt[...], jnp.concatenate([got_brick[p, :, k].reshape(G, 128) for k in range(first, last)], axis=1)
        )

        def make(pair):
            at = pl.multiple_of(pair * 16, 16)
            done = []
            for k in range(last - first):
                lanes = pl.ds(k * 128, 128)
                values = after[pl.ds(at, 16), lanes] - turn(after[pl.ds(G + at, 16), lanes])
                done.append(values.reshape(2, 8, 128))
            for tile in range(*TILES[u]):
                two = 2 * tile - first
                back_slab[p, pl.ds(2 * pair, 2), tile] = jnp.concatenate(done[two : two + 2], axis=1).astype(BF)

        send_slabs(make, back_slab, got_slab, u, slab_sems2)

    def home(p):
        there = 0
        for half in range(HALVES):
            for u in UNITS_OF[p]:
                if there < 2 * half + 2 and there == TILES[u][0]:
                    wait_slabs(got_slab, u, slab_sems2.at[1, u])
                    there = TILES[u][1]

            def unpack(s, carry, half=half):
                rows = []
                for eight in range(2):
                    held = got_slab[p, pl.ds(4 * s + 2 * eight, 2), pl.ds(2 * half, 2)].astype(jnp.float32)
                    rows.append(jnp.swapaxes(held.reshape(8, 8, 128), 0, 1))
                at = pl.multiple_of(half * 128 + s * 16, 16)
                freq_back[:, pl.ds(at, 16), :] = jnp.concatenate(rows, axis=1).astype(BF)
                return carry

            lax.fori_loop(0, SLABS // 4, unpack, 0, unroll=8)

        def back_z(x):
            out = dot(izt[...], jnp.concatenate([freq_back[x - 1], freq_back[x]], axis=1))
            for k in range(2):
                lanes = slice(k * 128, k * 128 + 128)
                potential[p, x + k] = (out[0:G, lanes] - turn(out[G:, lanes])).astype(BF)

        back_z(1)
        near["left2", p] = remote(
            potential.at[p, pl.ds(1, 2)], potential.at[p, pl.ds(9, 2)], near_sems, 8 * p + 4, left
        )
        back_z(7)
        near["right2", p] = remote(
            potential.at[p, pl.ds(8, 1)], potential.at[p, pl.ds(0, 1)], near_sems, 8 * p + 5, right
        )
        back_z(3)
        back_z(5)
        rim_part[...] = pack_rims(p, range(1, 9))
        place(p, 0)

    def place(p, part):
        def one(step, carry):
            rows = pl.ds(pl.multiple_of(step * 16, 16), 16)
            blank = jnp.zeros((8, 128), jnp.float32)
            turned = []
            for four in range(2):
                if 8 * part + 4 * four >= WIDE:
                    turned.append(jnp.zeros((8, 8, 128), jnp.float32))
                    continue
                tiles = []
                for x in ORDER[8 * part + 4 * four : 8 * part + 4 * four + 4]:
                    held = potential[p, x, rows, :].astype(jnp.float32)
                    a, b = held[0:8], held[8:16]
                    tiles.append(jnp.where(low_half, a, pltpu.roll(b, 64, 1)))
                    tiles.append(jnp.where(low_half, pltpu.roll(a, 64, 1), b))
                tiles += [blank] * (8 - len(tiles))
                turned.append(jnp.swapaxes(jnp.stack(tiles, axis=0), 0, 1))
            mesh_back[p, pl.ds(step * 8, 8), pl.ds(part * 16, 16), :] = jnp.concatenate(turned, axis=1).astype(BF)
            return carry

        lax.fori_loop(0, 16, one, 0, unroll=8)

    def send_back_rims(p):
        near["left2", p].wait_recv()
        near["right2", p].wait_recv()
        rim_out2[p] = (rim_part[...] + pack_rims(p, (0, 9, 10))).astype(BF)
        near["down2", p] = remote(rim_out2.at[p], rim_in2.at[p, 0], near_sems, 8 * p + 6, down)
        near["up2", p] = remote(rim_out2.at[p], rim_in2.at[p, 1], near_sems, 8 * p + 7, up)
        place(p, 1)
        mesh_back[p, 128] = mesh_back[p, 0]
        mesh_back[p, 129] = mesh_back[p, 1]

    back_slab_of = iota((BACK_ROWS, LANES), 1) >> 6
    rim_of = iota((WINDOW, 128), 1) >> 5

    def reduce_x(own):
        return own[0:8] + own[8:16] + own[16:24] + own[24:32]

    def read_mesh(p):
        def one(g, carry):
            seen = jnp.zeros((4 * BACK_ROWS, LANES), jnp.float32)
            for z in range(0, 12, 4):
                rows = []
                for i in range(4):
                    at = g * 16 + i * 4 + z // 2
                    rows.append(jnp.concatenate([mesh_back[p, at + side] for side in range(2)], axis=1))
                seen = seen + dot(jnp.concatenate(rows, axis=0), pairs[g, z // 4])
            own = jnp.zeros((BACK_ROWS, LANES), jnp.float32)
            for i in range(4):
                own = own + jnp.where(back_slab_of == i, seen[i * BACK_ROWS : i * BACK_ROWS + BACK_ROWS], 0.0)
            read_ref[:, slot_lanes(g)] = reduce_x(own * line_ref[g])
            return carry

        lax.fori_loop(0, GROUPS, one, 0, unroll=8)

    def read_rims(p):
        near["down2", p].wait_recv()
        near["up2", p].wait_recv()
        rims = both_rims(rim_in2, p)
        rim_near[0:G, :] = rims
        rim_near[G : G + 16, :] = rims[0:16]

        def one(g, carry):
            window = rim_near[pl.ds(pl.multiple_of(g * 32, 16), WINDOW), :]
            window = jnp.concatenate([jnp.where(rim_of == h, window, 0.0) for h in range(3)], axis=0).astype(BF)
            rim = lax.dot_general(
                window, rim_pairs[g], (((0,), (0,)), ((), ())), preferred_element_type=jnp.float32
            )
            own = rim[0:32] + rim[32:64] + rim[64:96]
            readings = reduce_x(own * line_ref[g]) + read_ref[:, slot_lanes(g)]
            readings = readings + pltpu.roll(readings, 4, 0)
            read_ref[:, slot_lanes(g)] = readings + pltpu.roll(readings, 2, 0)
            return carry

        lax.fori_loop(0, GROUPS, one, 0, unroll=8)

    def to_atoms(p):
        def unsort(g, total):
            rows = []
            for part in double(read_ref[:, pl.ds(pl.multiple_of(g * 512, 512), 512)]):
                for t in range(4):
                    tile = part[:, t * 128 : t * 128 + 128]
                    rows += [jnp.where(low_half, tile, 0.0), jnp.where(low_half, 0.0, tile)]
            moved = dot(jnp.concatenate(rows, axis=0).astype(BF), rank_ref[...])
            moved = moved[0:64] + moved[64:128]
            for t in range(8):
                total = total + jnp.where(target == g * 8 + t, moved[t * 8 : t * 8 + 8], 0.0)
            return total

        total = lax.fori_loop(0, SLABS // 8, unsort, jnp.zeros((8, atoms), jnp.float32), unroll=4)
        out_ref[p : p + 1, :] = total[0:1]
        out_ref[2 + p : 3 + p, :] = total[1:2]

    spread(0)
    cut(0)
    loads[0].wait()
    send_sides(0)
    for load in loads[1:]:
        load.wait()
    inner_z(0)
    make_gain()
    outer_z(0)
    spread(1)
    cut(1)
    send_sides(1)
    for u in UNITS_OF[0]:
        x_stage(u)
    inner_z(1)
    outer_z(1)
    for u in UNITS_OF[0]:
        y_stage(u)
    for u in UNITS_OF[1]:
        x_stage(u)
    for u in UNITS_OF[0]:
        i_stage(u)
    for u in UNITS_OF[1]:
        y_stage(u)
    home(0)
    for u in UNITS_OF[1]:
        i_stage(u)
    send_back_rims(0)
    read_mesh(0)
    home(1)
    read_rims(0)
    send_back_rims(1)
    to_atoms(0)
    read_mesh(1)
    read_rims(1)
    to_atoms(1)
    for copy in near.values():
        copy.wait_send()
    for u in range(UNITS):
        wait_slabs(block, u, slab_sems.at[0, u])
        wait_bricks(to_brick, u, brick_sems.at[0, u])
        wait_bricks(back_brick, u, brick_sems2.at[0, u])
        wait_slabs(back_slab, u, slab_sems2.at[0, u])


def body(charges, fractions, inner_cell, dest_slab, filter_amp):
    vmem = pl.BlockSpec(memory_space=pltpu.VMEM)
    anywhere = pl.BlockSpec(memory_space=pl.ANY)
    dma = pltpu.SemaphoreType.DMA
    atoms = charges.shape[1]
    tables = [jnp.asarray(table) for table in make_tables()]
    to_slab = (2, SLABS, 4, 16, 128)
    to_brick = (2, BRICKS, 8, 64, 128)
    return pl.pallas_call(
        kernel,
        out_shape=jax.ShapeDtypeStruct((4, atoms), jnp.float32),
        in_specs=[vmem] * 4 + [pl.BlockSpec(memory_space=pltpu.SMEM)] + [anywhere] * len(tables),
        out_specs=vmem,
        scratch_shapes=[pltpu.VMEM(table.shape, BF) for table in tables]
        + [
            pltpu.VMEM((8, SLABS * CAP), jnp.float32),
            pltpu.VMEM((4, 8, SLABS * CAP), jnp.float32),
            pltpu.VMEM((GROUPS, BACK_ROWS, LANES), jnp.float32),
            pltpu.VMEM((8, SLABS * CAP), jnp.float32),
            pltpu.VMEM((128, atoms), BF),
            pltpu.VMEM((GROUPS, 3, 256, LANES), BF),
            pltpu.VMEM((GROUPS, 3 * WINDOW, LANES), BF),
            pltpu.VMEM((G + 16, 256), jnp.float32),
            pltpu.VMEM((G + 16, 128), jnp.float32),
            pltpu.VMEM((G, 128), jnp.float32),
            pltpu.VMEM((2, PLACES, ROWS, 128), jnp.float32),
            pltpu.VMEM((2, PLACES, BACK_ROWS, 128), BF),
            pltpu.VMEM((2, WIDE, G, 128), jnp.float32),
            pltpu.VMEM((2, G, 128), BF),
            pltpu.VMEM((2, 2, G, 128), BF),
            pltpu.VMEM((2, G, 128), BF),
            pltpu.VMEM((2, 2, G, 128), BF),
            pltpu.VMEM((2, 3, G, 128), BF),
            pltpu.VMEM((2, 3, G, 128), BF),
            pltpu.VMEM((HALVES, 8, 128, 128), jnp.float32),
            pltpu.VMEM((8, G, 128), BF),
        ]
        + [pltpu.VMEM(to_slab, BF)] * 2
        + [pltpu.VMEM(to_brick, BF)] * 4
        + [pltpu.VMEM(to_slab, BF)] * 2
        + [
            pltpu.VMEM((512, 4 * 128), jnp.float32),
            pltpu.VMEM((2, WIDE, G, 128), BF),
            pltpu.VMEM((2, 512, G), jnp.float32),
            dma((len(tables),)),
            dma((2, 16)),
        ]
        + [dma((2, UNITS))] * 4,
        compiler_params=pltpu.CompilerParams(collective_id=0, has_side_effects=True, vmem_limit_bytes=VMEM_LIMIT),
    )(
        charges, fractions, inner_cell.reshape(1, -1), dest_slab.reshape(1, -1), filter_amp, *tables
    )


def solution(mesh):
    in_specs = (
        P(None, ("slab", "brick")),
        P(None, ("slab", "brick")),
        P(("slab", "brick")),
        P(("slab", "brick"), None),
        P(),
    )
    out_specs = P(None, ("slab", "brick"))
    return jax.shard_map(body, mesh=mesh, in_specs=in_specs, out_specs=out_specs, check_vma=False)
```
